32 devices in a mesh: gx: 4 (over y, x), gy: 8 (over z, core).
Axes of the slice: x: 2, y: 2, z: 4, core: 2. Of those that a mesh axis runs over, the one named last changes fastest.
Arguments:
- velocity: float32 [3, 32, 256, 128], P(None, 'gx', 'gy'), may hold values from -6 to 6
- stress: float32 [6, 32, 256, 128], P(None, 'gx', 'gy'), may hold values from -6 to 6
- density: float32 [32, 256, 128], P('gx', 'gy'), may hold values from 1 to 3
- lame_lambda: float32 [32, 256, 128], P('gx', 'gy'), may hold values from 0.2 to 1
- lame_mu: float32 [32, 256, 128], P('gx', 'gy'), may hold values from 0.1 to 1
Outputs:
- new_velocity: float32 [3, 32, 256, 128], P(None, 'gx', 'gy')
- new_stress: float32 [6, 32, 256, 128], P(None, 'gx', 'gy')
The draws below stay inside these ranges and needn't reach their ends.
All inputs are finite; a program needn't handle non-finite values.
Results may differ from the reference program's by a relative error of at most 0.00002.
Values sent between devices are 32-bit elements; how exact they have to be, the bound alone decides.
No kernel may reach another device: no remote copies, remote signals or barrier semaphores. Data moves between devices by JAX's collectives and lax.ppermute only.
A program may use at most 64 MiB of HBM per device.

```python
import math
import jax
import jax.numpy as jnp

NZ = 128
NX = 32
NY = 256


def block_scale(rng, shape, split, low, top_value):
    loudness = 1.0
    for axis_at, parts in split:
        steps = jax.random.uniform(jax.random.fold_in(jax.random.fold_in(rng, 6), axis_at), (parts,), jnp.float32, low / len(split), top_value / len(split))
        loudness = loudness * jnp.repeat(jnp.exp(steps), shape[axis_at] // parts).reshape((-1,) + (1,) * (len(shape) - 1 - axis_at))
    return loudness


def gaussian(rng, dims, deviation, limit, split=(), held_as=jnp.bfloat16):
    entries = deviation * jax.random.normal(rng, dims, jnp.float32)
    if split:
        entries = entries * block_scale(rng, dims, split, -0.22, 0.18)
    return jnp.clip(entries, -limit, limit).astype(held_as)


def setup_inputs(seed: int = 0) -> dict:
    arg_keys = jax.random.split(jax.random.key(seed), 6)
    return {
        "velocity": gaussian(arg_keys[0], (3, NX, NY, NZ), 1.0, 6.0, ((1, 4), (2, 8)), jnp.float32),
        "stress": gaussian(arg_keys[1], (6, NX, NY, NZ), 1.0, 6.0, ((1, 4), (2, 8)), jnp.float32),
        "density": jnp.clip(jnp.exp(math.log(3.0) - 1.0986123 * jax.random.uniform(arg_keys[2], (NX, NY, NZ), jnp.float32) ** block_scale(arg_keys[2], (NX, NY, NZ), ((0, 4), (1, 8)), -0.2, 0.2)), 1.0, 3.0),
        "lame_lambda": jnp.clip(0.2 + 0.8 * jax.random.uniform(arg_keys[3], (NX, NY, NZ), jnp.float32) ** block_scale(arg_keys[3], (NX, NY, NZ), ((0, 4), (1, 8)), -0.2, 0.2), 0.2, 1.0),
        "lame_mu": jnp.clip(jnp.exp(math.log(1.0) - 2.3025851 * jax.random.uniform(arg_keys[4], (NX, NY, NZ), jnp.float32) ** block_scale(arg_keys[4], (NX, NY, NZ), ((0, 4), (1, 8)), -0.2, 0.2)), 0.1, 1.0),
    }


first_coef = 9.0 / 8.0
second_coef = -1.0 / 24.0
time_step = 0.25


def take(field, axis, start):
    count = field.shape[axis] - 4
    index = []
    for dim in range(3):
        if dim == axis:
            index.append(slice(start, start + count))
        else:
            index.append(slice(2, field.shape[dim] - 2))
    return field[tuple(index)]


def forward(field, axis):
    return first_coef * (take(field, axis, 3) - take(field, axis, 2)) + second_coef * (take(field, axis, 4) - take(field, axis, 1))


def backward(field, axis):
    return first_coef * (take(field, axis, 2) - take(field, axis, 1)) + second_coef * (take(field, axis, 3) - take(field, axis, 0))


def coefficients(recips, lam, shear):
    size_x, size_y, size_z = lam.shape
    buoy = recips[0]
    comp = recips[1]

    def part(field, dx, dy, dz):
        return field[dx:dx + size_x, dy:dy + size_y, dz:dz + size_z]

    base_b = part(buoy, 0, 0, 0)
    buoy_x = 0.5 * (base_b + part(buoy, 1, 0, 0))
    buoy_y = 0.5 * (base_b + part(buoy, 0, 1, 0))
    buoy_z = 0.5 * (base_b + part(buoy, 0, 0, 1))
    base_c = part(comp, 0, 0, 0)
    shear_xy = 4.0 / (base_c + part(comp, 1, 0, 0) + part(comp, 0, 1, 0) + part(comp, 1, 1, 0))
    shear_xz = 4.0 / (base_c + part(comp, 1, 0, 0) + part(comp, 0, 0, 1) + part(comp, 1, 0, 1))
    shear_yz = 4.0 / (base_c + part(comp, 0, 1, 0) + part(comp, 0, 0, 1) + part(comp, 0, 1, 1))
    return (buoy_x, buoy_y, buoy_z), (lam, lam + 2.0 * shear, shear_xy, shear_xz, shear_yz)


def velocity_update(velocity, padded_stress, buoys):
    stress_xx, stress_yy, stress_zz = padded_stress[0], padded_stress[1], padded_stress[2]
    stress_xy, stress_xz, stress_yz = padded_stress[3], padded_stress[4], padded_stress[5]
    accel_x = forward(stress_xx, 0) + backward(stress_xy, 1) + backward(stress_xz, 2)
    accel_y = backward(stress_xy, 0) + forward(stress_yy, 1) + backward(stress_yz, 2)
    accel_z = backward(stress_xz, 0) + backward(stress_yz, 1) + forward(stress_zz, 2)
    return velocity + time_step * jnp.stack([buoys[0] * accel_x, buoys[1] * accel_y, buoys[2] * accel_z])


def stress_update(stress, padded_velocity, moduli):
    lam, lam_two, shear_xy, shear_xz, shear_yz = moduli
    vel_x, vel_y, vel_z = padded_velocity[0], padded_velocity[1], padded_velocity[2]
    strain_xx = backward(vel_x, 0)
    strain_yy = backward(vel_y, 1)
    strain_zz = backward(vel_z, 2)
    new_xx = stress[0] + time_step * (lam_two * strain_xx + lam * (strain_yy + strain_zz))
    new_yy = stress[1] + time_step * (lam_two * strain_yy + lam * (strain_xx + strain_zz))
    new_zz = stress[2] + time_step * (lam_two * strain_zz + lam * (strain_xx + strain_yy))
    new_xy = stress[3] + time_step * shear_xy * (forward(vel_x, 1) + forward(vel_y, 0))
    new_xz = stress[4] + time_step * shear_xz * (forward(vel_x, 2) + forward(vel_z, 0))
    new_yz = stress[5] + time_step * shear_yz * (forward(vel_y, 2) + forward(vel_z, 1))
    return jnp.stack([new_xx, new_yy, new_zz, new_xy, new_xz, new_yz])


def reference(velocity, stress, density, lame_lambda, lame_mu):
    recips = jnp.stack([1.0 / density, 1.0 / lame_mu])
    recips = jnp.pad(recips, ((0, 0), (0, 1), (0, 1), (0, 1)))
    buoys, moduli = coefficients(recips, lame_lambda, lame_mu)
    widths = ((0, 0), (2, 2), (2, 2), (2, 2))
    for step in range(2):
        velocity = velocity_update(velocity, jnp.pad(stress, widths), buoys)
        stress = stress_update(stress, jnp.pad(velocity, widths), moduli)
    return velocity, stress
```

```python
import jax
import jax.numpy as jnp
from jax import lax
from jax.experimental import pallas as pl
from jax.experimental.pallas import tpu as pltpu
from jax.sharding import PartitionSpec as P

near = 9.0 / 8.0
far = 1.0 / 24.0
time_step = 0.25
tile = 8
AXES = ("gx", "gy")


def pairings(count_x, count_y):
    other = 2 if count_x % 4 == 0 else 1

    def across(i, count):
        return ((i + 1) ^ 1) - 1

    def route(rule):
        pairs = []
        for i in range(count_x):
            for j in range(count_y):
                ti, tj = rule(i, j)
                pairs.append((i * count_y + j, ti * count_y + tj))
        return pairs

    def inner_x(i, j):
        return (i ^ 1, j)

    def outer_x(i, j):
        return (across(i, count_x), j) if 0 < i < count_x - 1 else (i, j ^ 1)

    def inner_y(i, j):
        return (i, j ^ 1)

    def outer_y(i, j):
        return (i, across(j, count_y)) if 0 < j < count_y - 1 else (i ^ other, j)

    return [route(rule) for rule in (inner_x, outer_x, inner_y, outer_y)]


def position():
    i, j = lax.axis_index("gx"), lax.axis_index("gy")
    return i, j, lax.rem(i, 2) == 0, lax.rem(j, 2) == 0


def unpack(inner, outer, low, high, even, first, last):
    for start in range(0, inner.shape[0], tile):
        rows = pl.ds(start, tile)
        a, b = inner[rows, :], outer[rows, :]
        low[rows, :] = jnp.where(first, 0.0, jnp.where(even, b, a))
        high[rows, :] = jnp.where(last, 0.0, jnp.where(even, a, b))


class Pack:
    def __init__(self, inner, outer, even):
        self.inner, self.outer, self.even = inner, outer, even

    def put(self, up, down):
        even, inner, outer = self.even, self.inner, self.outer

        @pl.when(even)
        def _():
            for rows, value in up():
                inner[rows, :] = value
            for rows, value in down():
                outer[rows, :] = value

        @pl.when(jnp.logical_not(even))
        def _():
            for rows, value in up():
                outer[rows, :] = value
            for rows, value in down():
                inner[rows, :] = value


def planes(items):
    out = []
    start = 0
    for ref, f, x in items:
        size = ref.shape[-2]
        value = ref[f, x] if f is not None else ref[x]
        out.append((pl.ds(start, size), value))
        start += size
    return out


def rows_of(items, count_x):
    out = []
    for x in range(count_x):
        start = tile * x
        for ref, f, row, count in items:
            value = ref[f, x, pl.ds(row, count), :] if f is not None else ref[x, pl.ds(row, count), :]
            out.append((pl.ds(start, count), value))
            start += count
    return out


def sides(i, j):
    return i == 0, i == lax.axis_size("gx") - 1, j == 0, j == lax.axis_size("gy") - 1


def lanes():
    return lax.broadcasted_iota(jnp.int32, (tile, 128), 1)


def z_shift(value, k, lane):
    size = value.shape[-1]
    moved = pltpu.roll(value, (-k) % size, 1)
    inside = lane < size - k if k > 0 else lane >= -k
    return jnp.where(inside, moved, 0.0)


def difference(at, base):
    return near * (at(base + 1) - at(base)) - far * (at(base + 2) - at(base - 1))


def first_pack(stress, density, shear, ax, bx, ay, by, recips):
    i, j, even_x, even_y = position()
    nx, ny = density.shape[0], density.shape[1]
    for x in range(nx):
        recips[0, x] = 1.0 / density[x]
        recips[1, x] = 1.0 / shear[x]
    Pack(ax, bx, even_x).put(
        lambda: planes([(stress, 3, nx - 2), (stress, 3, nx - 1), (stress, 4, nx - 2), (stress, 4, nx - 1), (stress, 0, nx - 1)]),
        lambda: planes([(stress, 3, 0), (stress, 4, 0), (stress, 0, 0), (stress, 0, 1), (recips, 0, 0), (recips, 1, 0)]),
    )
    Pack(ay, by, even_y).put(
        lambda: rows_of([(stress, 3, ny - 2, 2), (stress, 5, ny - 2, 2), (stress, 1, ny - 1, 1)], nx),
        lambda: rows_of([(stress, 3, 0, 1), (stress, 5, 0, 1), (stress, 1, 0, 2), (recips, 0, 0, 1), (recips, 1, 0, 1)], nx),
    )


class Field:
    def __init__(self, ref, f, low_x=None, high_x=None, low_y=None, high_y=None):
        self.ref, self.f = ref, f
        self.low_x, self.high_x, self.low_y, self.high_y = low_x, high_x, low_y, high_y

    def at(self, x, t):
        rows = pl.ds(tile * t, tile)
        nx, ny = self.ref.shape[-3], self.ref.shape[-2]
        if x < 0:
            ref, index = self.low_x
            return ref[pl.ds(ny * (index + x) + tile * t, tile), :]
        if x >= nx:
            ref, index = self.high_x
            return ref[pl.ds(ny * (index + x - nx) + tile * t, tile), :]
        return self.ref[self.f, x, rows, :]

    def y(self, x, t, k):
        ny = self.ref.shape[-2]
        start = tile * t + k
        if start < 0:
            return self.low_y[x, pl.ds(tile + k, tile), :]
        if start + tile > ny:
            return self.high_y[x, pl.ds(k, tile), :]
        return self.ref[self.f, x, pl.ds(start, tile), :]


def fill_edges(ref, f, edge, lows, highs, low_row, low_count, high_row, high_count):
    nx, ny = ref.shape[-3], ref.shape[-2]
    for x in range(nx):
        if low_count:
            edge[0, x, pl.ds(tile - low_count, low_count), :] = lows[pl.ds(tile * x + low_row, low_count), :]
            edge[0, x, pl.ds(tile, tile), :] = ref[f, x, pl.ds(0, tile), :]
        if high_count:
            edge[1, x, pl.ds(0, tile), :] = ref[f, x, pl.ds(ny - tile, tile), :]
            edge[1, x, pl.ds(tile, high_count), :] = highs[pl.ds(tile * x + high_row, high_count), :]


def receive(args, scratch):
    i, j, even_x, even_y = position()
    ax, bx, ay, by = args
    low_x, high_x, low_y, high_y = scratch
    first_x, last_x, first_y, last_y = sides(i, j)
    unpack(ax, bx, low_x, high_x, even_x, first_x, last_x)
    unpack(ay, by, low_y, high_y, even_y, first_y, last_y)
    return even_x, even_y


def velocity_kernel(step, *refs):
    if step == 0:
        (velocity, stress, recips, ax, bx, ay, by, out, pax, pbx, pay, pby, buoys,
         low_x, high_x, low_y, high_y, edges, edge_b) = refs
    else:
        (velocity, stress, buoys, ax, bx, ay, by, out, pax, pbx, pay, pby,
         low_x, high_x, low_y, high_y, edges) = refs
    nx, ny = stress.shape[1], stress.shape[2]
    even_x, even_y = receive((ax, bx, ay, by), (low_x, high_x, low_y, high_y))
    fill_edges(stress, 3, edges.at[0], low_y, high_y, 0, 2, 0, 1)
    fill_edges(stress, 5, edges.at[1], low_y, high_y, 2, 2, 1, 1)
    fill_edges(stress, 1, edges.at[2], low_y, high_y, 4, 1, 2, 2)
    xx = Field(stress, 0, (low_x, 5), (high_x, 2))
    yy = Field(stress, 1, low_y=edges.at[2, 0], high_y=edges.at[2, 1])
    zz = Field(stress, 2)
    xy = Field(stress, 3, (low_x, 2), (high_x, 0), edges.at[0, 0], edges.at[0, 1])
    xz = Field(stress, 4, (low_x, 4), (high_x, 1))
    yz = Field(stress, 5, low_y=edges.at[1, 0], high_y=edges.at[1, 1])
    if step == 0:
        fill_edges(recips, 0, edge_b, low_y, high_y, 0, 0, 4, 1)
        buoy = Field(recips, 0, None, (high_x, 4), None, edge_b.at[1])
    lane = lanes()
    for x in range(nx):
        for t in range(ny // tile):
            rows = pl.ds(tile * t, tile)

            def dx(field, base):
                return difference(lambda k: field.at(x + k, t), base)

            def dy(field, base):
                return difference(lambda k: field.y(x, t, k), base)

            def dz(field, base):
                value = field.at(x, t)
                return difference(lambda k: z_shift(value, k, lane) if k else value, base)

            if step == 0:
                here = buoy.at(x, t)
                half = 0.5 * time_step
                bx_ = half * (here + buoy.at(x + 1, t))
                by_ = half * (here + buoy.y(x, t, 1))
                bz_ = half * (here + z_shift(here, 1, lane))
                buoys[0, x, rows, :] = bx_
                buoys[1, x, rows, :] = by_
                buoys[2, x, rows, :] = bz_
            else:
                bx_, by_, bz_ = (buoys[c, x, rows, :] for c in range(3))
            out[0, x, rows, :] = velocity[0, x, rows, :] + bx_ * (dx(xx, 0) + dy(xy, -1) + dz(xz, -1))
            out[1, x, rows, :] = velocity[1, x, rows, :] + by_ * (dx(xy, -1) + dy(yy, 0) + dz(yz, -1))
            out[2, x, rows, :] = velocity[2, x, rows, :] + bz_ * (dx(xz, -1) + dy(yz, -1) + dz(zz, 0))

    def down():
        items = planes([(out, 0, 0), (out, 1, 0), (out, 1, 1), (out, 2, 0), (out, 2, 1)])
        if step == 0:
            start = sum(value.shape[0] for _, value in items)
            items.append((pl.ds(start, 1), high_y[pl.ds(5, 1), :]))
        return items

    Pack(pax, pbx, even_x).put(
        lambda: planes([(out, 0, nx - 2), (out, 0, nx - 1), (out, 1, nx - 1), (out, 2, nx - 1)]), down)
    Pack(pay, pby, even_y).put(
        lambda: rows_of([(out, 1, ny - 2, 2), (out, 0, ny - 1, 1), (out, 2, ny - 1, 1)], nx),
        lambda: rows_of([(out, 1, 0, 1), (out, 0, 0, 2), (out, 2, 0, 2)], nx),
    )


def stress_kernel(step, *refs):
    if step == 0:
        (velocity, stress, lam, shear, recips, halo_c, edge_c, ax, bx, ay, by,
         out, pax, pbx, pay, pby, shears, low_x, high_x, low_y, high_y, edges, corner) = refs
    else:
        (velocity, stress, lam, shear, shears, ax, bx, ay, by,
         out, low_x, high_x, low_y, high_y, edges) = refs
    nx, ny = stress.shape[1], stress.shape[2]
    even_x, even_y = receive((ax, bx, ay, by), (low_x, high_x, low_y, high_y))
    fill_edges(velocity, 1, edges.at[0], low_y, high_y, 0, 2, 0, 1)
    fill_edges(velocity, 0, edges.at[1], low_y, high_y, 2, 1, 1, 2)
    fill_edges(velocity, 2, edges.at[2], low_y, high_y, 3, 1, 3, 2)
    vx = Field(velocity, 0, (low_x, 2), (high_x, 0), edges.at[1, 0], edges.at[1, 1])
    vy = Field(velocity, 1, (low_x, 3), (high_x, 1), edges.at[0, 0], edges.at[0, 1])
    vz = Field(velocity, 2, (low_x, 4), (high_x, 3), edges.at[2, 0], edges.at[2, 1])
    lane = lanes()
    if step == 0:
        corner[pl.ds(0, tile), :] = halo_c[pl.ds(ny - tile, tile), :]
        corner[pl.ds(tile, 1), :] = high_x[pl.ds(5 * ny, 1), :]

        def comp(x, t, k):
            if k == 1 and t == ny // tile - 1:
                return corner[pl.ds(1, tile), :] if x == nx else edge_c[x, pl.ds(1, tile), :]
            if x == nx:
                return halo_c[pl.ds(tile * t + k, tile), :]
            return recips[1, x, pl.ds(tile * t + k, tile), :]

    for x in range(nx):
        for t in range(ny // tile):
            rows = pl.ds(tile * t, tile)

            def dx(field, base):
                return difference(lambda k: field.at(x + k, t), base)

            def dy(field, base):
                return difference(lambda k: field.y(x, t, k), base)

            def dz(field, base):
                value = field.at(x, t)
                return difference(lambda k: z_shift(value, k, lane) if k else value, base)

            if step == 0:
                here = comp(x, t, 0)
                next_x, next_y = comp(x + 1, t, 0), comp(x, t, 1)
                pair_x, pair_y = here + next_x, here + next_y
                four = 4.0 * time_step
                mxy = four / (pair_x + (next_y + comp(x + 1, t, 1)))
                mxz = four / (pair_x + z_shift(pair_x, 1, lane))
                myz = four / (pair_y + z_shift(pair_y, 1, lane))
                shears[0, x, rows, :] = mxy
                shears[1, x, rows, :] = mxz
                shears[2, x, rows, :] = myz
            else:
                mxy, mxz, myz = (shears[c, x, rows, :] for c in range(3))
            exx, eyy, ezz = dx(vx, -1), dy(vy, -1), dz(vz, -1)
            la = time_step * lam[x, rows, :]
            two = (2.0 * time_step) * shear[x, rows, :]
            common = la * (exx + eyy + ezz)
            out[0, x, rows, :] = stress[0, x, rows, :] + (common + two * exx)
            out[1, x, rows, :] = stress[1, x, rows, :] + (common + two * eyy)
            out[2, x, rows, :] = stress[2, x, rows, :] + (common + two * ezz)
            out[3, x, rows, :] = stress[3, x, rows, :] + mxy * (dy(vx, 0) + dx(vy, 0))
            out[4, x, rows, :] = stress[4, x, rows, :] + mxz * (dz(vx, 0) + dx(vz, 0))
            out[5, x, rows, :] = stress[5, x, rows, :] + myz * (dz(vy, 0) + dy(vz, 0))
    if step == 0:
        Pack(pax, pbx, even_x).put(
            lambda: planes([(out, 3, nx - 2), (out, 3, nx - 1), (out, 4, nx - 2), (out, 4, nx - 1), (out, 0, nx - 1)]),
            lambda: planes([(out, 3, 0), (out, 4, 0), (out, 0, 0), (out, 0, 1)]),
        )
        Pack(pay, pby, even_y).put(
            lambda: rows_of([(out, 3, ny - 2, 2), (out, 5, ny - 2, 2), (out, 1, ny - 1, 1)], nx),
            lambda: rows_of([(out, 3, 0, 1), (out, 5, 0, 1), (out, 1, 0, 2)], nx),
        )


def compliance_kernel(recips, ax, ay_in, by_in, bx, halo_c, edge_c):
    i, j, even_x, even_y = position()
    first_x, last_x, first_y, last_y = sides(i, j)
    nx, ny = recips.shape[1], recips.shape[2]
    for t in range(ny // tile):
        rows = pl.ds(5 * ny + tile * t, tile)
        halo_c[pl.ds(tile * t, tile), :] = jnp.where(last_x, 0.0, jnp.where(even_x, ax[rows, :], bx[rows, :]))
    for x in range(nx):
        edge_c[x, pl.ds(0, tile), :] = recips[1, x, pl.ds(ny - tile, tile), :]
        row = pl.ds(tile * x + 5, 1)
        edge_c[x, pl.ds(tile, 1), :] = jnp.where(last_y, 0.0, jnp.where(even_y, ay_in[row, :], by_in[row, :]))


def call(kernel, outs, scratch, args, flops):
    vmem = pl.BlockSpec(memory_space=pltpu.VMEM)
    return pl.pallas_call(
        kernel,
        out_shape=[jax.ShapeDtypeStruct(shape, jnp.float32) for shape in outs],
        in_specs=[vmem] * len(args),
        out_specs=[vmem] * len(outs),
        scratch_shapes=[pltpu.VMEM(shape, jnp.float32) for shape in scratch],
        compiler_params=pltpu.CompilerParams(vmem_limit_bytes=16 * 1024 * 1024),
        cost_estimate=pl.CostEstimate(flops=flops, bytes_accessed=2 * 1024 * 1024, transcendentals=0),
    )(*args)


def per_device(velocity, stress, density, lame_lambda, lame_mu):
    _, nx, ny, nz = velocity.shape
    routes = pairings(lax.axis_size("gx"), lax.axis_size("gy"))
    cells = nx * ny * nz

    def packages(x_rows):
        return [(x_rows, nz)] * 2 + [(nx * tile, nz)] * 2

    def exchange(arrays):
        return [lax.ppermute(array, AXES, route) for array, route in zip(arrays, routes)]

    def scratch(x_rows):
        return packages(x_rows) + [(3, 2, nx, 2 * tile, nz)]

    first, second, later = 6 * ny, 5 * ny + tile, 5 * ny
    *packed, recips = call(
        first_pack, packages(first) + [(2, nx, ny, nz)], [], (stress, density, lame_mu), 10 * cells)
    got = exchange(packed)
    velocity, *packed, buoys = call(
        lambda *refs: velocity_kernel(0, *refs),
        [velocity.shape] + packages(second) + [(3, nx, ny, nz)],
        scratch(first) + [(2, nx, 2 * tile, nz)],
        (velocity, stress, recips, *got), 60 * cells)
    halo_c, edge_c = call(
        lambda ax, bx, ay, by, recips, halo, edge: compliance_kernel(recips, ax, ay, by, bx, halo, edge),
        [(ny, nz), (nx, 2 * tile, nz)], [], (*got, recips), cells)
    got = exchange(packed)
    stress, *packed, shears = call(
        lambda *refs: stress_kernel(0, *refs),
        [stress.shape] + packages(later) + [(3, nx, ny, nz)],
        scratch(second) + [(2 * tile, nz)],
        (velocity, stress, lame_lambda, lame_mu, recips, halo_c, edge_c, *got), 80 * cells)
    got = exchange(packed)
    velocity, *packed = call(
        lambda *refs: velocity_kernel(1, *refs),
        [velocity.shape] + packages(later),
        scratch(later),
        (velocity, stress, buoys, *got), 60 * cells)
    got = exchange(packed)
    (stress,) = call(
        lambda *refs: stress_kernel(1, *refs),
        [stress.shape],
        scratch(later),
        (velocity, stress, lame_lambda, lame_mu, shears, *got), 80 * cells)
    return (velocity, stress)


def solution(mesh):
    in_specs = (
        P(None, "gx", "gy", None),
        P(None, "gx", "gy", None),
        P("gx", "gy", None),
        P("gx", "gy", None),
        P("gx", "gy", None),
    )
    out_specs = (P(None, "gx", "gy", None), P(None, "gx", "gy", None))
    return jax.shard_map(
        per_device, mesh=mesh, in_specs=in_specs, out_specs=out_specs, check_vma=False
    )
```

```python
import jax
import jax.numpy as jnp
from jax import lax
from jax.experimental import pallas as pl
from jax.experimental.pallas import tpu as pltpu
from jax.sharding import PartitionSpec as P

near = 9.0 / 8.0
far = 1.0 / 24.0
time_step = 0.25
tile = 8
AXES = ("gx", "gy")


def pairings(count_x, count_y):
    other = 2 if count_x % 4 == 0 else 1

    def across(i, count):
        return ((i + 1) ^ 1) - 1

    def route(rule):
        pairs = []
        for i in range(count_x):
            for j in range(count_y):
                ti, tj = rule(i, j)
                pairs.append((i * count_y + j, ti * count_y + tj))
        return pairs

    def inner_x(i, j):
        return (i ^ 1, j)

    def outer_x(i, j):
        return (across(i, count_x), j) if 0 < i < count_x - 1 else (i, j ^ 1)

    def inner_y(i, j):
        return (i, j ^ 1)

    def outer_y(i, j):
        return (i, across(j, count_y)) if 0 < j < count_y - 1 else (i ^ other, j)

    return [route(rule) for rule in (inner_x, outer_x, inner_y, outer_y)]


def position():
    i, j = lax.axis_index("gx"), lax.axis_index("gy")
    return i, j, lax.rem(i, 2) == 0, lax.rem(j, 2) == 0


def unpack(inner, outer, low, high, even, first, last):
    for start in range(0, inner.shape[0], tile):
        rows = pl.ds(start, tile)
        a, b = inner[rows, :], outer[rows, :]
        low[rows, :] = jnp.where(first, 0.0, jnp.where(even, b, a))
        high[rows, :] = jnp.where(last, 0.0, jnp.where(even, a, b))


class Pack:
    def __init__(self, inner, outer, even):
        self.inner, self.outer, self.even = inner, outer, even

    def put(self, up, down):
        even, inner, outer = self.even, self.inner, self.outer

        @pl.when(even)
        def _():
            up(inner)
            down(outer)

        @pl.when(jnp.logical_not(even))
        def _():
            up(outer)
            down(inner)


def put_planes(items):
    def put(out):
        start = 0
        for ref, f, x in items:
            value = ref[f, x]
            out[pl.ds(start, value.shape[0]), :] = value
            start += value.shape[0]

    return put


def put_rows(items, count_x):
    def put(out):
        for x in range(count_x):
            start = tile * x
            for ref, f, row, count in items:
                out[pl.ds(start, count), :] = ref[f, x, pl.ds(row, count), :]
                start += count

    return put


def sides(i, j):
    return i == 0, i == lax.axis_size("gx") - 1, j == 0, j == lax.axis_size("gy") - 1


def lanes():
    return lax.broadcasted_iota(jnp.int32, (tile, 128), 1)


def z_shift(value, k, lane):
    size = value.shape[-1]
    moved = pltpu.roll(value, (-k) % size, 1)
    inside = lane < size - k if k > 0 else lane >= -k
    return jnp.where(inside, moved, 0.0)


def difference(at, base):
    return near * (at(base + 1) - at(base)) - far * (at(base + 2) - at(base - 1))


class Field:
    def __init__(self, ref, f, low_x=None, high_x=None, edge=None):
        self.ref, self.f = ref, f
        self.low_x, self.high_x, self.edge = low_x, high_x, edge

    def at(self, x, t):
        nx, ny = self.ref.shape[-3], self.ref.shape[-2]
        if x < 0:
            ref, index = self.low_x
            return ref[pl.ds(ny * (index + x) + tile * t, tile), :]
        if x >= nx:
            ref, index = self.high_x
            return ref[pl.ds(ny * (index + x - nx) + tile * t, tile), :]
        return self.ref[self.f, x, pl.ds(tile * t, tile), :]

    def y(self, x, t, k):
        ny = self.ref.shape[-2]
        start = tile * t + k
        if start < 0:
            return self.edge[0, x, pl.ds(tile + k, tile), :]
        if start + tile > ny:
            return self.edge[1, x, pl.ds(k, tile), :]
        return self.ref[self.f, x, pl.ds(start, tile), :]


class Differences:
    def __init__(self, x, t, lane):
        self.x, self.t, self.lane = x, t, lane

    def dx(self, field, base):
        return difference(lambda k: field.at(self.x + k, self.t), base)

    def dy(self, field, base):
        return difference(lambda k: field.y(self.x, self.t, k), base)

    def dz(self, field, base):
        value = field.at(self.x, self.t)
        return difference(lambda k: z_shift(value, k, self.lane) if k else value, base)


def inner_plane(x, base, nx):
    return x + base - 1 >= 0 and x + base + 2 < nx


def inner_tile(t, ny):
    return 0 < t < ny // tile - 1


def fill_edges(ref, f, edge, lows, highs, low_row, low_count, high_row, high_count):
    nx, ny = ref.shape[-3], ref.shape[-2]
    for x in range(nx):
        if low_count:
            edge[0, x, pl.ds(tile - low_count, low_count), :] = lows[pl.ds(tile * x + low_row, low_count), :]
            edge[0, x, pl.ds(tile, tile), :] = ref[f, x, pl.ds(0, tile), :]
        if high_count:
            edge[1, x, pl.ds(0, tile), :] = ref[f, x, pl.ds(ny - tile, tile), :]
            edge[1, x, pl.ds(tile, high_count), :] = highs[pl.ds(tile * x + high_row, high_count), :]


def receive(got, halos):
    i, j, even_x, even_y = position()
    ax, bx, ay, by = got
    low_x, high_x, low_y, high_y = halos
    first_x, last_x, first_y, last_y = sides(i, j)
    unpack(ax, bx, low_x, high_x, even_x, first_x, last_x)
    unpack(ay, by, low_y, high_y, even_y, first_y, last_y)
    return even_x, even_y, last_x, last_y


def first_pack(stress, density, shear, ax, bx, ay, by, tiles, sems):
    i, j, even_x, even_y = position()
    nx, ny = density.shape[0], density.shape[1]
    planes_up = [(stress, 3, nx - 2), (stress, 3, nx - 1), (stress, 4, nx - 2), (stress, 4, nx - 1), (stress, 0, nx - 1)]
    planes_down = [(stress, 3, 0), (stress, 4, 0), (stress, 0, 0), (stress, 0, 1), (density, None, 0), (shear, None, 0)]
    columns = [(stress, 3, ny - tile), (stress, 5, ny - tile), (stress, 1, ny - tile),
               (stress, 3, 0), (stress, 5, 0), (stress, 1, 0), (density, None, 0), (shear, None, 0)]

    def plane_copies(items, out, sem):
        copies = []
        for n, (ref, f, x) in enumerate(items):
            source = ref.at[x] if f is None else ref.at[f, x]
            copies.append(pltpu.make_async_copy(source, out.at[pl.ds(n * ny, ny), :], sem.at[n]))
        return copies

    copies = []
    for n, (ref, f, row) in enumerate(columns):
        source = ref if f is None else ref.at[f]
        copies.append(pltpu.make_async_copy(source.at[:, pl.ds(row, tile), :], tiles.at[n], sems.at[2, n]))
    for copy in copies:
        copy.start()

    @pl.when(even_x)
    def _():
        for copy in plane_copies(planes_up, ax, sems.at[0]) + plane_copies(planes_down, bx, sems.at[1]):
            copy.start()

    @pl.when(jnp.logical_not(even_x))
    def _():
        for copy in plane_copies(planes_up, bx, sems.at[0]) + plane_copies(planes_down, ax, sems.at[1]):
            copy.start()

    for copy in copies:
        copy.wait()
    Pack(ay, by, even_y).put(
        put_rows([(tiles, 0, tile - 2, 2), (tiles, 1, tile - 2, 2), (tiles, 2, tile - 1, 1)], nx),
        put_rows([(tiles, 3, 0, 1), (tiles, 4, 0, 1), (tiles, 5, 0, 2), (tiles, 6, 0, 1), (tiles, 7, 0, 1)], nx),
    )
    for copy in plane_copies(planes_up, ax, sems.at[0]) + plane_copies(planes_down, bx, sems.at[1]):
        copy.wait()


def velocity_terms(stress, low_x, high_x, edges):
    xx = Field(stress, 0, (low_x, 5), (high_x, 2))
    yy = Field(stress, 1, edge=edges.at[2] if edges is not None else None)
    zz = Field(stress, 2)
    xy = Field(stress, 3, (low_x, 2), (high_x, 0), edges.at[0] if edges is not None else None)
    xz = Field(stress, 4, (low_x, 4), (high_x, 1))
    yz = Field(stress, 5, edge=edges.at[1] if edges is not None else None)
    return ((xx, 0), (xy, -1), (xz, -1)), ((xy, -1), (yy, 0), (yz, -1)), ((xz, -1), (yz, -1), (zz, 0))


def velocity_inside(step, *refs):
    if step == 0:
        velocity, stress, density, out, buoy, buoys = refs
    else:
        velocity, stress, buoys, out = refs
    nx, ny = stress.shape[1], stress.shape[2]
    lane = lanes()
    terms = velocity_terms(stress, None, None, None)
    if step == 0:
        for x in range(nx):
            buoy[0, x] = 1.0 / density[x]
        buoy_field = Field(buoy, 0)
    for x in range(nx):
        for t in range(ny // tile):
            rows = pl.ds(tile * t, tile)
            d = Differences(x, t, lane)
            if step == 0:
                here = buoy_field.at(x, t)
                half = 0.5 * time_step
                if x < nx - 1:
                    buoys[0, x, rows, :] = half * (here + buoy_field.at(x + 1, t))
                if t < ny // tile - 1:
                    buoys[1, x, rows, :] = half * (here + buoy_field.y(x, t, 1))
                buoys[2, x, rows, :] = half * (here + z_shift(here, 1, lane))
            for c, ((fx, sx), (fy, sy), (fz, sz)) in enumerate(terms):
                total = d.dz(fz, sz)
                whole_x, whole_y = inner_plane(x, sx, nx), inner_tile(t, ny)
                if whole_x:
                    total += d.dx(fx, sx)
                if whole_y:
                    total += d.dy(fy, sy)
                if whole_x and whole_y:
                    total = velocity[c, x, rows, :] + buoys[c, x, rows, :] * total
                out[c, x, rows, :] = total


def velocity_edges(step, *refs):
    if step == 0:
        (velocity, stress, buoy, buoys, part, ax, bx, ay, by, out, buoys_end, pax, pbx, pay, pby,
         low_x, high_x, low_y, high_y, edges, edge_b) = refs
    else:
        (velocity, stress, buoys, buoys_end, part, ax, bx, ay, by, out, pax, pbx, pay, pby,
         low_x, high_x, low_y, high_y, edges) = refs
    nx, ny = stress.shape[1], stress.shape[2]
    even_x, even_y, last_x, last_y = receive((ax, bx, ay, by), (low_x, high_x, low_y, high_y))
    fill_edges(stress, 3, edges.at[0], low_y, high_y, 0, 2, 0, 1)
    fill_edges(stress, 5, edges.at[1], low_y, high_y, 2, 2, 1, 1)
    fill_edges(stress, 1, edges.at[2], low_y, high_y, 4, 1, 2, 2)
    terms = velocity_terms(stress, low_x, high_x, edges)
    lane = lanes()
    if step == 0:
        half = 0.5 * time_step
        for t in range(ny // tile):
            rows = pl.ds(tile * t, tile)
            above = jnp.where(last_x, 0.0, 1.0 / jnp.where(last_x, 1.0, high_x[pl.ds(4 * ny + tile * t, tile), :]))
            buoys_end[rows, :] = half * (buoy[0, nx - 1, rows, :] + above)
        rows = pl.ds(ny - tile, tile)
        for x in range(nx):
            here = buoy[0, x, rows, :]
            row = high_y[pl.ds(tile * x + 4, 1), :]
            edge_b[pl.ds(0, tile), :] = here
            edge_b[pl.ds(tile, 1), :] = jnp.where(last_y, 0.0, 1.0 / jnp.where(last_y, 1.0, row))
            buoys_end[pl.ds(ny + tile * x, tile), :] = half * (here + edge_b[pl.ds(1, tile), :])
    for x in range(nx):
        for t in range(ny // tile):
            rows = pl.ds(tile * t, tile)
            d = Differences(x, t, lane)
            for c, ((fx, sx), (fy, sy), _) in enumerate(terms):
                whole_x, whole_y = inner_plane(x, sx, nx), inner_tile(t, ny)
                total = part[c, x, rows, :]
                if whole_x and whole_y:
                    out[c, x, rows, :] = total
                    continue
                if not whole_x:
                    total += d.dx(fx, sx)
                if not whole_y:
                    total += d.dy(fy, sy)
                if c == 0 and x == nx - 1:
                    factor = buoys_end[rows, :]
                elif c == 1 and t == ny // tile - 1:
                    factor = buoys_end[pl.ds(ny + tile * x, tile), :]
                else:
                    factor = buoys[c, x, rows, :]
                out[c, x, rows, :] = velocity[c, x, rows, :] + factor * total

    planes_down = put_planes([(out, 0, 0), (out, 1, 0), (out, 1, 1), (out, 2, 0), (out, 2, 1)])

    def down(package):
        planes_down(package)
        if step == 0:
            row = high_y[pl.ds(5, 1), :]
            package[pl.ds(5 * ny, 1), :] = jnp.where(last_y, 0.0, 1.0 / jnp.where(last_y, 1.0, row))

    Pack(pax, pbx, even_x).put(
        put_planes([(out, 0, nx - 2), (out, 0, nx - 1), (out, 1, nx - 1), (out, 2, nx - 1)]), down)
    Pack(pay, pby, even_y).put(
        put_rows([(out, 1, ny - 2, 2), (out, 0, ny - 1, 1), (out, 2, ny - 1, 1)], nx),
        put_rows([(out, 1, 0, 1), (out, 0, 0, 2), (out, 2, 0, 2)], nx),
    )


def stress_fields(velocity, low_x, high_x, edges):
    vx = Field(velocity, 0, (low_x, 2), (high_x, 0), edges.at[1] if edges is not None else None)
    vy = Field(velocity, 1, (low_x, 3), (high_x, 1), edges.at[0] if edges is not None else None)
    vz = Field(velocity, 2, (low_x, 4), (high_x, 3), edges.at[2] if edges is not None else None)
    return vx, vy, vz


def new_normal(stress, lam, shear, x, rows, strains):
    la = time_step * lam[x, rows, :]
    two = (2.0 * time_step) * shear[x, rows, :]
    common = la * (strains[0] + strains[1] + strains[2])
    return [stress[c, x, rows, :] + (common + two * strains[c]) for c in range(3)]


def stress_inside(step, *refs):
    if step == 0:
        velocity, stress, lam, shear, ax, bx, ay, by, out, shears, halo_c, comps, edge_c = refs
    else:
        velocity, stress, lam, shear, shears, out, final_velocity, sem = refs
    nx, ny = stress.shape[1], stress.shape[2]
    lane = lanes()
    vx, vy, vz = stress_fields(velocity, None, None, None)
    if step == 1:
        copy = pltpu.make_async_copy(velocity, final_velocity, sem)
        copy.start()
    if step == 0:
        i, j, even_x, even_y = position()
        _, last_x, _, last_y = sides(i, j)
        for x in range(nx):
            comps[x] = 1.0 / shear[x]
            edge_c[x, pl.ds(0, tile), :] = comps[x, pl.ds(ny - tile, tile), :]
            row = pl.ds(tile * x + 5, 1)
            value = jnp.where(last_y, 1.0, jnp.where(even_y, ay[row, :], by[row, :]))
            edge_c[x, pl.ds(tile, 1), :] = jnp.where(last_y, 0.0, 1.0 / value)
        for t in range(ny // tile):
            rows = pl.ds(5 * ny + tile * t, tile)
            value = jnp.where(last_x, 1.0, jnp.where(even_x, ax[rows, :], bx[rows, :]))
            halo_c[pl.ds(tile * t, tile), :] = jnp.where(last_x, 0.0, 1.0 / value)
        halo_c[pl.ds(ny, tile), :] = edge_c[nx - 1, pl.ds(1, tile), :]

        def comp(x, t, k):
            if x == nx:
                return halo_c[pl.ds(tile * t + k, tile), :]
            if k == 1 and t == ny // tile - 1:
                return edge_c[x, pl.ds(1, tile), :]
            return comps[x, pl.ds(tile * t + k, tile), :]

    for x in range(nx):
        for t in range(ny // tile):
            rows = pl.ds(tile * t, tile)
            d = Differences(x, t, lane)
            if step == 0:
                here = comp(x, t, 0)
                next_x, next_y = comp(x + 1, t, 0), comp(x, t, 1)
                pair_x, pair_y = here + next_x, here + next_y
                four = 4.0 * time_step
                if x == nx - 1 and t == ny // tile - 1:
                    shears[0, x, rows, :] = pair_x + next_y
                else:
                    shears[0, x, rows, :] = four / (pair_x + (next_y + comp(x + 1, t, 1)))
                shears[1, x, rows, :] = four / (pair_x + z_shift(pair_x, 1, lane))
                shears[2, x, rows, :] = four / (pair_y + z_shift(pair_y, 1, lane))
            whole_y = inner_tile(t, ny)
            whole_x = inner_plane(x, -1, nx)
            zero = jnp.zeros((tile, 128), jnp.float32)
            strains = [d.dx(vx, -1) if whole_x else zero, d.dy(vy, -1) if whole_y else zero, d.dz(vz, -1)]
            if whole_x and whole_y:
                strains = new_normal(stress, lam, shear, x, rows, strains)
            for c in range(3):
                out[c, x, rows, :] = strains[c]
            whole_x = inner_plane(x, 0, nx)
            total = zero
            if whole_y:
                total += d.dy(vx, 0)
            if whole_x:
                total += d.dx(vy, 0)
            if whole_x and whole_y:
                total = stress[3, x, rows, :] + shears[0, x, rows, :] * total
            out[3, x, rows, :] = total
            total = d.dz(vx, 0)
            if whole_x:
                total = stress[4, x, rows, :] + shears[1, x, rows, :] * (total + d.dx(vz, 0))
            out[4, x, rows, :] = total
            total = d.dz(vy, 0)
            if whole_y:
                total = stress[5, x, rows, :] + shears[2, x, rows, :] * (total + d.dy(vz, 0))
            out[5, x, rows, :] = total
    if step == 1:
        copy.wait()


def stress_edges(step, *refs):
    if step == 0:
        (velocity, stress, lam, shear, halo_c, shears, part, ax, bx, ay, by,
         out, shear_end, pax, pbx, pay, pby, low_x, high_x, low_y, high_y, edges, corner) = refs
    else:
        (velocity, stress, lam, shear, shears, shear_end, part, ax, bx, ay, by,
         final_stress, low_x, high_x, low_y, high_y, edges, out, sems) = refs
    nx, ny = stress.shape[1], stress.shape[2]
    even_x, even_y, _, _ = receive((ax, bx, ay, by), (low_x, high_x, low_y, high_y))
    fill_edges(velocity, 1, edges.at[0], low_y, high_y, 0, 2, 0, 1)
    fill_edges(velocity, 0, edges.at[1], low_y, high_y, 2, 1, 1, 2)
    fill_edges(velocity, 2, edges.at[2], low_y, high_y, 3, 1, 3, 2)
    vx, vy, vz = stress_fields(velocity, low_x, high_x, edges)
    lane = lanes()
    if step == 0:
        last = pl.ds(ny - tile, tile)
        corner[pl.ds(0, tile), :] = halo_c[last, :]
        corner[pl.ds(tile, 1), :] = high_x[pl.ds(5 * ny, 1), :]
        shear_end[...] = (4.0 * time_step) / (shears[0, nx - 1, last, :] + corner[pl.ds(1, tile), :])
    copies = []
    for x in sorted(range(nx), key=lambda x: not inner_plane(x, 0, nx) or not inner_plane(x, -1, nx)):
        for t in range(ny // tile):
            rows = pl.ds(tile * t, tile)
            d = Differences(x, t, lane)
            whole_y = inner_tile(t, ny)
            whole_x = inner_plane(x, -1, nx)
            strains = [part[c, x, rows, :] for c in range(3)]
            if not (whole_x and whole_y):
                if not whole_x:
                    strains[0] = d.dx(vx, -1)
                if not whole_y:
                    strains[1] = d.dy(vy, -1)
                strains = new_normal(stress, lam, shear, x, rows, strains)
            for c in range(3):
                out[c, x, rows, :] = strains[c]
            whole_x = inner_plane(x, 0, nx)
            total = part[3, x, rows, :]
            if not (whole_x and whole_y):
                if not whole_y:
                    total += d.dy(vx, 0)
                if not whole_x:
                    total += d.dx(vy, 0)
                at_end = x == nx - 1 and t == ny // tile - 1
                factor = shear_end[...] if at_end else shears[0, x, rows, :]
                total = stress[3, x, rows, :] + factor * total
            out[3, x, rows, :] = total
            total = part[4, x, rows, :]
            if not whole_x:
                total = stress[4, x, rows, :] + shears[1, x, rows, :] * (total + d.dx(vz, 0))
            out[4, x, rows, :] = total
            total = part[5, x, rows, :]
            if not whole_y:
                total = stress[5, x, rows, :] + shears[2, x, rows, :] * (total + d.dy(vz, 0))
            out[5, x, rows, :] = total
        if step == 1:
            copy = pltpu.make_async_copy(out.at[:, x], final_stress.at[:, x], sems.at[x])
            copy.start()
            copies.append(copy)
    for copy in copies:
        copy.wait()
    if step == 0:
        Pack(pax, pbx, even_x).put(
            put_planes([(out, 3, nx - 2), (out, 3, nx - 1), (out, 4, nx - 2), (out, 4, nx - 1), (out, 0, nx - 1)]),
            put_planes([(out, 3, 0), (out, 4, 0), (out, 0, 0), (out, 0, 1)]),
        )
        Pack(pay, pby, even_y).put(
            put_rows([(out, 3, ny - 2, 2), (out, 5, ny - 2, 2), (out, 1, ny - 1, 1)], nx),
            put_rows([(out, 3, 0, 1), (out, 5, 0, 1), (out, 1, 0, 2)], nx),
        )


def call(kernel, outs, scratch, args, flops, hbm_in=(), hbm_out=()):
    def spec(far_away):
        return pl.BlockSpec(memory_space=pltpu.HBM if far_away else pltpu.VMEM)

    scratch = [pltpu.VMEM(shape, jnp.float32) if isinstance(shape, tuple) else shape for shape in scratch]
    return pl.pallas_call(
        kernel,
        out_shape=[jax.ShapeDtypeStruct(shape, jnp.float32) for shape in outs],
        in_specs=[spec(n in hbm_in) for n in range(len(args))],
        out_specs=[spec(n in hbm_out) for n in range(len(outs))],
        scratch_shapes=scratch,
        compiler_params=pltpu.CompilerParams(vmem_limit_bytes=16 * 1024 * 1024),
        cost_estimate=pl.CostEstimate(flops=flops, bytes_accessed=2 * 1024 * 1024, transcendentals=0),
    )(*args)


def per_device(velocity, stress, density, lame_lambda, lame_mu):
    _, nx, ny, nz = velocity.shape
    routes = pairings(lax.axis_size("gx"), lax.axis_size("gy"))
    cells = nx * ny * nz
    one, three = (1, nx, ny, nz), (3, nx, ny, nz)
    dma = pltpu.SemaphoreType.DMA

    def packages(x_rows):
        return [(x_rows, nz)] * 2 + [(nx * tile, nz)] * 2

    def exchange(arrays):
        return [lax.ppermute(array, AXES, route) for array, route in zip(arrays, routes)]

    def halos(x_rows):
        return packages(x_rows) + [(3, 2, nx, 2 * tile, nz)]

    def kernel(function, step):
        return lambda *refs: function(step, *refs)

    first, second, later = 6 * ny, 5 * ny + tile, 5 * ny
    packed = call(
        first_pack, packages(first), [(8, nx, tile, nz), dma((3, 8))],
        (stress, density, lame_mu), cells, hbm_in=(0, 1, 2))
    got = exchange(packed)
    part, buoy, buoys = call(
        kernel(velocity_inside, 0), [three, one, three], [], (velocity, stress, density), 60 * cells)
    new_velocity, buoys_end, *packed = call(
        kernel(velocity_edges, 0), [three, (ny + nx * tile, nz)] + packages(second), halos(first) + [(2 * tile, nz)],
        (velocity, stress, buoy, buoys, part, *got), 20 * cells)
    materials = got
    got = exchange(packed)
    part, shears, halo_c = call(
        kernel(stress_inside, 0), [stress.shape, three, (ny + tile, nz)], [(nx, ny, nz), (nx, 2 * tile, nz)],
        (new_velocity, stress, lame_lambda, lame_mu, *materials), 80 * cells)
    new_stress, shear_end, *packed = call(
        kernel(stress_edges, 0), [stress.shape, (tile, nz)] + packages(later), halos(second) + [(2 * tile, nz)],
        (new_velocity, stress, lame_lambda, lame_mu, halo_c, shears, part, *got), 20 * cells)
    velocity, stress = new_velocity, new_stress
    got = exchange(packed)
    (part,) = call(
        kernel(velocity_inside, 1), [three], [], (velocity, stress, buoys), 60 * cells)
    velocity, *packed = call(
        kernel(velocity_edges, 1), [three] + packages(later), halos(later),
        (velocity, stress, buoys, buoys_end, part, *got), 20 * cells)
    got = exchange(packed)
    part, final_velocity = call(
        kernel(stress_inside, 1), [stress.shape, three], [dma],
        (velocity, stress, lame_lambda, lame_mu, shears), 80 * cells, hbm_out=(1,))
    (final_stress,) = call(
        kernel(stress_edges, 1), [stress.shape], halos(later) + [stress.shape, dma((nx,))],
        (velocity, stress, lame_lambda, lame_mu, shears, shear_end, part, *got), 20 * cells, hbm_out=(0,))
    return (final_velocity, final_stress)


def solution(mesh):
    in_specs = (
        P(None, "gx", "gy", None),
        P(None, "gx", "gy", None),
        P("gx", "gy", None),
        P("gx", "gy", None),
        P("gx", "gy", None),
    )
    out_specs = (P(None, "gx", "gy", None), P(None, "gx", "gy", None))
    return jax.shard_map(
        per_device, mesh=mesh, in_specs=in_specs, out_specs=out_specs, check_vma=False
    )
```

```python
import jax
import jax.numpy as jnp
from jax import lax
from jax.experimental import pallas as pl
from jax.experimental.pallas import tpu as pltpu
from jax.sharding import PartitionSpec as P

near = 9.0 / 8.0
far = 1.0 / 24.0
time_step = 0.25
tile = 8
AXES = ("gx", "gy")


def pairings(count_x, count_y):
    other = 2 if count_x % 4 == 0 else 1

    def across(i, count):
        return ((i + 1) ^ 1) - 1

    def route(rule):
        pairs = []
        for i in range(count_x):
            for j in range(count_y):
                ti, tj = rule(i, j)
                pairs.append((i * count_y + j, ti * count_y + tj))
        return pairs

    def inner_x(i, j):
        return (i ^ 1, j)

    def outer_x(i, j):
        return (across(i, count_x), j) if 0 < i < count_x - 1 else (i, j ^ 1)

    def inner_y(i, j):
        return (i, j ^ 1)

    def outer_y(i, j):
        return (i, across(j, count_y)) if 0 < j < count_y - 1 else (i ^ other, j)

    return [route(rule) for rule in (inner_x, outer_x, inner_y, outer_y)]


def position():
    i, j = lax.axis_index("gx"), lax.axis_index("gy")
    return i, j, lax.rem(i, 2) == 0, lax.rem(j, 2) == 0


def unpack(inner, outer, low, high, even, first, last):
    for start in range(0, inner.shape[0], tile):
        rows = pl.ds(start, tile)
        a, b = inner[rows, :], outer[rows, :]
        low[rows, :] = jnp.where(first, 0.0, jnp.where(even, b, a))
        high[rows, :] = jnp.where(last, 0.0, jnp.where(even, a, b))


class Pack:
    def __init__(self, inner, outer, even):
        self.inner, self.outer, self.even = inner, outer, even

    def put(self, up, down):
        even, inner, outer = self.even, self.inner, self.outer

        @pl.when(even)
        def _():
            up(inner)
            down(outer)

        @pl.when(jnp.logical_not(even))
        def _():
            up(outer)
            down(inner)


def put_planes(items):
    def put(out):
        start = 0
        for ref, f, x in items:
            value = ref[f, x]
            out[pl.ds(start, value.shape[0]), :] = value
            start += value.shape[0]

    return put


def put_rows(items, count_x):
    def put(out):
        for x in range(count_x):
            start = tile * x
            for ref, f, row, count in items:
                out[pl.ds(start, count), :] = ref[f, x, pl.ds(row, count), :]
                start += count

    return put


def sides(i, j):
    return i == 0, i == lax.axis_size("gx") - 1, j == 0, j == lax.axis_size("gy") - 1


def lanes():
    return lax.broadcasted_iota(jnp.int32, (tile, 128), 1)


def z_shift(value, k, lane):
    size = value.shape[-1]
    moved = pltpu.roll(value, (-k) % size, 1)
    inside = lane < size - k if k > 0 else lane >= -k
    return jnp.where(inside, moved, 0.0)


def difference(at, base):
    return near * (at(base + 1) - at(base)) - far * (at(base + 2) - at(base - 1))


class Field:
    def __init__(self, ref, f, low_x=None, high_x=None, edge=None):
        self.ref, self.f = ref, f
        self.low_x, self.high_x, self.edge = low_x, high_x, edge

    def at(self, x, t):
        nx, ny = self.ref.shape[-3], self.ref.shape[-2]
        if x < 0:
            ref, index = self.low_x
            return ref[pl.ds(ny * (index + x) + tile * t, tile), :]
        if x >= nx:
            ref, index = self.high_x
            return ref[pl.ds(ny * (index + x - nx) + tile * t, tile), :]
        return self.ref[self.f, x, pl.ds(tile * t, tile), :]

    def y(self, x, t, k):
        ny = self.ref.shape[-2]
        start = tile * t + k
        if start < 0:
            return self.edge[0, x, pl.ds(tile + k, tile), :]
        if start + tile > ny:
            return self.edge[1, x, pl.ds(k, tile), :]
        return self.ref[self.f, x, pl.ds(start, tile), :]


class Differences:
    def __init__(self, x, t, lane):
        self.x, self.t, self.lane = x, t, lane

    def dx(self, field, base):
        return difference(lambda k: field.at(self.x + k, self.t), base)

    def dy(self, field, base):
        return difference(lambda k: field.y(self.x, self.t, k), base)

    def dz(self, field, base):
        value = field.at(self.x, self.t)
        return difference(lambda k: z_shift(value, k, self.lane) if k else value, base)


def inner_plane(x, base, nx):
    return x + base - 1 >= 0 and x + base + 2 < nx


def inner_tile(t, ny):
    return 0 < t < ny // tile - 1


def fill_edges(ref, f, edge, lows, highs, low_row, low_count, high_row, high_count):
    nx, ny = ref.shape[-3], ref.shape[-2]
    for x in range(nx):
        if low_count:
            edge[0, x, pl.ds(tile - low_count, low_count), :] = lows[pl.ds(tile * x + low_row, low_count), :]
            edge[0, x, pl.ds(tile, tile), :] = ref[f, x, pl.ds(0, tile), :]
        if high_count:
            edge[1, x, pl.ds(0, tile), :] = ref[f, x, pl.ds(ny - tile, tile), :]
            edge[1, x, pl.ds(tile, high_count), :] = highs[pl.ds(tile * x + high_row, high_count), :]


def receive(got, halos):
    i, j, even_x, even_y = position()
    ax, bx, ay, by = got
    low_x, high_x, low_y, high_y = halos
    first_x, last_x, first_y, last_y = sides(i, j)
    unpack(ax, bx, low_x, high_x, even_x, first_x, last_x)
    unpack(ay, by, low_y, high_y, even_y, first_y, last_y)
    return even_x, even_y, last_x, last_y


def first_pack(stress, density, shear, ax, bx, ay, by, tiles, sems):
    i, j, even_x, even_y = position()
    nx, ny = density.shape[0], density.shape[1]
    planes_up = [(stress, 3, nx - 2), (stress, 3, nx - 1), (stress, 4, nx - 2), (stress, 4, nx - 1), (stress, 0, nx - 1)]
    planes_down = [(stress, 3, 0), (stress, 4, 0), (stress, 0, 0), (stress, 0, 1), (density, None, 0), (shear, None, 0)]
    columns = [(stress, 3, ny - tile), (stress, 5, ny - tile), (stress, 1, ny - tile),
               (stress, 3, 0), (stress, 5, 0), (stress, 1, 0), (density, None, 0), (shear, None, 0)]

    def plane_copies(items, out, sem):
        copies = []
        for n, (ref, f, x) in enumerate(items):
            source = ref.at[x] if f is None else ref.at[f, x]
            copies.append(pltpu.make_async_copy(source, out.at[pl.ds(n * ny, ny), :], sem.at[n]))
        return copies

    copies = []
    for n, (ref, f, row) in enumerate(columns):
        source = ref if f is None else ref.at[f]
        copies.append(pltpu.make_async_copy(source.at[:, pl.ds(row, tile), :], tiles.at[n], sems.at[2, n]))
    for copy in copies:
        copy.start()

    @pl.when(even_x)
    def _():
        for copy in plane_copies(planes_up, ax, sems.at[0]) + plane_copies(planes_down, bx, sems.at[1]):
            copy.start()

    @pl.when(jnp.logical_not(even_x))
    def _():
        for copy in plane_copies(planes_up, bx, sems.at[0]) + plane_copies(planes_down, ax, sems.at[1]):
            copy.start()

    for copy in copies:
        copy.wait()
    Pack(ay, by, even_y).put(
        put_rows([(tiles, 0, tile - 2, 2), (tiles, 1, tile - 2, 2), (tiles, 2, tile - 1, 1)], nx),
        put_rows([(tiles, 3, 0, 1), (tiles, 4, 0, 1), (tiles, 5, 0, 2), (tiles, 6, 0, 1), (tiles, 7, 0, 1)], nx),
    )
    for copy in plane_copies(planes_up, ax, sems.at[0]) + plane_copies(planes_down, bx, sems.at[1]):
        copy.wait()


def velocity_terms(stress, low_x, high_x, edges):
    xx = Field(stress, 0, (low_x, 5), (high_x, 2))
    yy = Field(stress, 1, edge=edges.at[2] if edges is not None else None)
    zz = Field(stress, 2)
    xy = Field(stress, 3, (low_x, 2), (high_x, 0), edges.at[0] if edges is not None else None)
    xz = Field(stress, 4, (low_x, 4), (high_x, 1))
    yz = Field(stress, 5, edge=edges.at[1] if edges is not None else None)
    return ((xx, 0), (xy, -1), (xz, -1)), ((xy, -1), (yy, 0), (yz, -1)), ((xz, -1), (yz, -1), (zz, 0))


def velocity_inside(step, *refs):
    if step == 0:
        velocity, stress, density, out, buoy, buoys = refs
    else:
        velocity, stress, buoys, out = refs
    nx, ny = stress.shape[1], stress.shape[2]
    lane = lanes()
    terms = velocity_terms(stress, None, None, None)
    if step == 0:
        for x in range(nx):
            buoy[0, x] = 1.0 / density[x]
        buoy_field = Field(buoy, 0)
    for x in range(nx):
        for t in range(ny // tile):
            rows = pl.ds(tile * t, tile)
            d = Differences(x, t, lane)
            if step == 0:
                here = buoy_field.at(x, t)
                half = 0.5 * time_step
                if x < nx - 1:
                    buoys[0, x, rows, :] = half * (here + buoy_field.at(x + 1, t))
                if t < ny // tile - 1:
                    buoys[1, x, rows, :] = half * (here + buoy_field.y(x, t, 1))
                buoys[2, x, rows, :] = half * (here + z_shift(here, 1, lane))
            for c, ((fx, sx), (fy, sy), (fz, sz)) in enumerate(terms):
                total = d.dz(fz, sz)
                whole_x, whole_y = inner_plane(x, sx, nx), inner_tile(t, ny)
                if whole_x:
                    total += d.dx(fx, sx)
                if whole_y:
                    total += d.dy(fy, sy)
                if whole_x and whole_y:
                    total = velocity[c, x, rows, :] + buoys[c, x, rows, :] * total
                out[c, x, rows, :] = total


def velocity_edges(step, *refs):
    if step == 0:
        (velocity, stress, buoy, buoys, part, ax, bx, ay, by, out, buoys_end, pax, pbx, pay, pby,
         low_x, high_x, low_y, high_y, edges, edge_b) = refs
    else:
        (velocity, stress, buoys, buoys_end, part, ax, bx, ay, by, out, pax, pbx, pay, pby,
         low_x, high_x, low_y, high_y, edges) = refs
    nx, ny = stress.shape[1], stress.shape[2]
    even_x, even_y, last_x, last_y = receive((ax, bx, ay, by), (low_x, high_x, low_y, high_y))
    fill_edges(stress, 3, edges.at[0], low_y, high_y, 0, 2, 0, 1)
    fill_edges(stress, 5, edges.at[1], low_y, high_y, 2, 2, 1, 1)
    fill_edges(stress, 1, edges.at[2], low_y, high_y, 4, 1, 2, 2)
    terms = velocity_terms(stress, low_x, high_x, edges)
    lane = lanes()
    if step == 0:
        half = 0.5 * time_step
        for t in range(ny // tile):
            rows = pl.ds(tile * t, tile)
            above = jnp.where(last_x, 0.0, 1.0 / jnp.where(last_x, 1.0, high_x[pl.ds(4 * ny + tile * t, tile), :]))
            buoys_end[rows, :] = half * (buoy[0, nx - 1, rows, :] + above)
        rows = pl.ds(ny - tile, tile)
        for x in range(nx):
            here = buoy[0, x, rows, :]
            row = high_y[pl.ds(tile * x + 4, 1), :]
            edge_b[pl.ds(0, tile), :] = here
            edge_b[pl.ds(tile, 1), :] = jnp.where(last_y, 0.0, 1.0 / jnp.where(last_y, 1.0, row))
            buoys_end[pl.ds(ny + tile * x, tile), :] = half * (here + edge_b[pl.ds(1, tile), :])
    for x in range(nx):
        for t in range(ny // tile):
            rows = pl.ds(tile * t, tile)
            d = Differences(x, t, lane)
            for c, ((fx, sx), (fy, sy), _) in enumerate(terms):
                whole_x, whole_y = inner_plane(x, sx, nx), inner_tile(t, ny)
                total = part[c, x, rows, :]
                if whole_x and whole_y:
                    out[c, x, rows, :] = total
                    continue
                if not whole_x:
                    total += d.dx(fx, sx)
                if not whole_y:
                    total += d.dy(fy, sy)
                if c == 0 and x == nx - 1:
                    factor = buoys_end[rows, :]
                elif c == 1 and t == ny // tile - 1:
                    factor = buoys_end[pl.ds(ny + tile * x, tile), :]
                else:
                    factor = buoys[c, x, rows, :]
                out[c, x, rows, :] = velocity[c, x, rows, :] + factor * total

    planes_down = put_planes([(out, 0, 0), (out, 1, 0), (out, 1, 1), (out, 2, 0), (out, 2, 1)])

    def down(package):
        planes_down(package)
        if step == 0:
            row = high_y[pl.ds(5, 1), :]
            package[pl.ds(5 * ny, 1), :] = jnp.where(last_y, 0.0, 1.0 / jnp.where(last_y, 1.0, row))

    Pack(pax, pbx, even_x).put(
        put_planes([(out, 0, nx - 2), (out, 0, nx - 1), (out, 1, nx - 1), (out, 2, nx - 1)]), down)
    Pack(pay, pby, even_y).put(
        put_rows([(out, 1, ny - 2, 2), (out, 0, ny - 1, 1), (out, 2, ny - 1, 1)], nx),
        put_rows([(out, 1, 0, 1), (out, 0, 0, 2), (out, 2, 0, 2)], nx),
    )


def stress_fields(velocity, low_x, high_x, edges):
    vx = Field(velocity, 0, (low_x, 2), (high_x, 0), edges.at[1] if edges is not None else None)
    vy = Field(velocity, 1, (low_x, 3), (high_x, 1), edges.at[0] if edges is not None else None)
    vz = Field(velocity, 2, (low_x, 4), (high_x, 3), edges.at[2] if edges is not None else None)
    return vx, vy, vz


def new_normal(stress, lam, shear, x, rows, strains):
    la = time_step * lam[x, rows, :]
    two = (2.0 * time_step) * shear[x, rows, :]
    common = la * (strains[0] + strains[1] + strains[2])
    return [stress[c, x, rows, :] + (common + two * strains[c]) for c in range(3)]


def stress_inside(step, *refs):
    if step == 0:
        velocity, stress, lam, shear, ax, bx, ay, by, out, shears, halo_c, comps, edge_c = refs
    else:
        velocity, stress, lam, shear, shears, out, final_velocity, sem = refs
    nx, ny = stress.shape[1], stress.shape[2]
    lane = lanes()
    vx, vy, vz = stress_fields(velocity, None, None, None)
    if step == 1:
        copy = pltpu.make_async_copy(velocity, final_velocity, sem)
        copy.start()
    if step == 0:
        i, j, even_x, even_y = position()
        _, last_x, _, last_y = sides(i, j)
        for x in range(nx):
            comps[x] = 1.0 / shear[x]
            edge_c[x, pl.ds(0, tile), :] = comps[x, pl.ds(ny - tile, tile), :]
            row = pl.ds(tile * x + 5, 1)
            value = jnp.where(last_y, 1.0, jnp.where(even_y, ay[row, :], by[row, :]))
            edge_c[x, pl.ds(tile, 1), :] = jnp.where(last_y, 0.0, 1.0 / value)
        for t in range(ny // tile):
            rows = pl.ds(5 * ny + tile * t, tile)
            value = jnp.where(last_x, 1.0, jnp.where(even_x, ax[rows, :], bx[rows, :]))
            halo_c[pl.ds(tile * t, tile), :] = jnp.where(last_x, 0.0, 1.0 / value)
        halo_c[pl.ds(ny, tile), :] = edge_c[nx - 1, pl.ds(1, tile), :]

        def comp(x, t, k):
            if x == nx:
                return halo_c[pl.ds(tile * t + k, tile), :]
            if k == 1 and t == ny // tile - 1:
                return edge_c[x, pl.ds(1, tile), :]
            return comps[x, pl.ds(tile * t + k, tile), :]

    for x in range(nx):
        for t in range(ny // tile):
            rows = pl.ds(tile * t, tile)
            d = Differences(x, t, lane)
            if step == 0:
                here = comp(x, t, 0)
                next_x, next_y = comp(x + 1, t, 0), comp(x, t, 1)
                pair_x, pair_y = here + next_x, here + next_y
                four = 4.0 * time_step
                if x == nx - 1 and t == ny // tile - 1:
                    shears[0, x, rows, :] = pair_x + next_y
                else:
                    shears[0, x, rows, :] = four / (pair_x + (next_y + comp(x + 1, t, 1)))
                shears[1, x, rows, :] = four / (pair_x + z_shift(pair_x, 1, lane))
                shears[2, x, rows, :] = four / (pair_y + z_shift(pair_y, 1, lane))
            whole_y = inner_tile(t, ny)
            whole_x = inner_plane(x, -1, nx)
            zero = jnp.zeros((tile, 128), jnp.float32)
            strains = [d.dx(vx, -1) if whole_x else zero, d.dy(vy, -1) if whole_y else zero, d.dz(vz, -1)]
            if whole_x and whole_y:
                strains = new_normal(stress, lam, shear, x, rows, strains)
            for c in range(3):
                out[c, x, rows, :] = strains[c]
            whole_x = inner_plane(x, 0, nx)
            total = zero
            if whole_y:
                total += d.dy(vx, 0)
            if whole_x:
                total += d.dx(vy, 0)
            if whole_x and whole_y:
                total = stress[3, x, rows, :] + shears[0, x, rows, :] * total
            out[3, x, rows, :] = total
            total = d.dz(vx, 0)
            if whole_x:
                total = stress[4, x, rows, :] + shears[1, x, rows, :] * (total + d.dx(vz, 0))
            out[4, x, rows, :] = total
            total = d.dz(vy, 0)
            if whole_y:
                total = stress[5, x, rows, :] + shears[2, x, rows, :] * (total + d.dy(vz, 0))
            out[5, x, rows, :] = total
    if step == 1:
        copy.wait()


def stress_edges(step, *refs):
    if step == 0:
        (velocity, stress, lam, shear, halo_c, shears, part, ax, bx, ay, by,
         out, shear_end, pax, pbx, pay, pby, low_x, high_x, low_y, high_y, edges, corner) = refs
    else:
        (velocity, stress, lam, shear, shears, shear_end, part, ax, bx, ay, by,
         final_stress, low_x, high_x, low_y, high_y, edges, out, sems) = refs
    nx, ny = stress.shape[1], stress.shape[2]
    even_x, even_y, _, _ = receive((ax, bx, ay, by), (low_x, high_x, low_y, high_y))
    fill_edges(velocity, 1, edges.at[0], low_y, high_y, 0, 2, 0, 1)
    fill_edges(velocity, 0, edges.at[1], low_y, high_y, 2, 1, 1, 2)
    fill_edges(velocity, 2, edges.at[2], low_y, high_y, 3, 1, 3, 2)
    vx, vy, vz = stress_fields(velocity, low_x, high_x, edges)
    lane = lanes()
    if step == 0:
        last = pl.ds(ny - tile, tile)
        corner[pl.ds(0, tile), :] = halo_c[last, :]
        corner[pl.ds(tile, 1), :] = high_x[pl.ds(5 * ny, 1), :]
        shear_end[...] = (4.0 * time_step) / (shears[0, nx - 1, last, :] + corner[pl.ds(1, tile), :])
    copies = []
    for x in sorted(range(nx), key=lambda x: not inner_plane(x, 0, nx) or not inner_plane(x, -1, nx)):
        for t in range(ny // tile):
            rows = pl.ds(tile * t, tile)
            d = Differences(x, t, lane)
            whole_y = inner_tile(t, ny)
            whole_x = inner_plane(x, -1, nx)
            strains = [part[c, x, rows, :] for c in range(3)]
            if not (whole_x and whole_y):
                if not whole_x:
                    strains[0] = d.dx(vx, -1)
                if not whole_y:
                    strains[1] = d.dy(vy, -1)
                strains = new_normal(stress, lam, shear, x, rows, strains)
            for c in range(3):
                out[c, x, rows, :] = strains[c]
            whole_x = inner_plane(x, 0, nx)
            total = part[3, x, rows, :]
            if not (whole_x and whole_y):
                if not whole_y:
                    total += d.dy(vx, 0)
                if not whole_x:
                    total += d.dx(vy, 0)
                at_end = x == nx - 1 and t == ny // tile - 1
                factor = shear_end[...] if at_end else shears[0, x, rows, :]
                total = stress[3, x, rows, :] + factor * total
            out[3, x, rows, :] = total
            total = part[4, x, rows, :]
            if not whole_x:
                total = stress[4, x, rows, :] + shears[1, x, rows, :] * (total + d.dx(vz, 0))
            out[4, x, rows, :] = total
            total = part[5, x, rows, :]
            if not whole_y:
                total = stress[5, x, rows, :] + shears[2, x, rows, :] * (total + d.dy(vz, 0))
            out[5, x, rows, :] = total
        if step == 1:
            copy = pltpu.make_async_copy(out.at[:, x], final_stress.at[:, x], sems.at[x])
            copy.start()
            copies.append(copy)
    for copy in copies:
        copy.wait()
    if step == 0:
        Pack(pax, pbx, even_x).put(
            put_planes([(out, 3, nx - 2), (out, 3, nx - 1), (out, 4, nx - 2), (out, 4, nx - 1), (out, 0, nx - 1)]),
            put_planes([(out, 3, 0), (out, 4, 0), (out, 0, 0), (out, 0, 1)]),
        )
        Pack(pay, pby, even_y).put(
            put_rows([(out, 3, ny - 2, 2), (out, 5, ny - 2, 2), (out, 1, ny - 1, 1)], nx),
            put_rows([(out, 3, 0, 1), (out, 5, 0, 1), (out, 1, 0, 2)], nx),
        )


def call(kernel, outs, scratch, args, flops, hbm_in=(), hbm_out=()):
    def spec(far_away):
        return pl.BlockSpec(memory_space=pltpu.HBM if far_away else pltpu.VMEM)

    scratch = [pltpu.VMEM(shape, jnp.float32) if isinstance(shape, tuple) else shape for shape in scratch]
    args = [pltpu.with_memory_space_constraint(a, pltpu.HBM) if n in hbm_in else a for n, a in enumerate(args)]
    return pl.pallas_call(
        kernel,
        out_shape=[(pltpu.HBM if n in hbm_out else pltpu.VMEM)(shape, jnp.float32) for n, shape in enumerate(outs)],
        in_specs=[spec(n in hbm_in) for n in range(len(args))],
        out_specs=[spec(n in hbm_out) for n in range(len(outs))],
        scratch_shapes=scratch,
        compiler_params=pltpu.CompilerParams(vmem_limit_bytes=16 * 1024 * 1024),
        cost_estimate=pl.CostEstimate(flops=flops, bytes_accessed=2 * 1024 * 1024, transcendentals=0),
    )(*args)


def per_device(velocity, stress, density, lame_lambda, lame_mu):
    _, nx, ny, nz = velocity.shape
    routes = pairings(lax.axis_size("gx"), lax.axis_size("gy"))
    cells = nx * ny * nz
    one, three = (1, nx, ny, nz), (3, nx, ny, nz)
    dma = pltpu.SemaphoreType.DMA

    def packages(x_rows):
        return [(x_rows, nz)] * 2 + [(nx * tile, nz)] * 2

    def exchange(arrays):
        return [lax.ppermute(array, AXES, route) for array, route in zip(arrays, routes)]

    def halos(x_rows):
        return packages(x_rows) + [(3, 2, nx, 2 * tile, nz)]

    def kernel(function, step):
        return lambda *refs: function(step, *refs)

    first, second, later = 6 * ny, 5 * ny + tile, 5 * ny
    packed = call(
        first_pack, packages(first), [(8, nx, tile, nz), dma((3, 8))],
        (stress, density, lame_mu), cells, hbm_in=(0, 1, 2))
    got = exchange(packed)
    part, buoy, buoys = call(
        kernel(velocity_inside, 0), [three, one, three], [], (velocity, stress, density), 60 * cells)
    new_velocity, buoys_end, *packed = call(
        kernel(velocity_edges, 0), [three, (ny + nx * tile, nz)] + packages(second), halos(first) + [(2 * tile, nz)],
        (velocity, stress, buoy, buoys, part, *got), 20 * cells)
    materials = got
    got = exchange(packed)
    part, shears, halo_c = call(
        kernel(stress_inside, 0), [stress.shape, three, (ny + tile, nz)], [(nx, ny, nz), (nx, 2 * tile, nz)],
        (new_velocity, stress, lame_lambda, lame_mu, *materials), 80 * cells)
    new_stress, shear_end, *packed = call(
        kernel(stress_edges, 0), [stress.shape, (tile, nz)] + packages(later), halos(second) + [(2 * tile, nz)],
        (new_velocity, stress, lame_lambda, lame_mu, halo_c, shears, part, *got), 20 * cells)
    velocity, stress = new_velocity, new_stress
    got = exchange(packed)
    (part,) = call(
        kernel(velocity_inside, 1), [three], [], (velocity, stress, buoys), 60 * cells)
    velocity, *packed = call(
        kernel(velocity_edges, 1), [three] + packages(later), halos(later),
        (velocity, stress, buoys, buoys_end, part, *got), 20 * cells)
    got = exchange(packed)
    part, final_velocity = call(
        kernel(stress_inside, 1), [stress.shape, three], [dma],
        (velocity, stress, lame_lambda, lame_mu, shears), 80 * cells, hbm_out=(1,))
    (final_stress,) = call(
        kernel(stress_edges, 1), [stress.shape], halos(later) + [stress.shape, dma((nx,))],
        (velocity, stress, lame_lambda, lame_mu, shears, shear_end, part, *got), 20 * cells, hbm_out=(0,))
    return (final_velocity, final_stress)


def solution(mesh):
    in_specs = (
        P(None, "gx", "gy", None),
        P(None, "gx", "gy", None),
        P("gx", "gy", None),
        P("gx", "gy", None),
        P("gx", "gy", None),
    )
    out_specs = (P(None, "gx", "gy", None), P(None, "gx", "gy", None))
    return jax.shard_map(
        per_device, mesh=mesh, in_specs=in_specs, out_specs=out_specs, check_vma=False
    )
```

```python
import jax
import jax.numpy as jnp
from jax import lax
from jax.experimental import pallas as pl
from jax.experimental.pallas import tpu as pltpu
from jax.sharding import PartitionSpec as P

near = 9.0 / 8.0
far = 1.0 / 24.0
time_step = 0.25
tile = 8
AXES = ("gx", "gy")


def pairings(count_x, count_y):
    other = 2 if count_x % 4 == 0 else 1

    def across(i, count):
        return ((i + 1) ^ 1) - 1

    def route(rule):
        pairs = []
        for i in range(count_x):
            for j in range(count_y):
                ti, tj = rule(i, j)
                pairs.append((i * count_y + j, ti * count_y + tj))
        return pairs

    def inner_x(i, j):
        return (i ^ 1, j)

    def outer_x(i, j):
        return (across(i, count_x), j) if 0 < i < count_x - 1 else (i, j ^ 1)

    def inner_y(i, j):
        return (i, j ^ 1)

    def outer_y(i, j):
        return (i, across(j, count_y)) if 0 < j < count_y - 1 else (i ^ other, j)

    return [route(rule) for rule in (outer_x, inner_x, outer_y, inner_y)]


def position():
    i, j = lax.axis_index("gx"), lax.axis_index("gy")
    return i, j, lax.rem(i, 2) == 0, lax.rem(j, 2) == 0


def unpack(inner, outer, low, high, even, first, last):
    for start in range(0, inner.shape[0], tile):
        rows = pl.ds(start, tile)
        a, b = inner[rows, :], outer[rows, :]
        low[rows, :] = jnp.where(first, 0.0, jnp.where(even, b, a))
        high[rows, :] = jnp.where(last, 0.0, jnp.where(even, a, b))


class Pack:
    def __init__(self, inner, outer, even):
        self.inner, self.outer, self.even = inner, outer, even

    def put(self, up, down):
        even, inner, outer = self.even, self.inner, self.outer

        @pl.when(even)
        def _():
            up(inner)
            down(outer)

        @pl.when(jnp.logical_not(even))
        def _():
            up(outer)
            down(inner)


def put_planes(items):
    def put(out):
        start = 0
        for ref, f, x in items:
            value = ref[f, x]
            out[pl.ds(start, value.shape[0]), :] = value
            start += value.shape[0]

    return put


def put_rows(items, count_x):
    def put(out):
        each = out.shape[0] // count_x
        for x in range(count_x):
            start = each * x
            for ref, f, row, count in items:
                out[pl.ds(start, count), :] = ref[f, x, pl.ds(row, count), :]
                start += count

    return put


def sides(i, j):
    return i == 0, i == lax.axis_size("gx") - 1, j == 0, j == lax.axis_size("gy") - 1


def lanes():
    return lax.broadcasted_iota(jnp.int32, (tile, 128), 1)


def z_shift(value, k, lane):
    size = value.shape[-1]
    moved = pltpu.roll(value, (-k) % size, 1)
    inside = lane < size - k if k > 0 else lane >= -k
    return jnp.where(inside, moved, 0.0)


def difference(at, base):
    return near * (at(base + 1) - at(base)) - far * (at(base + 2) - at(base - 1))


class Field:
    def __init__(self, ref, f, low_x=None, high_x=None, edge=None):
        self.ref, self.f = ref, f
        self.low_x, self.high_x, self.edge = low_x, high_x, edge

    def at(self, x, t):
        nx, ny = self.ref.shape[-3], self.ref.shape[-2]
        if x < 0:
            ref, index = self.low_x
            return ref[pl.ds(ny * (index + x) + tile * t, tile), :]
        if x >= nx:
            ref, index = self.high_x
            return ref[pl.ds(ny * (index + x - nx) + tile * t, tile), :]
        return self.ref[self.f, x, pl.ds(tile * t, tile), :]

    def y(self, x, t, k):
        ny = self.ref.shape[-2]
        start = tile * t + k
        if start < 0:
            return self.edge[0, x, pl.ds(tile + k, tile), :]
        if start + tile > ny:
            return self.edge[1, x, pl.ds(k, tile), :]
        return self.ref[self.f, x, pl.ds(start, tile), :]


class Differences:
    def __init__(self, x, t, lane):
        self.x, self.t, self.lane = x, t, lane

    def dx(self, field, base):
        return difference(lambda k: field.at(self.x + k, self.t), base)

    def dy(self, field, base):
        return difference(lambda k: field.y(self.x, self.t, k), base)

    def dz(self, field, base):
        value = field.at(self.x, self.t)
        return difference(lambda k: z_shift(value, k, self.lane) if k else value, base)


def inner_plane(x, base, nx):
    return x + base - 1 >= 0 and x + base + 2 < nx


def inner_tile(t, ny):
    return 0 < t < ny // tile - 1


def fill_edges(ref, f, edge, lows, highs, low_row, low_count, high_row, high_count):
    nx, ny = ref.shape[-3], ref.shape[-2]
    each = lows.shape[0] // nx
    for x in range(nx):
        if low_count:
            edge[0, x, pl.ds(tile - low_count, low_count), :] = lows[pl.ds(each * x + low_row, low_count), :]
            edge[0, x, pl.ds(tile, tile), :] = ref[f, x, pl.ds(0, tile), :]
        if high_count:
            edge[1, x, pl.ds(0, tile), :] = ref[f, x, pl.ds(ny - tile, tile), :]
            edge[1, x, pl.ds(tile, high_count), :] = highs[pl.ds(each * x + high_row, high_count), :]


def receive(got, halos):
    i, j, even_x, even_y = position()
    bx, ax, by, ay = got
    low_x, high_x, low_y, high_y = halos
    first_x, last_x, first_y, last_y = sides(i, j)
    unpack(ax, bx, low_x, high_x, even_x, first_x, last_x)
    unpack(ay, by, low_y, high_y, even_y, first_y, last_y)
    return even_x, even_y, last_x, last_y


def first_pack(stress, density, shear, bx, ax, by, ay, tiles, sems):
    i, j, even_x, even_y = position()
    nx, ny = density.shape[0], density.shape[1]
    copies = [
        pltpu.make_async_copy(stress.at[:, :, pl.ds(ny - tile, tile), :], tiles.at[pl.ds(0, 6)], sems.at[0]),
        pltpu.make_async_copy(stress.at[:, :, pl.ds(0, tile), :], tiles.at[pl.ds(6, 6)], sems.at[0]),
        pltpu.make_async_copy(density.at[:, pl.ds(0, tile), :], tiles.at[12], sems.at[0]),
        pltpu.make_async_copy(shear.at[:, pl.ds(0, tile), :], tiles.at[13], sems.at[0]),
    ]
    for copy in copies:
        copy.start()

    def up(out):
        return [
            pltpu.make_async_copy(stress.at[f, x], out.at[pl.ds(n * ny, ny), :], sems.at[1])
            for n, (f, x) in enumerate([(3, nx - 2), (3, nx - 1), (4, nx - 2), (4, nx - 1), (0, nx - 1)])
        ]

    def down(out):
        sources = [stress.at[3, 0], stress.at[4, 0], stress.at[0, 0], stress.at[0, 1], density.at[0], shear.at[0]]
        return [
            pltpu.make_async_copy(source, out.at[pl.ds(n * ny, ny), :], sems.at[2])
            for n, source in enumerate(sources)
        ]

    @pl.when(even_x)
    def _():
        for copy in up(ax) + down(bx):
            copy.start()

    @pl.when(jnp.logical_not(even_x))
    def _():
        for copy in up(bx) + down(ax):
            copy.start()

    for copy in copies:
        copy.wait()
    Pack(ay, by, even_y).put(
        put_rows([(tiles, 3, tile - 2, 2), (tiles, 5, tile - 2, 2), (tiles, 1, tile - 1, 1)], nx),
        put_rows([(tiles, 9, 0, 1), (tiles, 11, 0, 1), (tiles, 7, 0, 2), (tiles, 12, 0, 1), (tiles, 13, 0, 1)], nx),
    )
    for copy in up(ax) + down(bx):
        copy.wait()


def velocity_terms(stress, low_x, high_x, edges):
    xx = Field(stress, 0, (low_x, 5), (high_x, 2))
    yy = Field(stress, 1, edge=edges.at[2] if edges is not None else None)
    zz = Field(stress, 2)
    xy = Field(stress, 3, (low_x, 2), (high_x, 0), edges.at[0] if edges is not None else None)
    xz = Field(stress, 4, (low_x, 4), (high_x, 1))
    yz = Field(stress, 5, edge=edges.at[1] if edges is not None else None)
    return ((xx, 0), (xy, -1), (xz, -1)), ((xy, -1), (yy, 0), (yz, -1)), ((xz, -1), (yz, -1), (zz, 0))


def velocity_inside(step, *refs):
    if step == 0:
        velocity, stress, density, out, buoy, buoys = refs
    else:
        velocity, stress, buoys, out = refs
    nx, ny = stress.shape[1], stress.shape[2]
    lane = lanes()
    terms = velocity_terms(stress, None, None, None)
    if step == 0:
        for x in range(nx):
            buoy[0, x] = 1.0 / density[x]
        buoy_field = Field(buoy, 0)
    for x in range(nx):
        for t in range(ny // tile):
            rows = pl.ds(tile * t, tile)
            d = Differences(x, t, lane)
            if step == 0:
                here = buoy_field.at(x, t)
                half = 0.5 * time_step
                if x < nx - 1:
                    buoys[0, x, rows, :] = half * (here + buoy_field.at(x + 1, t))
                if t < ny // tile - 1:
                    buoys[1, x, rows, :] = half * (here + buoy_field.y(x, t, 1))
                buoys[2, x, rows, :] = half * (here + z_shift(here, 1, lane))
            for c, ((fx, sx), (fy, sy), (fz, sz)) in enumerate(terms):
                total = d.dz(fz, sz)
                whole_x, whole_y = inner_plane(x, sx, nx), inner_tile(t, ny)
                if whole_x:
                    total += d.dx(fx, sx)
                if whole_y:
                    total += d.dy(fy, sy)
                if whole_x and whole_y:
                    total = velocity[c, x, rows, :] + buoys[c, x, rows, :] * total
                out[c, x, rows, :] = total


def velocity_edges(step, *refs):
    if step == 0:
        (velocity, stress, buoy, buoys, part, bx, ax, by, ay, out, buoys_end, pbx, pax, pby, pay,
         low_x, high_x, low_y, high_y, edges, edge_b) = refs
    else:
        (velocity, stress, buoys, buoys_end, part, bx, ax, by, ay, out, pbx, pax, pby, pay,
         low_x, high_x, low_y, high_y, edges) = refs
    nx, ny = stress.shape[1], stress.shape[2]
    even_x, even_y, last_x, last_y = receive((bx, ax, by, ay), (low_x, high_x, low_y, high_y))
    fill_edges(stress, 3, edges.at[0], low_y, high_y, 0, 2, 0, 1)
    fill_edges(stress, 5, edges.at[1], low_y, high_y, 2, 2, 1, 1)
    fill_edges(stress, 1, edges.at[2], low_y, high_y, 4, 1, 2, 2)
    terms = velocity_terms(stress, low_x, high_x, edges)
    lane = lanes()
    if step == 0:
        half = 0.5 * time_step
        for t in range(ny // tile):
            rows = pl.ds(tile * t, tile)
            above = jnp.where(last_x, 0.0, 1.0 / jnp.where(last_x, 1.0, high_x[pl.ds(4 * ny + tile * t, tile), :]))
            buoys_end[rows, :] = half * (buoy[0, nx - 1, rows, :] + above)
        rows = pl.ds(ny - tile, tile)
        for x in range(nx):
            here = buoy[0, x, rows, :]
            row = high_y[pl.ds(high_y.shape[0] // nx * x + 4, 1), :]
            edge_b[pl.ds(0, tile), :] = here
            edge_b[pl.ds(tile, 1), :] = jnp.where(last_y, 0.0, 1.0 / jnp.where(last_y, 1.0, row))
            buoys_end[pl.ds(ny + tile * x, tile), :] = half * (here + edge_b[pl.ds(1, tile), :])
    for x in range(nx):
        for t in range(ny // tile):
            rows = pl.ds(tile * t, tile)
            d = Differences(x, t, lane)
            for c, ((fx, sx), (fy, sy), _) in enumerate(terms):
                whole_x, whole_y = inner_plane(x, sx, nx), inner_tile(t, ny)
                total = part[c, x, rows, :]
                if whole_x and whole_y:
                    out[c, x, rows, :] = total
                    continue
                if not whole_x:
                    total += d.dx(fx, sx)
                if not whole_y:
                    total += d.dy(fy, sy)
                if c == 0 and x == nx - 1:
                    factor = buoys_end[rows, :]
                elif c == 1 and t == ny // tile - 1:
                    factor = buoys_end[pl.ds(ny + tile * x, tile), :]
                else:
                    factor = buoys[c, x, rows, :]
                out[c, x, rows, :] = velocity[c, x, rows, :] + factor * total

    planes_down = put_planes([(out, 0, 0), (out, 1, 0), (out, 1, 1), (out, 2, 0), (out, 2, 1)])

    def down(package):
        planes_down(package)
        if step == 0:
            row = high_y[pl.ds(5, 1), :]
            package[pl.ds(5 * ny, 1), :] = jnp.where(last_y, 0.0, 1.0 / jnp.where(last_y, 1.0, row))

    Pack(pax, pbx, even_x).put(
        put_planes([(out, 0, nx - 2), (out, 0, nx - 1), (out, 1, nx - 1), (out, 2, nx - 1)]), down)
    Pack(pay, pby, even_y).put(
        put_rows([(out, 1, ny - 2, 2), (out, 0, ny - 1, 1), (out, 2, ny - 1, 1)], nx),
        put_rows([(out, 1, 0, 1), (out, 0, 0, 2), (out, 2, 0, 2)], nx),
    )


def stress_fields(velocity, low_x, high_x, edges):
    vx = Field(velocity, 0, (low_x, 2), (high_x, 0), edges.at[1] if edges is not None else None)
    vy = Field(velocity, 1, (low_x, 3), (high_x, 1), edges.at[0] if edges is not None else None)
    vz = Field(velocity, 2, (low_x, 4), (high_x, 3), edges.at[2] if edges is not None else None)
    return vx, vy, vz


def new_normal(stress, lam, shear, x, rows, strains):
    la = time_step * lam[x, rows, :]
    two = (2.0 * time_step) * shear[x, rows, :]
    common = la * (strains[0] + strains[1] + strains[2])
    return [stress[c, x, rows, :] + (common + two * strains[c]) for c in range(3)]


def stress_inside(step, *refs):
    if step == 0:
        velocity, stress, lam, shear, bx, ax, by, ay, out, shears, halo_c, comps, edge_c = refs
    else:
        velocity, stress, lam, shear, shears, out, final_velocity, sem = refs
    nx, ny = stress.shape[1], stress.shape[2]
    lane = lanes()
    vx, vy, vz = stress_fields(velocity, None, None, None)
    if step == 1:
        copy = pltpu.make_async_copy(velocity, final_velocity, sem)
        copy.start()
    if step == 0:
        i, j, even_x, even_y = position()
        _, last_x, _, last_y = sides(i, j)
        for x in range(nx):
            comps[x] = 1.0 / shear[x]
            edge_c[x, pl.ds(0, tile), :] = comps[x, pl.ds(ny - tile, tile), :]
            row = pl.ds(ay.shape[0] // nx * x + 5, 1)
            value = jnp.where(last_y, 1.0, jnp.where(even_y, ay[row, :], by[row, :]))
            edge_c[x, pl.ds(tile, 1), :] = jnp.where(last_y, 0.0, 1.0 / value)
        for t in range(ny // tile):
            rows = pl.ds(5 * ny + tile * t, tile)
            value = jnp.where(last_x, 1.0, jnp.where(even_x, ax[rows, :], bx[rows, :]))
            halo_c[pl.ds(tile * t, tile), :] = jnp.where(last_x, 0.0, 1.0 / value)
        halo_c[pl.ds(ny, tile), :] = edge_c[nx - 1, pl.ds(1, tile), :]

        def comp(x, t, k):
            if x == nx:
                return halo_c[pl.ds(tile * t + k, tile), :]
            if k == 1 and t == ny // tile - 1:
                return edge_c[x, pl.ds(1, tile), :]
            return comps[x, pl.ds(tile * t + k, tile), :]

    for x in range(nx):
        for t in range(ny // tile):
            rows = pl.ds(tile * t, tile)
            d = Differences(x, t, lane)
            if step == 0:
                here = comp(x, t, 0)
                next_x, next_y = comp(x + 1, t, 0), comp(x, t, 1)
                pair_x, pair_y = here + next_x, here + next_y
                four = 4.0 * time_step
                if x == nx - 1 and t == ny // tile - 1:
                    shears[0, x, rows, :] = pair_x + next_y
                else:
                    shears[0, x, rows, :] = four / (pair_x + (next_y + comp(x + 1, t, 1)))
                shears[1, x, rows, :] = four / (pair_x + z_shift(pair_x, 1, lane))
                shears[2, x, rows, :] = four / (pair_y + z_shift(pair_y, 1, lane))
            whole_y = inner_tile(t, ny)
            whole_x = inner_plane(x, -1, nx)
            zero = jnp.zeros((tile, 128), jnp.float32)
            strains = [d.dx(vx, -1) if whole_x else zero, d.dy(vy, -1) if whole_y else zero, d.dz(vz, -1)]
            if whole_x and whole_y:
                strains = new_normal(stress, lam, shear, x, rows, strains)
            for c in range(3):
                out[c, x, rows, :] = strains[c]
            whole_x = inner_plane(x, 0, nx)
            total = zero
            if whole_y:
                total += d.dy(vx, 0)
            if whole_x:
                total += d.dx(vy, 0)
            if whole_x and whole_y:
                total = stress[3, x, rows, :] + shears[0, x, rows, :] * total
            out[3, x, rows, :] = total
            total = d.dz(vx, 0)
            if whole_x:
                total = stress[4, x, rows, :] + shears[1, x, rows, :] * (total + d.dx(vz, 0))
            out[4, x, rows, :] = total
            total = d.dz(vy, 0)
            if whole_y:
                total = stress[5, x, rows, :] + shears[2, x, rows, :] * (total + d.dy(vz, 0))
            out[5, x, rows, :] = total
    if step == 1:
        copy.wait()


def stress_edges(step, *refs):
    if step == 0:
        (velocity, stress, lam, shear, halo_c, shears, part, bx, ax, by, ay,
         out, shear_end, pbx, pax, pby, pay, low_x, high_x, low_y, high_y, edges, corner) = refs
    else:
        (velocity, stress, lam, shear, shears, shear_end, part, bx, ax, by, ay,
         final_stress, low_x, high_x, low_y, high_y, edges, out, sems) = refs
    nx, ny = stress.shape[1], stress.shape[2]
    even_x, even_y, _, _ = receive((bx, ax, by, ay), (low_x, high_x, low_y, high_y))
    fill_edges(velocity, 1, edges.at[0], low_y, high_y, 0, 2, 0, 1)
    fill_edges(velocity, 0, edges.at[1], low_y, high_y, 2, 1, 1, 2)
    fill_edges(velocity, 2, edges.at[2], low_y, high_y, 3, 1, 3, 2)
    vx, vy, vz = stress_fields(velocity, low_x, high_x, edges)
    lane = lanes()
    if step == 0:
        last = pl.ds(ny - tile, tile)
        corner[pl.ds(0, tile), :] = halo_c[last, :]
        corner[pl.ds(tile, 1), :] = high_x[pl.ds(5 * ny, 1), :]
        shear_end[...] = (4.0 * time_step) / (shears[0, nx - 1, last, :] + corner[pl.ds(1, tile), :])
    copies = []
    for x in sorted(range(nx), key=lambda x: not inner_plane(x, 0, nx) or not inner_plane(x, -1, nx)):
        for t in range(ny // tile):
            rows = pl.ds(tile * t, tile)
            d = Differences(x, t, lane)
            whole_y = inner_tile(t, ny)
            whole_x = inner_plane(x, -1, nx)
            strains = [part[c, x, rows, :] for c in range(3)]
            if not (whole_x and whole_y):
                if not whole_x:
                    strains[0] = d.dx(vx, -1)
                if not whole_y:
                    strains[1] = d.dy(vy, -1)
                strains = new_normal(stress, lam, shear, x, rows, strains)
            for c in range(3):
                out[c, x, rows, :] = strains[c]
            whole_x = inner_plane(x, 0, nx)
            total = part[3, x, rows, :]
            if not (whole_x and whole_y):
                if not whole_y:
                    total += d.dy(vx, 0)
                if not whole_x:
                    total += d.dx(vy, 0)
                at_end = x == nx - 1 and t == ny // tile - 1
                factor = shear_end[...] if at_end else shears[0, x, rows, :]
                total = stress[3, x, rows, :] + factor * total
            out[3, x, rows, :] = total
            total = part[4, x, rows, :]
            if not whole_x:
                total = stress[4, x, rows, :] + shears[1, x, rows, :] * (total + d.dx(vz, 0))
            out[4, x, rows, :] = total
            total = part[5, x, rows, :]
            if not whole_y:
                total = stress[5, x, rows, :] + shears[2, x, rows, :] * (total + d.dy(vz, 0))
            out[5, x, rows, :] = total
        if step == 1:
            copy = pltpu.make_async_copy(out.at[:, x], final_stress.at[:, x], sems.at[x])
            copy.start()
            copies.append(copy)
    for copy in copies:
        copy.wait()
    if step == 0:
        Pack(pax, pbx, even_x).put(
            put_planes([(out, 3, nx - 2), (out, 3, nx - 1), (out, 4, nx - 2), (out, 4, nx - 1), (out, 0, nx - 1)]),
            put_planes([(out, 3, 0), (out, 4, 0), (out, 0, 0), (out, 0, 1)]),
        )
        Pack(pay, pby, even_y).put(
            put_rows([(out, 3, ny - 2, 2), (out, 5, ny - 2, 2), (out, 1, ny - 1, 1)], nx),
            put_rows([(out, 3, 0, 1), (out, 5, 0, 1), (out, 1, 0, 2)], nx),
        )


def call(kernel, outs, scratch, args, flops, hbm_in=(), hbm_out=()):
    def spec(far_away):
        return pl.BlockSpec(memory_space=pltpu.HBM if far_away else pltpu.VMEM)

    scratch = [pltpu.VMEM(shape, jnp.float32) if isinstance(shape, tuple) else shape for shape in scratch]
    args = [pltpu.with_memory_space_constraint(a, pltpu.HBM) if n in hbm_in else a for n, a in enumerate(args)]
    return pl.pallas_call(
        kernel,
        out_shape=[(pltpu.HBM if n in hbm_out else pltpu.VMEM)(shape, jnp.float32) for n, shape in enumerate(outs)],
        in_specs=[spec(n in hbm_in) for n in range(len(args))],
        out_specs=[spec(n in hbm_out) for n in range(len(outs))],
        scratch_shapes=scratch,
        compiler_params=pltpu.CompilerParams(vmem_limit_bytes=16 * 1024 * 1024),
        cost_estimate=pl.CostEstimate(flops=flops, bytes_accessed=2 * 1024 * 1024, transcendentals=0),
    )(*args)


def per_device(velocity, stress, density, lame_lambda, lame_mu):
    _, nx, ny, nz = velocity.shape
    routes = pairings(lax.axis_size("gx"), lax.axis_size("gy"))
    cells = nx * ny * nz
    one, three = (1, nx, ny, nz), (3, nx, ny, nz)
    dma = pltpu.SemaphoreType.DMA

    def packages(x_rows, y_rows=5):
        return [(x_rows, nz)] * 2 + [(nx * y_rows, nz)] * 2

    def exchange(arrays):
        return [lax.ppermute(array, AXES, route) for array, route in zip(arrays, routes)]

    def halos(*rows):
        return packages(*rows) + [(3, 2, nx, 2 * tile, nz)]

    def kernel(function, step):
        return lambda *refs: function(step, *refs)

    first, second, later = (6 * ny, 6), 5 * ny + tile, 5 * ny
    packed = call(
        first_pack, packages(*first), [(14, nx, tile, nz), dma((4,))],
        (stress, density, lame_mu), cells, hbm_in=(0, 1, 2))
    got = exchange(packed)
    part, buoy, buoys = call(
        kernel(velocity_inside, 0), [three, one, three], [], (velocity, stress, density), 60 * cells)
    new_velocity, buoys_end, *packed = call(
        kernel(velocity_edges, 0), [three, (ny + nx * tile, nz)] + packages(second), halos(*first) + [(2 * tile, nz)],
        (velocity, stress, buoy, buoys, part, *got), 20 * cells)
    materials = got
    got = exchange(packed)
    part, shears, halo_c = call(
        kernel(stress_inside, 0), [stress.shape, three, (ny + tile, nz)], [(nx, ny, nz), (nx, 2 * tile, nz)],
        (new_velocity, stress, lame_lambda, lame_mu, *materials), 80 * cells)
    new_stress, shear_end, *packed = call(
        kernel(stress_edges, 0), [stress.shape, (tile, nz)] + packages(later), halos(second) + [(2 * tile, nz)],
        (new_velocity, stress, lame_lambda, lame_mu, halo_c, shears, part, *got), 20 * cells)
    velocity, stress = new_velocity, new_stress
    got = exchange(packed)
    (part,) = call(
        kernel(velocity_inside, 1), [three], [], (velocity, stress, buoys), 60 * cells)
    velocity, *packed = call(
        kernel(velocity_edges, 1), [three] + packages(later), halos(later),
        (velocity, stress, buoys, buoys_end, part, *got), 20 * cells)
    got = exchange(packed)
    part, final_velocity = call(
        kernel(stress_inside, 1), [stress.shape, three], [dma],
        (velocity, stress, lame_lambda, lame_mu, shears), 80 * cells, hbm_out=(1,))
    (final_stress,) = call(
        kernel(stress_edges, 1), [stress.shape], halos(later) + [stress.shape, dma((nx,))],
        (velocity, stress, lame_lambda, lame_mu, shears, shear_end, part, *got), 20 * cells, hbm_out=(0,))
    return (final_velocity, final_stress)


def solution(mesh):
    in_specs = (
        P(None, "gx", "gy", None),
        P(None, "gx", "gy", None),
        P("gx", "gy", None),
        P("gx", "gy", None),
        P("gx", "gy", None),
    )
    out_specs = (P(None, "gx", "gy", None), P(None, "gx", "gy", None))
    return jax.shard_map(
        per_device, mesh=mesh, in_specs=in_specs, out_specs=out_specs, check_vma=False
    )
```

```python
import jax
import jax.numpy as jnp
from jax import lax
from jax.experimental import pallas as pl
from jax.experimental.pallas import tpu as pltpu
from jax.sharding import PartitionSpec as P

near = 9.0 / 8.0
far = 1.0 / 24.0
time_step = 0.25
tile = 8
AXES = ("gx", "gy")


def pairings(count_x, count_y):
    other = 2 if count_x % 4 == 0 else 1

    def across(i, count):
        return ((i + 1) ^ 1) - 1

    def route(rule):
        pairs = []
        for i in range(count_x):
            for j in range(count_y):
                ti, tj = rule(i, j)
                pairs.append((i * count_y + j, ti * count_y + tj))
        return pairs

    def inner_x(i, j):
        return (i ^ 1, j)

    def outer_x(i, j):
        return (across(i, count_x), j) if 0 < i < count_x - 1 else (i, j ^ 1)

    def inner_y(i, j):
        return (i, j ^ 1)

    def outer_y(i, j):
        return (i, across(j, count_y)) if 0 < j < count_y - 1 else (i ^ other, j)

    return [route(rule) for rule in (inner_x, outer_x, outer_y, inner_y)]


def position():
    i, j = lax.axis_index("gx"), lax.axis_index("gy")
    return i, j, lax.rem(i, 2) == 0, lax.rem(j, 2) == 0


def unpack(inner, outer, low, high, even, first, last):
    for start in range(0, inner.shape[0], tile):
        rows = pl.ds(start, tile)
        a, b = inner[rows, :], outer[rows, :]
        low[rows, :] = jnp.where(first, 0.0, jnp.where(even, b, a))
        high[rows, :] = jnp.where(last, 0.0, jnp.where(even, a, b))


class Pack:
    def __init__(self, inner, outer, even):
        self.inner, self.outer, self.even = inner, outer, even

    def put(self, up, down):
        even, inner, outer = self.even, self.inner, self.outer

        @pl.when(even)
        def _():
            up(inner)
            down(outer)

        @pl.when(jnp.logical_not(even))
        def _():
            up(outer)
            down(inner)


def put_planes(items):
    def put(out):
        start = 0
        for ref, f, x in items:
            value = ref[f, x]
            out[pl.ds(start, value.shape[0]), :] = value
            start += value.shape[0]

    return put


def put_rows(items, count_x):
    def put(out):
        each = out.shape[0] // count_x
        for x in range(count_x):
            start = each * x
            for ref, f, row, count in items:
                out[pl.ds(start, count), :] = ref[f, x, pl.ds(row, count), :]
                start += count

    return put


def sides(i, j):
    return i == 0, i == lax.axis_size("gx") - 1, j == 0, j == lax.axis_size("gy") - 1


def lanes():
    return lax.broadcasted_iota(jnp.int32, (tile, 128), 1)


def z_shift(value, k, lane):
    size = value.shape[-1]
    moved = pltpu.roll(value, (-k) % size, 1)
    inside = lane < size - k if k > 0 else lane >= -k
    return jnp.where(inside, moved, 0.0)


def difference(at, base):
    return near * (at(base + 1) - at(base)) - far * (at(base + 2) - at(base - 1))


class Field:
    def __init__(self, ref, f, low_x=None, high_x=None, edge=None):
        self.ref, self.f = ref, f
        self.low_x, self.high_x, self.edge = low_x, high_x, edge

    def at(self, x, t):
        nx, ny = self.ref.shape[-3], self.ref.shape[-2]
        if x < 0:
            ref, index = self.low_x
            return ref[pl.ds(ny * (index + x) + tile * t, tile), :]
        if x >= nx:
            ref, index = self.high_x
            return ref[pl.ds(ny * (index + x - nx) + tile * t, tile), :]
        return self.ref[self.f, x, pl.ds(tile * t, tile), :]

    def y(self, x, t, k):
        ny = self.ref.shape[-2]
        start = tile * t + k
        if start < 0:
            return self.edge[0, x, pl.ds(tile + k, tile), :]
        if start + tile > ny:
            return self.edge[1, x, pl.ds(k, tile), :]
        return self.ref[self.f, x, pl.ds(start, tile), :]


class Differences:
    def __init__(self, x, t, lane):
        self.x, self.t, self.lane = x, t, lane

    def dx(self, field, base):
        return difference(lambda k: field.at(self.x + k, self.t), base)

    def dy(self, field, base):
        return difference(lambda k: field.y(self.x, self.t, k), base)

    def dz(self, field, base):
        value = field.at(self.x, self.t)
        return difference(lambda k: z_shift(value, k, self.lane) if k else value, base)


def inner_plane(x, base, nx):
    return x + base - 1 >= 0 and x + base + 2 < nx


def inner_tile(t, ny):
    return 0 < t < ny // tile - 1


def fill_edges(ref, f, edge, lows, highs, low_row, low_count, high_row, high_count):
    nx, ny = ref.shape[-3], ref.shape[-2]
    each = lows.shape[0] // nx
    for x in range(nx):
        if low_count:
            edge[0, x, pl.ds(tile - low_count, low_count), :] = lows[pl.ds(each * x + low_row, low_count), :]
            edge[0, x, pl.ds(tile, tile), :] = ref[f, x, pl.ds(0, tile), :]
        if high_count:
            edge[1, x, pl.ds(0, tile), :] = ref[f, x, pl.ds(ny - tile, tile), :]
            edge[1, x, pl.ds(tile, high_count), :] = highs[pl.ds(each * x + high_row, high_count), :]


def receive(got, halos):
    i, j, even_x, even_y = position()
    ax, bx, by, ay = got
    low_x, high_x, low_y, high_y = halos
    first_x, last_x, first_y, last_y = sides(i, j)
    unpack(ax, bx, low_x, high_x, even_x, first_x, last_x)
    unpack(ay, by, low_y, high_y, even_y, first_y, last_y)
    return even_x, even_y, last_x, last_y


def first_pack(stress, density, shear, ax, bx, by, ay, tiles, sems):
    i, j, even_x, even_y = position()
    nx, ny = density.shape[0], density.shape[1]
    copies = [
        pltpu.make_async_copy(stress.at[:, :, pl.ds(ny - tile, tile), :], tiles.at[pl.ds(0, 6)], sems.at[0]),
        pltpu.make_async_copy(stress.at[:, :, pl.ds(0, tile), :], tiles.at[pl.ds(6, 6)], sems.at[0]),
        pltpu.make_async_copy(density.at[:, pl.ds(0, tile), :], tiles.at[12], sems.at[0]),
        pltpu.make_async_copy(shear.at[:, pl.ds(0, tile), :], tiles.at[13], sems.at[0]),
    ]
    for copy in copies:
        copy.start()

    def up(out):
        return [
            pltpu.make_async_copy(stress.at[f, x], out.at[pl.ds(n * ny, ny), :], sems.at[1])
            for n, (f, x) in enumerate([(3, nx - 2), (3, nx - 1), (4, nx - 2), (4, nx - 1), (0, nx - 1)])
        ]

    def down(out):
        sources = [stress.at[3, 0], stress.at[4, 0], stress.at[0, 0], stress.at[0, 1], density.at[0], shear.at[0]]
        return [
            pltpu.make_async_copy(source, out.at[pl.ds(n * ny, ny), :], sems.at[2])
            for n, source in enumerate(sources)
        ]

    @pl.when(even_x)
    def _():
        for copy in up(ax) + down(bx):
            copy.start()

    @pl.when(jnp.logical_not(even_x))
    def _():
        for copy in up(bx) + down(ax):
            copy.start()

    for copy in copies:
        copy.wait()
    Pack(ay, by, even_y).put(
        put_rows([(tiles, 3, tile - 2, 2), (tiles, 5, tile - 2, 2), (tiles, 1, tile - 1, 1)], nx),
        put_rows([(tiles, 9, 0, 1), (tiles, 11, 0, 1), (tiles, 7, 0, 2), (tiles, 12, 0, 1), (tiles, 13, 0, 1)], nx),
    )
    for copy in up(ax) + down(bx):
        copy.wait()


def velocity_terms(stress, low_x, high_x, edges):
    xx = Field(stress, 0, (low_x, 5), (high_x, 2))
    yy = Field(stress, 1, edge=edges.at[2] if edges is not None else None)
    zz = Field(stress, 2)
    xy = Field(stress, 3, (low_x, 2), (high_x, 0), edges.at[0] if edges is not None else None)
    xz = Field(stress, 4, (low_x, 4), (high_x, 1))
    yz = Field(stress, 5, edge=edges.at[1] if edges is not None else None)
    return ((xx, 0), (xy, -1), (xz, -1)), ((xy, -1), (yy, 0), (yz, -1)), ((xz, -1), (yz, -1), (zz, 0))


def velocity_inside(step, *refs):
    if step == 0:
        velocity, stress, density, out, buoy, buoys = refs
    else:
        velocity, stress, buoys, out = refs
    nx, ny = stress.shape[1], stress.shape[2]
    lane = lanes()
    terms = velocity_terms(stress, None, None, None)
    if step == 0:
        for x in range(nx):
            buoy[0, x] = 1.0 / density[x]
        buoy_field = Field(buoy, 0)
    for x in range(nx):
        for t in range(ny // tile):
            rows = pl.ds(tile * t, tile)
            d = Differences(x, t, lane)
            if step == 0:
                here = buoy_field.at(x, t)
                half = 0.5 * time_step
                if x < nx - 1:
                    buoys[0, x, rows, :] = half * (here + buoy_field.at(x + 1, t))
                if t < ny // tile - 1:
                    buoys[1, x, rows, :] = half * (here + buoy_field.y(x, t, 1))
                buoys[2, x, rows, :] = half * (here + z_shift(here, 1, lane))
            for c, ((fx, sx), (fy, sy), (fz, sz)) in enumerate(terms):
                total = d.dz(fz, sz)
                whole_x, whole_y = inner_plane(x, sx, nx), inner_tile(t, ny)
                if whole_x:
                    total += d.dx(fx, sx)
                if whole_y:
                    total += d.dy(fy, sy)
                if whole_x and whole_y:
                    total = velocity[c, x, rows, :] + buoys[c, x, rows, :] * total
                out[c, x, rows, :] = total


def velocity_edges(step, *refs):
    if step == 0:
        (velocity, stress, buoy, buoys, part, ax, bx, by, ay, out, buoys_end, pax, pbx, pby, pay,
         low_x, high_x, low_y, high_y, edges, edge_b) = refs
    else:
        (velocity, stress, buoys, buoys_end, part, ax, bx, by, ay, out, pax, pbx, pby, pay,
         low_x, high_x, low_y, high_y, edges) = refs
    nx, ny = stress.shape[1], stress.shape[2]
    even_x, even_y, last_x, last_y = receive((ax, bx, by, ay), (low_x, high_x, low_y, high_y))
    fill_edges(stress, 3, edges.at[0], low_y, high_y, 0, 2, 0, 1)
    fill_edges(stress, 5, edges.at[1], low_y, high_y, 2, 2, 1, 1)
    fill_edges(stress, 1, edges.at[2], low_y, high_y, 4, 1, 2, 2)
    terms = velocity_terms(stress, low_x, high_x, edges)
    lane = lanes()
    if step == 0:
        half = 0.5 * time_step
        for t in range(ny // tile):
            rows = pl.ds(tile * t, tile)
            above = jnp.where(last_x, 0.0, 1.0 / jnp.where(last_x, 1.0, high_x[pl.ds(4 * ny + tile * t, tile), :]))
            buoys_end[rows, :] = half * (buoy[0, nx - 1, rows, :] + above)
        rows = pl.ds(ny - tile, tile)
        for x in range(nx):
            here = buoy[0, x, rows, :]
            row = high_y[pl.ds(high_y.shape[0] // nx * x + 4, 1), :]
            edge_b[pl.ds(0, tile), :] = here
            edge_b[pl.ds(tile, 1), :] = jnp.where(last_y, 0.0, 1.0 / jnp.where(last_y, 1.0, row))
            buoys_end[pl.ds(ny + tile * x, tile), :] = half * (here + edge_b[pl.ds(1, tile), :])
    for x in range(nx):
        for t in range(ny // tile):
            rows = pl.ds(tile * t, tile)
            d = Differences(x, t, lane)
            for c, ((fx, sx), (fy, sy), _) in enumerate(terms):
                whole_x, whole_y = inner_plane(x, sx, nx), inner_tile(t, ny)
                total = part[c, x, rows, :]
                if whole_x and whole_y:
                    out[c, x, rows, :] = total
                    continue
                if not whole_x:
                    total += d.dx(fx, sx)
                if not whole_y:
                    total += d.dy(fy, sy)
                if c == 0 and x == nx - 1:
                    factor = buoys_end[rows, :]
                elif c == 1 and t == ny // tile - 1:
                    factor = buoys_end[pl.ds(ny + tile * x, tile), :]
                else:
                    factor = buoys[c, x, rows, :]
                out[c, x, rows, :] = velocity[c, x, rows, :] + factor * total

    planes_down = put_planes([(out, 0, 0), (out, 1, 0), (out, 1, 1), (out, 2, 0), (out, 2, 1)])

    def down(package):
        planes_down(package)
        if step == 0:
            row = high_y[pl.ds(5, 1), :]
            package[pl.ds(5 * ny, 1), :] = jnp.where(last_y, 0.0, 1.0 / jnp.where(last_y, 1.0, row))

    Pack(pax, pbx, even_x).put(
        put_planes([(out, 0, nx - 2), (out, 0, nx - 1), (out, 1, nx - 1), (out, 2, nx - 1)]), down)
    Pack(pay, pby, even_y).put(
        put_rows([(out, 1, ny - 2, 2), (out, 0, ny - 1, 1), (out, 2, ny - 1, 1)], nx),
        put_rows([(out, 1, 0, 1), (out, 0, 0, 2), (out, 2, 0, 2)], nx),
    )


def stress_fields(velocity, low_x, high_x, edges):
    vx = Field(velocity, 0, (low_x, 2), (high_x, 0), edges.at[1] if edges is not None else None)
    vy = Field(velocity, 1, (low_x, 3), (high_x, 1), edges.at[0] if edges is not None else None)
    vz = Field(velocity, 2, (low_x, 4), (high_x, 3), edges.at[2] if edges is not None else None)
    return vx, vy, vz


def new_normal(stress, lam, shear, x, rows, strains):
    la = time_step * lam[x, rows, :]
    two = (2.0 * time_step) * shear[x, rows, :]
    common = la * (strains[0] + strains[1] + strains[2])
    return [stress[c, x, rows, :] + (common + two * strains[c]) for c in range(3)]


def stress_inside(step, *refs):
    if step == 0:
        velocity, stress, lam, shear, ax, bx, by, ay, out, shears, halo_c, comps, edge_c = refs
    else:
        velocity, stress, lam, shear, shears, out, final_velocity, sem = refs
    nx, ny = stress.shape[1], stress.shape[2]
    lane = lanes()
    vx, vy, vz = stress_fields(velocity, None, None, None)
    if step == 1:
        copy = pltpu.make_async_copy(velocity, final_velocity, sem)
        copy.start()
    if step == 0:
        i, j, even_x, even_y = position()
        _, last_x, _, last_y = sides(i, j)
        for x in range(nx):
            comps[x] = 1.0 / shear[x]
            edge_c[x, pl.ds(0, tile), :] = comps[x, pl.ds(ny - tile, tile), :]
            row = pl.ds(ay.shape[0] // nx * x + 5, 1)
            value = jnp.where(last_y, 1.0, jnp.where(even_y, ay[row, :], by[row, :]))
            edge_c[x, pl.ds(tile, 1), :] = jnp.where(last_y, 0.0, 1.0 / value)
        for t in range(ny // tile):
            rows = pl.ds(5 * ny + tile * t, tile)
            value = jnp.where(last_x, 1.0, jnp.where(even_x, ax[rows, :], bx[rows, :]))
            halo_c[pl.ds(tile * t, tile), :] = jnp.where(last_x, 0.0, 1.0 / value)
        halo_c[pl.ds(ny, tile), :] = edge_c[nx - 1, pl.ds(1, tile), :]

        def comp(x, t, k):
            if x == nx:
                return halo_c[pl.ds(tile * t + k, tile), :]
            if k == 1 and t == ny // tile - 1:
                return edge_c[x, pl.ds(1, tile), :]
            return comps[x, pl.ds(tile * t + k, tile), :]

    for x in range(nx):
        for t in range(ny // tile):
            rows = pl.ds(tile * t, tile)
            d = Differences(x, t, lane)
            if step == 0:
                here = comp(x, t, 0)
                next_x, next_y = comp(x + 1, t, 0), comp(x, t, 1)
                pair_x, pair_y = here + next_x, here + next_y
                four = 4.0 * time_step
                if x == nx - 1 and t == ny // tile - 1:
                    shears[0, x, rows, :] = pair_x + next_y
                else:
                    shears[0, x, rows, :] = four / (pair_x + (next_y + comp(x + 1, t, 1)))
                shears[1, x, rows, :] = four / (pair_x + z_shift(pair_x, 1, lane))
                shears[2, x, rows, :] = four / (pair_y + z_shift(pair_y, 1, lane))
            whole_y = inner_tile(t, ny)
            whole_x = inner_plane(x, -1, nx)
            zero = jnp.zeros((tile, 128), jnp.float32)
            strains = [d.dx(vx, -1) if whole_x else zero, d.dy(vy, -1) if whole_y else zero, d.dz(vz, -1)]
            if whole_x and whole_y:
                strains = new_normal(stress, lam, shear, x, rows, strains)
            for c in range(3):
                out[c, x, rows, :] = strains[c]
            whole_x = inner_plane(x, 0, nx)
            total = zero
            if whole_y:
                total += d.dy(vx, 0)
            if whole_x:
                total += d.dx(vy, 0)
            if whole_x and whole_y:
                total = stress[3, x, rows, :] + shears[0, x, rows, :] * total
            out[3, x, rows, :] = total
            total = d.dz(vx, 0)
            if whole_x:
                total = stress[4, x, rows, :] + shears[1, x, rows, :] * (total + d.dx(vz, 0))
            out[4, x, rows, :] = total
            total = d.dz(vy, 0)
            if whole_y:
                total = stress[5, x, rows, :] + shears[2, x, rows, :] * (total + d.dy(vz, 0))
            out[5, x, rows, :] = total
    if step == 1:
        copy.wait()


def stress_edges(step, *refs):
    if step == 0:
        (velocity, stress, lam, shear, halo_c, shears, part, ax, bx, by, ay,
         out, shear_end, pax, pbx, pby, pay, low_x, high_x, low_y, high_y, edges, corner) = refs
    else:
        (velocity, stress, lam, shear, shears, shear_end, part, ax, bx, by, ay,
         final_stress, low_x, high_x, low_y, high_y, edges, out, sems) = refs
    nx, ny = stress.shape[1], stress.shape[2]
    even_x, even_y, _, _ = receive((ax, bx, by, ay), (low_x, high_x, low_y, high_y))
    fill_edges(velocity, 1, edges.at[0], low_y, high_y, 0, 2, 0, 1)
    fill_edges(velocity, 0, edges.at[1], low_y, high_y, 2, 1, 1, 2)
    fill_edges(velocity, 2, edges.at[2], low_y, high_y, 3, 1, 3, 2)
    vx, vy, vz = stress_fields(velocity, low_x, high_x, edges)
    lane = lanes()
    if step == 0:
        last = pl.ds(ny - tile, tile)
        corner[pl.ds(0, tile), :] = halo_c[last, :]
        corner[pl.ds(tile, 1), :] = high_x[pl.ds(5 * ny, 1), :]
        shear_end[...] = (4.0 * time_step) / (shears[0, nx - 1, last, :] + corner[pl.ds(1, tile), :])
    copies = []
    for x in sorted(range(nx), key=lambda x: not inner_plane(x, 0, nx) or not inner_plane(x, -1, nx)):
        for t in range(ny // tile):
            rows = pl.ds(tile * t, tile)
            d = Differences(x, t, lane)
            whole_y = inner_tile(t, ny)
            whole_x = inner_plane(x, -1, nx)
            strains = [part[c, x, rows, :] for c in range(3)]
            if not (whole_x and whole_y):
                if not whole_x:
                    strains[0] = d.dx(vx, -1)
                if not whole_y:
                    strains[1] = d.dy(vy, -1)
                strains = new_normal(stress, lam, shear, x, rows, strains)
            for c in range(3):
                out[c, x, rows, :] = strains[c]
            whole_x = inner_plane(x, 0, nx)
            total = part[3, x, rows, :]
            if not (whole_x and whole_y):
                if not whole_y:
                    total += d.dy(vx, 0)
                if not whole_x:
                    total += d.dx(vy, 0)
                at_end = x == nx - 1 and t == ny // tile - 1
                factor = shear_end[...] if at_end else shears[0, x, rows, :]
                total = stress[3, x, rows, :] + factor * total
            out[3, x, rows, :] = total
            total = part[4, x, rows, :]
            if not whole_x:
                total = stress[4, x, rows, :] + shears[1, x, rows, :] * (total + d.dx(vz, 0))
            out[4, x, rows, :] = total
            total = part[5, x, rows, :]
            if not whole_y:
                total = stress[5, x, rows, :] + shears[2, x, rows, :] * (total + d.dy(vz, 0))
            out[5, x, rows, :] = total
        if step == 1:
            copy = pltpu.make_async_copy(out.at[:, x], final_stress.at[:, x], sems.at[x])
            copy.start()
            copies.append(copy)
    for copy in copies:
        copy.wait()
    if step == 0:
        Pack(pax, pbx, even_x).put(
            put_planes([(out, 3, nx - 2), (out, 3, nx - 1), (out, 4, nx - 2), (out, 4, nx - 1), (out, 0, nx - 1)]),
            put_planes([(out, 3, 0), (out, 4, 0), (out, 0, 0), (out, 0, 1)]),
        )
        Pack(pay, pby, even_y).put(
            put_rows([(out, 3, ny - 2, 2), (out, 5, ny - 2, 2), (out, 1, ny - 1, 1)], nx),
            put_rows([(out, 3, 0, 1), (out, 5, 0, 1), (out, 1, 0, 2)], nx),
        )


def call(kernel, outs, scratch, args, flops, hbm_in=(), hbm_out=()):
    def spec(far_away):
        return pl.BlockSpec(memory_space=pltpu.HBM if far_away else pltpu.VMEM)

    scratch = [pltpu.VMEM(shape, jnp.float32) if isinstance(shape, tuple) else shape for shape in scratch]
    args = [pltpu.with_memory_space_constraint(a, pltpu.HBM) if n in hbm_in else a for n, a in enumerate(args)]
    return pl.pallas_call(
        kernel,
        out_shape=[(pltpu.HBM if n in hbm_out else pltpu.VMEM)(shape, jnp.float32) for n, shape in enumerate(outs)],
        in_specs=[spec(n in hbm_in) for n in range(len(args))],
        out_specs=[spec(n in hbm_out) for n in range(len(outs))],
        scratch_shapes=scratch,
        compiler_params=pltpu.CompilerParams(vmem_limit_bytes=16 * 1024 * 1024),
        cost_estimate=pl.CostEstimate(flops=flops, bytes_accessed=2 * 1024 * 1024, transcendentals=0),
    )(*args)


def per_device(velocity, stress, density, lame_lambda, lame_mu):
    _, nx, ny, nz = velocity.shape
    routes = pairings(lax.axis_size("gx"), lax.axis_size("gy"))
    cells = nx * ny * nz
    one, three = (1, nx, ny, nz), (3, nx, ny, nz)
    dma = pltpu.SemaphoreType.DMA

    def packages(x_rows, y_rows=5):
        return [(x_rows, nz)] * 2 + [(nx * y_rows, nz)] * 2

    def exchange(arrays):
        return [lax.ppermute(array, AXES, route) for array, route in zip(arrays, routes)]

    def halos(*rows):
        return packages(*rows) + [(3, 2, nx, 2 * tile, nz)]

    def kernel(function, step):
        return lambda *refs: function(step, *refs)

    first, second, later = (6 * ny, 6), 5 * ny + tile, 5 * ny
    packed = call(
        first_pack, packages(*first), [(14, nx, tile, nz), dma((4,))],
        (stress, density, lame_mu), cells, hbm_in=(0, 1, 2))
    got = exchange(packed)
    part, buoy, buoys = call(
        kernel(velocity_inside, 0), [three, one, three], [], (velocity, stress, density), 60 * cells)
    new_velocity, buoys_end, *packed = call(
        kernel(velocity_edges, 0), [three, (ny + nx * tile, nz)] + packages(second), halos(*first) + [(2 * tile, nz)],
        (velocity, stress, buoy, buoys, part, *got), 20 * cells)
    materials = got
    got = exchange(packed)
    part, shears, halo_c = call(
        kernel(stress_inside, 0), [stress.shape, three, (ny + tile, nz)], [(nx, ny, nz), (nx, 2 * tile, nz)],
        (new_velocity, stress, lame_lambda, lame_mu, *materials), 80 * cells)
    new_stress, shear_end, *packed = call(
        kernel(stress_edges, 0), [stress.shape, (tile, nz)] + packages(later), halos(second) + [(2 * tile, nz)],
        (new_velocity, stress, lame_lambda, lame_mu, halo_c, shears, part, *got), 20 * cells)
    velocity, stress = new_velocity, new_stress
    got = exchange(packed)
    (part,) = call(
        kernel(velocity_inside, 1), [three], [], (velocity, stress, buoys), 60 * cells)
    velocity, *packed = call(
        kernel(velocity_edges, 1), [three] + packages(later), halos(later),
        (velocity, stress, buoys, buoys_end, part, *got), 20 * cells)
    got = exchange(packed)
    part, final_velocity = call(
        kernel(stress_inside, 1), [stress.shape, three], [dma],
        (velocity, stress, lame_lambda, lame_mu, shears), 80 * cells, hbm_out=(1,))
    (final_stress,) = call(
        kernel(stress_edges, 1), [stress.shape], halos(later) + [stress.shape, dma((nx,))],
        (velocity, stress, lame_lambda, lame_mu, shears, shear_end, part, *got), 20 * cells, hbm_out=(0,))
    return (final_velocity, final_stress)


def solution(mesh):
    in_specs = (
        P(None, "gx", "gy", None),
        P(None, "gx", "gy", None),
        P("gx", "gy", None),
        P("gx", "gy", None),
        P("gx", "gy", None),
    )
    out_specs = (P(None, "gx", "gy", None), P(None, "gx", "gy", None))
    return jax.shard_map(
        per_device, mesh=mesh, in_specs=in_specs, out_specs=out_specs, check_vma=False
    )
```

```python
import jax
import jax.numpy as jnp
from jax import lax
from jax.experimental import pallas as pl
from jax.experimental.pallas import tpu as pltpu
from jax.sharding import PartitionSpec as P

near = 9.0 / 8.0
far = 1.0 / 24.0
time_step = 0.25
tile = 8
AXES = ("gx", "gy")


def pairings(count_x, count_y):
    other = 2 if count_x % 4 == 0 else 1

    def across(i, count):
        return ((i + 1) ^ 1) - 1

    def route(rule):
        pairs = []
        for i in range(count_x):
            for j in range(count_y):
                ti, tj = rule(i, j)
                pairs.append((i * count_y + j, ti * count_y + tj))
        return pairs

    def inner_x(i, j):
        return (i ^ 1, j)

    def outer_x(i, j):
        return (across(i, count_x), j) if 0 < i < count_x - 1 else (i, j ^ 1)

    def inner_y(i, j):
        return (i, j ^ 1)

    def outer_y(i, j):
        return (i, across(j, count_y)) if 0 < j < count_y - 1 else (i ^ other, j)

    return [route(rule) for rule in (inner_x, outer_x, outer_y, inner_y)]


def position():
    i, j = lax.axis_index("gx"), lax.axis_index("gy")
    return i, j, lax.rem(i, 2) == 0, lax.rem(j, 2) == 0


def unpack(inner, outer, low, high, even, first, last):
    for start in range(0, inner.shape[0], tile):
        rows = pl.ds(start, tile)
        a, b = inner[rows, :], outer[rows, :]
        low[rows, :] = jnp.where(first, 0.0, jnp.where(even, b, a))
        high[rows, :] = jnp.where(last, 0.0, jnp.where(even, a, b))


class Pack:
    def __init__(self, inner, outer, even):
        self.inner, self.outer, self.even = inner, outer, even

    def put(self, up, down):
        even, inner, outer = self.even, self.inner, self.outer

        @pl.when(even)
        def _():
            up(inner)
            down(outer)

        @pl.when(jnp.logical_not(even))
        def _():
            up(outer)
            down(inner)


def put_planes(items):
    def put(out):
        start = 0
        for ref, f, x in items:
            value = ref[x] if f is None else ref[f, x]
            out[pl.ds(start, value.shape[0]), :] = value
            start += value.shape[0]

    return put


def put_rows(items, count_x):
    def put(out):
        each = out.shape[0] // count_x
        for x in range(count_x):
            start = each * x
            for ref, f, row, count in items:
                out[pl.ds(start, count), :] = ref[f, x, pl.ds(row, count), :]
                start += count

    return put


def sides(i, j):
    return i == 0, i == lax.axis_size("gx") - 1, j == 0, j == lax.axis_size("gy") - 1


def lanes():
    return lax.broadcasted_iota(jnp.int32, (tile, 128), 1)


def z_shift(value, k, lane):
    size = value.shape[-1]
    moved = pltpu.roll(value, (-k) % size, 1)
    inside = lane < size - k if k > 0 else lane >= -k
    return jnp.where(inside, moved, 0.0)


def difference(at, base):
    return near * (at(base + 1) - at(base)) - far * (at(base + 2) - at(base - 1))


class Field:
    def __init__(self, ref, f, low_x=None, high_x=None, edge=None, last=None):
        self.ref, self.f = ref, f
        self.low_x, self.high_x, self.edge, self.last = low_x, high_x, edge, last

    def at(self, x, t):
        nx, ny = self.ref.shape[-3], self.ref.shape[-2]
        if x < 0:
            ref, index = self.low_x
            return ref[pl.ds(ny * (index + x) + tile * t, tile), :]
        if x >= nx:
            ref, index = self.high_x
            return ref[pl.ds(ny * (index + x - nx) + tile * t, tile), :]
        if self.last is not None and x == nx - 1:
            return self.last[pl.ds(tile * t, tile), :]
        return self.ref[self.f, x, pl.ds(tile * t, tile), :]

    def y(self, x, t, k):
        ny = self.ref.shape[-2]
        start = tile * t + k
        if start < 0:
            return self.edge[0, x, pl.ds(tile + k, tile), :]
        if start + tile > ny:
            return self.edge[1, x, pl.ds(k, tile), :]
        return self.ref[self.f, x, pl.ds(start, tile), :]


class Differences:
    def __init__(self, x, t, lane):
        self.x, self.t, self.lane = x, t, lane

    def dx(self, field, base):
        return difference(lambda k: field.at(self.x + k, self.t), base)

    def dy(self, field, base):
        return difference(lambda k: field.y(self.x, self.t, k), base)

    def dz(self, field, base):
        value = field.at(self.x, self.t)
        return difference(lambda k: z_shift(value, k, self.lane) if k else value, base)


def inner_plane(x, base, nx):
    return x + base - 1 >= 0 and x + base + 2 < nx


def inner_velocity_plane(step, c, x, base, nx):
    return inner_plane(x, base, nx) and not (step == 1 and c == 2 and x == nx - 2)


def inner_tile(t, ny):
    return 0 < t < ny // tile - 1


def fill_edges(ref, f, edge, lows, highs, low_row, low_count, high_row, high_count):
    nx, ny = ref.shape[-3], ref.shape[-2]
    each = lows.shape[0] // nx
    for x in range(nx):
        if low_count:
            edge[0, x, pl.ds(tile - low_count, low_count), :] = lows[pl.ds(each * x + low_row, low_count), :]
            edge[0, x, pl.ds(tile, tile), :] = ref[f, x, pl.ds(0, tile), :]
        if high_count:
            edge[1, x, pl.ds(0, tile), :] = ref[f, x, pl.ds(ny - tile, tile), :]
            edge[1, x, pl.ds(tile, high_count), :] = highs[pl.ds(each * x + high_row, high_count), :]


def receive(got, halos):
    i, j, even_x, even_y = position()
    ax, bx, by, ay = got
    low_x, high_x, low_y, high_y = halos
    first_x, last_x, first_y, last_y = sides(i, j)
    unpack(ax, bx, low_x, high_x, even_x, first_x, last_x)
    unpack(ay, by, low_y, high_y, even_y, first_y, last_y)
    return even_x, even_y, last_x, last_y


def first_pack(stress, density, shear, ax, bx, by, ay, ends, tiles, sems):
    i, j, even_x, even_y = position()
    nx, ny = density.shape[0], density.shape[1]
    def up(out):
        pairs = [
            (stress.at[3, pl.ds(nx - 2, 2)], 0, 2), (stress.at[4, pl.ds(nx - 2, 2)], 2, 2),
            (stress.at[0, pl.ds(nx - 1, 1)], 4, 1),
        ]
        return [pltpu.make_async_copy(source, out.at[pl.ds(n, count)], sems.at[1]) for source, n, count in pairs]

    def down(out):
        pairs = [
            (stress.at[pl.ds(3, 2), 0], 0, 2), (stress.at[0, pl.ds(0, 2)], 2, 2),
            (density.at[pl.ds(0, 1)], 4, 1),
        ]
        return [pltpu.make_async_copy(source, out.at[pl.ds(n, count)], sems.at[2]) for source, n, count in pairs]

    copies = [
        pltpu.make_async_copy(stress.at[pl.ds(1, 5), :, pl.ds(ny - tile, tile), :], tiles.at[pl.ds(0, 5)], sems.at[0]),
        pltpu.make_async_copy(stress.at[pl.ds(1, 5), :, pl.ds(0, tile), :], tiles.at[pl.ds(5, 5)], sems.at[0]),
        pltpu.make_async_copy(density.at[:, pl.ds(0, tile), :], tiles.at[10], sems.at[0]),
        pltpu.make_async_copy(shear.at[:, pl.ds(0, tile), :], tiles.at[11], sems.at[0]),
        pltpu.make_async_copy(shear.at[0], ends.at[0], sems.at[0]),
        pltpu.make_async_copy(shear.at[nx - 1], ends.at[1], sems.at[0]),
    ]
    for copy in copies:
        copy.start()

    @pl.when(even_x)
    def _():
        for copy in up(ax) + down(bx):
            copy.start()

    @pl.when(jnp.logical_not(even_x))
    def _():
        for copy in up(bx) + down(ax):
            copy.start()

    for copy in copies:
        copy.wait()
    Pack(ay, by, even_y).put(
        put_rows([(tiles, 2, tile - 2, 2), (tiles, 4, tile - 2, 2), (tiles, 0, tile - 1, 1)], nx),
        put_rows([(tiles, 7, 0, 1), (tiles, 9, 0, 1), (tiles, 5, 0, 2), (tiles, 10, 0, 1), (tiles, 11, 0, 1)], nx),
    )
    for copy in up(ax) + down(bx):
        copy.wait()


def velocity_terms(stress, low_x, high_x, edges, last_xz=None):
    xx = Field(stress, 0, (low_x, 5), (high_x, 2))
    yy = Field(stress, 1, edge=edges.at[2] if edges is not None else None)
    zz = Field(stress, 2)
    xy = Field(stress, 3, (low_x, 2), (high_x, 0), edges.at[0] if edges is not None else None)
    xz = Field(stress, 4, (low_x, 4), (high_x, 1), last=last_xz)
    yz = Field(stress, 5, edge=edges.at[1] if edges is not None else None)
    return ((xx, 0), (xy, -1), (xz, -1)), ((xy, -1), (yy, 0), (yz, -1)), ((xz, -1), (yz, -1), (zz, 0))


def velocity_inside(step, *refs):
    if step == 0:
        stress, density, out, buoy, buoys = refs
    else:
        velocity, stress, buoys, shear, ax, bx, out, factor_low = refs
    nx, ny = stress.shape[1], stress.shape[2]
    lane = lanes()
    terms = velocity_terms(stress, None, None, None)
    if step == 1:
        i, j, even_x, _ = position()
        for t in range(ny // tile):
            rows, source = pl.ds(tile * t, tile), pl.ds(4 * ny + tile * t, tile)
            below = 1.0 / jnp.where(i == 0, 1.0, jnp.where(even_x, bx[source, :], ax[source, :]))
            pair = below + 1.0 / shear[0, rows, :]
            factor = (-4.0 * time_step * far) / (pair + z_shift(pair, 1, lane))
            factor_low[rows, :] = jnp.where(i == 0, 0.0, factor)
    if step == 0:
        for x in range(nx):
            buoy[0, x] = 1.0 / density[x]
        buoy_field = Field(buoy, 0)
    for x in range(nx):
        for t in range(ny // tile):
            rows = pl.ds(tile * t, tile)
            d = Differences(x, t, lane)
            if step == 0:
                here = buoy_field.at(x, t)
                half = 0.5 * time_step
                if x < nx - 1:
                    buoys[0, x, rows, :] = half * (here + buoy_field.at(x + 1, t))
                if t < ny // tile - 1:
                    buoys[1, x, rows, :] = half * (here + buoy_field.y(x, t, 1))
                buoys[2, x, rows, :] = half * (here + z_shift(here, 1, lane))
            for c, ((fx, sx), (fy, sy), (fz, sz)) in enumerate(terms):
                late = step == 1 and c == 0 and x == nx - 1
                total = jnp.zeros((tile, 128), jnp.float32) if late else d.dz(fz, sz)
                whole_x, whole_y = inner_velocity_plane(step, c, x, sx, nx), inner_tile(t, ny)
                if whole_x:
                    total += d.dx(fx, sx)
                if whole_y:
                    total += d.dy(fy, sy)
                if whole_x and whole_y:
                    total = buoys[c, x, rows, :] * total
                    if step == 1:
                        total += velocity[c, x, rows, :]
                out[c, x, rows, :] = total


def velocity_edges(step, *refs):
    if step == 0:
        (velocity, stress, buoy, buoys, ends, part, ax, bx, by, ay, out, buoys_end, pax, pbx, pby, pay,
         low_x, high_x, low_y, high_y, edges, edge_b) = refs
        last_xz = None
    else:
        (velocity, stress, buoys, buoys_end, shear_end, factor_low, part, ax, bx, by, ay,
         out, last_xz, pax, pbx, pby, pay, low_x, high_x, low_y, high_y, edges) = refs
    nx, ny = stress.shape[1], stress.shape[2]
    even_x, even_y, last_x, last_y = receive((ax, bx, by, ay), (low_x, high_x, low_y, high_y))
    fill_edges(stress, 3, edges.at[0], low_y, high_y, 0, 2, 0, 1)
    fill_edges(stress, 5, edges.at[1], low_y, high_y, 2, 2, 1, 1)
    fill_edges(stress, 1, edges.at[2], low_y, high_y, 4, 1, 2, 2)
    terms = velocity_terms(stress, low_x, high_x, edges, last_xz)
    lane = lanes()
    if step == 1:
        for t in range(ny // tile):
            rows, source = pl.ds(tile * t, tile), pl.ds(4 * ny + tile * t, tile)
            last_xz[rows, :] = stress[4, nx - 1, rows, :] - far * shear_end[1, rows, :] * high_x[source, :]
            below = pl.ds(3 * ny + tile * t, tile)
            low_x[below, :] = low_x[below, :] + factor_low[rows, :] * velocity[2, 1, rows, :]
    if step == 0:
        half = 0.5 * time_step
        for t in range(ny // tile):
            rows = pl.ds(tile * t, tile)
            above = jnp.where(last_x, 0.0, 1.0 / jnp.where(last_x, 1.0, high_x[pl.ds(4 * ny + tile * t, tile), :]))
            buoys_end[rows, :] = half * (buoy[0, nx - 1, rows, :] + above)
        rows = pl.ds(ny - tile, tile)
        for x in range(nx):
            here = buoy[0, x, rows, :]
            row = high_y[pl.ds(high_y.shape[0] // nx * x + 4, 1), :]
            edge_b[pl.ds(0, tile), :] = here
            edge_b[pl.ds(tile, 1), :] = jnp.where(last_y, 0.0, 1.0 / jnp.where(last_y, 1.0, row))
            buoys_end[pl.ds(ny + tile * x, tile), :] = half * (here + edge_b[pl.ds(1, tile), :])
    for x in range(nx):
        for t in range(ny // tile):
            rows = pl.ds(tile * t, tile)
            d = Differences(x, t, lane)
            for c, ((fx, sx), (fy, sy), (fz, sz)) in enumerate(terms):
                whole_x, whole_y = inner_velocity_plane(step, c, x, sx, nx), inner_tile(t, ny)
                total = part[c, x, rows, :]
                if whole_x and whole_y:
                    out[c, x, rows, :] = velocity[c, x, rows, :] + total if step == 0 else total
                    continue
                if not whole_x:
                    total += d.dx(fx, sx)
                if not whole_y:
                    total += d.dy(fy, sy)
                if step == 1 and c == 0 and x == nx - 1:
                    total += d.dz(fz, sz)
                if c == 0 and x == nx - 1:
                    factor = buoys_end[rows, :]
                elif c == 1 and t == ny // tile - 1:
                    factor = buoys_end[pl.ds(ny + tile * x, tile), :]
                else:
                    factor = buoys[c, x, rows, :]
                out[c, x, rows, :] = velocity[c, x, rows, :] + factor * total

    planes_up = [(out, 0, nx - 2), (out, 0, nx - 1), (out, 1, nx - 1), (out, 2, nx - 1)]
    planes_down = [(out, 0, 0), (out, 1, 0), (out, 1, 1), (out, 2, 0)]
    if step == 0:
        planes_up.append((ends, None, 1))
        planes_down.append((ends, None, 0))
    else:
        planes_down.append((out, 2, 1))

    def down(package):
        put_planes(planes_down)(package)
        if step == 0:
            row = high_y[pl.ds(5, 1), :]
            package[pl.ds(5 * ny, 1), :] = jnp.where(last_y, 0.0, 1.0 / jnp.where(last_y, 1.0, row))

    Pack(pax, pbx, even_x).put(put_planes(planes_up), down)
    Pack(pay, pby, even_y).put(
        put_rows([(out, 1, ny - 2, 2), (out, 0, ny - 1, 1), (out, 2, ny - 1, 1)], nx),
        put_rows([(out, 1, 0, 1), (out, 0, 0, 2), (out, 2, 0, 2)], nx),
    )


def stress_fields(velocity, low_x, high_x, edges):
    vx = Field(velocity, 0, (low_x, 2), (high_x, 0), edges.at[1] if edges is not None else None)
    vy = Field(velocity, 1, (low_x, 3), (high_x, 1), edges.at[0] if edges is not None else None)
    vz = Field(velocity, 2, (low_x, 4), (high_x, 3), edges.at[2] if edges is not None else None)
    return vx, vy, vz


def new_normal(stress, lam, shear, x, rows, strains):
    la = time_step * lam[x, rows, :]
    two = (2.0 * time_step) * shear[x, rows, :]
    common = la * (strains[0] + strains[1] + strains[2])
    return [stress[c, x, rows, :] + (common + two * strains[c]) for c in range(3)]


def stress_inside(step, *refs):
    if step == 0:
        velocity, stress, lam, shear, by, ay, out, shears, comps, edge_c = refs
    else:
        velocity, stress, lam, shear, shears, out, final_velocity, sem = refs
    nx, ny = stress.shape[1], stress.shape[2]
    lane = lanes()
    vx, vy, vz = stress_fields(velocity, None, None, None)
    if step == 1:
        copy = pltpu.make_async_copy(velocity, final_velocity, sem)
        copy.start()
    if step == 0:
        i, j, _, even_y = position()
        _, _, _, last_y = sides(i, j)
        for x in range(nx):
            comps[x] = 1.0 / shear[x]
            edge_c[x, pl.ds(0, tile), :] = comps[x, pl.ds(ny - tile, tile), :]
            row = pl.ds(ay.shape[0] // nx * x + 5, 1)
            value = jnp.where(last_y, 1.0, jnp.where(even_y, ay[row, :], by[row, :]))
            edge_c[x, pl.ds(tile, 1), :] = jnp.where(last_y, 0.0, 1.0 / value)

        def comp(x, t, k):
            if k == 1 and t == ny // tile - 1:
                return edge_c[x, pl.ds(1, tile), :]
            return comps[x, pl.ds(tile * t + k, tile), :]

    for x in range(nx):
        for t in range(ny // tile):
            rows = pl.ds(tile * t, tile)
            d = Differences(x, t, lane)
            if step == 0:
                here, next_y = comp(x, t, 0), comp(x, t, 1)
                pair_y = here + next_y
                four = 4.0 * time_step
                if x == nx - 1:
                    shears[0, x, rows, :] = pair_y
                    shears[1, x, rows, :] = here + z_shift(here, 1, lane)
                else:
                    next_x = comp(x + 1, t, 0)
                    pair_x = here + next_x
                    shears[0, x, rows, :] = four / (pair_x + (next_y + comp(x + 1, t, 1)))
                    shears[1, x, rows, :] = four / (pair_x + z_shift(pair_x, 1, lane))
                shears[2, x, rows, :] = four / (pair_y + z_shift(pair_y, 1, lane))
            whole_y = inner_tile(t, ny)
            whole_x = inner_plane(x, -1, nx)
            zero = jnp.zeros((tile, 128), jnp.float32)
            strains = [d.dx(vx, -1) if whole_x else zero, d.dy(vy, -1) if whole_y else zero, d.dz(vz, -1)]
            if whole_x and whole_y:
                strains = new_normal(stress, lam, shear, x, rows, strains)
            for c in range(3):
                out[c, x, rows, :] = strains[c]
            whole_x = inner_plane(x, 0, nx)
            total = zero
            if whole_y:
                total += d.dy(vx, 0)
            if whole_x:
                total += d.dx(vy, 0)
            if whole_x and whole_y:
                total = stress[3, x, rows, :] + shears[0, x, rows, :] * total
            out[3, x, rows, :] = total
            total = d.dz(vx, 0)
            if whole_x:
                total = stress[4, x, rows, :] + shears[1, x, rows, :] * (total + d.dx(vz, 0))
            out[4, x, rows, :] = total
            total = d.dz(vy, 0)
            if whole_y:
                total = stress[5, x, rows, :] + shears[2, x, rows, :] * (total + d.dy(vz, 0))
            out[5, x, rows, :] = total
    if step == 1:
        copy.wait()


def stress_edges(step, *refs):
    if step == 0:
        (velocity, stress, lam, shear, shears, part, ax, bx, by, ay,
         out, shear_end, pax, pbx, pby, pay, low_x, high_x, low_y, high_y, edges, above) = refs
    else:
        (velocity, stress, lam, shear, shears, shear_end, last_xz, part, ax, bx, by, ay,
         final_stress, low_x, high_x, low_y, high_y, edges, out, sems) = refs
    nx, ny = stress.shape[1], stress.shape[2]
    even_x, even_y, last_x, _ = receive((ax, bx, by, ay), (low_x, high_x, low_y, high_y))
    fill_edges(velocity, 1, edges.at[0], low_y, high_y, 0, 2, 0, 1)
    fill_edges(velocity, 0, edges.at[1], low_y, high_y, 2, 1, 1, 2)
    fill_edges(velocity, 2, edges.at[2], low_y, high_y, 3, 1, 3, 2)
    vx, vy, vz = stress_fields(velocity, low_x, high_x, edges)
    lane = lanes()
    if step == 0:
        for t in range(ny // tile):
            value = jnp.where(last_x, 1.0, high_x[pl.ds(4 * ny + tile * t, tile), :])
            above[pl.ds(tile * t, tile), :] = jnp.where(last_x, 0.0, 1.0 / value)
        above[pl.ds(ny, 1), :] = high_x[pl.ds(5 * ny, 1), :]
        for t in range(ny // tile):
            rows = pl.ds(tile * t, tile)
            value = above[rows, :]
            pair = value + above[pl.ds(tile * t + 1, tile), :]
            shear_end[0, rows, :] = (4.0 * time_step) / (shears[0, nx - 1, rows, :] + pair)
            pair = value + z_shift(value, 1, lane)
            shear_end[1, rows, :] = (4.0 * time_step) / (shears[1, nx - 1, rows, :] + pair)
    copies = []
    for x in sorted(range(nx), key=lambda x: not inner_plane(x, 0, nx) or not inner_plane(x, -1, nx)):
        for t in range(ny // tile):
            rows = pl.ds(tile * t, tile)
            d = Differences(x, t, lane)
            whole_y = inner_tile(t, ny)
            whole_x = inner_plane(x, -1, nx)
            strains = [part[c, x, rows, :] for c in range(3)]
            if not (whole_x and whole_y):
                if not whole_x:
                    strains[0] = d.dx(vx, -1)
                if not whole_y:
                    strains[1] = d.dy(vy, -1)
                strains = new_normal(stress, lam, shear, x, rows, strains)
            for c in range(3):
                out[c, x, rows, :] = strains[c]
            whole_x = inner_plane(x, 0, nx)
            total = part[3, x, rows, :]
            if not (whole_x and whole_y):
                if not whole_y:
                    total += d.dy(vx, 0)
                if not whole_x:
                    total += d.dx(vy, 0)
                factor = shear_end[0, rows, :] if x == nx - 1 else shears[0, x, rows, :]
                total = stress[3, x, rows, :] + factor * total
            out[3, x, rows, :] = total
            total = part[4, x, rows, :]
            if not whole_x:
                before = stress[4, x, rows, :]
                factor = shears[1, x, rows, :]
                change = None
                if x == nx - 1:
                    factor = shear_end[1, rows, :]
                    if step == 0:
                        change = near * (vz.at(x + 1, t) - vz.at(x, t)) + far * vz.at(x - 1, t)
                    else:
                        before = last_xz[rows, :]
                if change is None:
                    change = d.dx(vz, 0)
                total = before + factor * (total + change)
            out[4, x, rows, :] = total
            total = part[5, x, rows, :]
            if not whole_y:
                total = stress[5, x, rows, :] + shears[2, x, rows, :] * (total + d.dy(vz, 0))
            out[5, x, rows, :] = total
        if step == 1:
            copy = pltpu.make_async_copy(out.at[:, x], final_stress.at[:, x], sems.at[x])
            copy.start()
            copies.append(copy)
    for copy in copies:
        copy.wait()
    if step == 0:
        Pack(pax, pbx, even_x).put(
            put_planes([(out, 3, nx - 2), (out, 3, nx - 1), (out, 4, nx - 2), (out, 4, nx - 1), (out, 0, nx - 1)]),
            put_planes([(out, 3, 0), (out, 4, 0), (out, 0, 0), (out, 0, 1), (velocity, 2, 1)]),
        )
        Pack(pay, pby, even_y).put(
            put_rows([(out, 3, ny - 2, 2), (out, 5, ny - 2, 2), (out, 1, ny - 1, 1)], nx),
            put_rows([(out, 3, 0, 1), (out, 5, 0, 1), (out, 1, 0, 2)], nx),
        )


def call(kernel, outs, scratch, args, flops, hbm_in=(), hbm_out=()):
    def spec(far_away):
        return pl.BlockSpec(memory_space=pltpu.HBM if far_away else pltpu.VMEM)

    scratch = [pltpu.VMEM(shape, jnp.float32) if isinstance(shape, tuple) else shape for shape in scratch]
    args = [pltpu.with_memory_space_constraint(a, pltpu.HBM) if n in hbm_in else a for n, a in enumerate(args)]
    return pl.pallas_call(
        kernel,
        out_shape=[(pltpu.HBM if n in hbm_out else pltpu.VMEM)(shape, jnp.float32) for n, shape in enumerate(outs)],
        in_specs=[spec(n in hbm_in) for n in range(len(args))],
        out_specs=[spec(n in hbm_out) for n in range(len(outs))],
        scratch_shapes=scratch,
        compiler_params=pltpu.CompilerParams(vmem_limit_bytes=16 * 1024 * 1024),
        cost_estimate=pl.CostEstimate(flops=flops, bytes_accessed=2 * 1024 * 1024, transcendentals=0),
    )(*args)


def per_device(velocity, stress, density, lame_lambda, lame_mu):
    _, nx, ny, nz = velocity.shape
    routes = pairings(lax.axis_size("gx"), lax.axis_size("gy"))
    cells = nx * ny * nz
    one, three = (1, nx, ny, nz), (3, nx, ny, nz)
    dma = pltpu.SemaphoreType.DMA

    def packages(x_rows, y_rows=5):
        return [(x_rows, nz)] * 2 + [(nx * y_rows, nz)] * 2

    def exchange(arrays):
        return [lax.ppermute(array, AXES, route) for array, route in zip(arrays, routes)]

    def halos(*rows):
        return packages(*rows) + [(3, 2, nx, 2 * tile, nz)]

    def kernel(function, step):
        return lambda *refs: function(step, *refs)

    first, second, later = (5 * ny, 6), (5 * ny + tile, 5), (5 * ny, 5)
    *packed, ends = call(
        first_pack, [(5, ny, nz)] * 2 + packages(*first)[2:] + [(2, ny, nz)], [(12, nx, tile, nz), dma((3,))],
        (stress, density, lame_mu), cells, hbm_in=(0, 1, 2))
    packed, velocity, stress, density, lame_lambda, lame_mu = lax.optimization_barrier(
        ([package.reshape(-1, nz) for package in packed], velocity, stress, density, lame_lambda, lame_mu))
    got = exchange(packed)
    part, buoy, buoys = call(
        kernel(velocity_inside, 0), [three, one, three], [], (stress, density), 60 * cells)
    new_velocity, buoys_end, *packed = call(
        kernel(velocity_edges, 0), [three, (ny + nx * tile, nz)] + packages(*second), halos(*first) + [(2 * tile, nz)],
        (velocity, stress, buoy, buoys, ends, part, *got), 20 * cells)
    rows_y = got[2:]
    got = exchange(packed)
    part, shears = call(
        kernel(stress_inside, 0), [stress.shape, three], [(nx, ny, nz), (nx, 2 * tile, nz)],
        (new_velocity, stress, lame_lambda, lame_mu, *rows_y), 80 * cells)
    new_stress, shear_end, *packed = call(
        kernel(stress_edges, 0), [stress.shape, (2, ny, nz)] + packages(*later), halos(*second) + [(ny + tile, nz)],
        (new_velocity, stress, lame_lambda, lame_mu, shears, part, *got), 20 * cells)
    velocity, stress = new_velocity, new_stress
    planes_x = got[:2]
    got = exchange(packed)
    part, factor_low = call(
        kernel(velocity_inside, 1), [three, (ny, nz)], [], (velocity, stress, buoys, lame_mu, *planes_x), 60 * cells)
    velocity, last_xz, *packed = call(
        kernel(velocity_edges, 1), [three, (ny, nz)] + packages(*later), halos(*later),
        (velocity, stress, buoys, buoys_end, shear_end, factor_low, part, *got), 20 * cells)
    got = exchange(packed)
    part, final_velocity = call(
        kernel(stress_inside, 1), [stress.shape, three], [dma],
        (velocity, stress, lame_lambda, lame_mu, shears), 80 * cells, hbm_out=(1,))
    (final_stress,) = call(
        kernel(stress_edges, 1), [stress.shape], halos(*later) + [stress.shape, dma((nx,))],
        (velocity, stress, lame_lambda, lame_mu, shears, shear_end, last_xz, part, *got), 20 * cells, hbm_out=(0,))
    return (final_velocity, final_stress)


def solution(mesh):
    in_specs = (
        P(None, "gx", "gy", None),
        P(None, "gx", "gy", None),
        P("gx", "gy", None),
        P("gx", "gy", None),
        P("gx", "gy", None),
    )
    out_specs = (P(None, "gx", "gy", None), P(None, "gx", "gy", None))
    return jax.shard_map(
        per_device, mesh=mesh, in_specs=in_specs, out_specs=out_specs, check_vma=False
    )
```

```python
import jax
import jax.numpy as jnp
from jax import lax
from jax.experimental import pallas as pl
from jax.experimental.pallas import tpu as pltpu
from jax.sharding import PartitionSpec as P

near = 9.0 / 8.0
far = 1.0 / 24.0
time_step = 0.25
tile = 8
AXES = ("gx", "gy")


def pairings(count_x, count_y):
    other = 2 if count_x % 4 == 0 else 1

    def across(i, count):
        return ((i + 1) ^ 1) - 1

    def route(rule):
        pairs = []
        for i in range(count_x):
            for j in range(count_y):
                ti, tj = rule(i, j)
                pairs.append((i * count_y + j, ti * count_y + tj))
        return pairs

    def inner_x(i, j):
        return (i ^ 1, j)

    def outer_x(i, j):
        return (across(i, count_x), j) if 0 < i < count_x - 1 else (i, j ^ 1)

    def inner_y(i, j):
        return (i, j ^ 1)

    def outer_y(i, j):
        return (i, across(j, count_y)) if 0 < j < count_y - 1 else (i ^ other, j)

    return [route(rule) for rule in (inner_x, outer_x, outer_y, inner_y)]


def position():
    i, j = lax.axis_index("gx"), lax.axis_index("gy")
    return i, j, lax.rem(i, 2) == 0, lax.rem(j, 2) == 0


class Halo:
    def __init__(self, inner, outer, by_inner, outside):
        self.inner, self.outer, self.by_inner, self.outside = inner, outer, by_inner, outside
        self.rows = inner.shape[0]

    def load(self, start, count):
        rows = pl.ds(start, count)
        value = jnp.where(self.by_inner, self.inner[rows, :], self.outer[rows, :])
        return jnp.where(self.outside, 0.0, value)


class Pack:
    def __init__(self, inner, outer, even):
        self.inner, self.outer, self.even = inner, outer, even

    def put(self, up, down):
        even, inner, outer = self.even, self.inner, self.outer

        @pl.when(even)
        def _():
            up(inner)
            down(outer)

        @pl.when(jnp.logical_not(even))
        def _():
            up(outer)
            down(inner)


def put_planes(items):
    def put(out):
        start = 0
        for ref, f, x in items:
            value = ref[x] if f is None else ref[f, x]
            out[pl.ds(start, value.shape[0]), :] = value
            start += value.shape[0]

    return put


def put_rows(items, count_x):
    def put(out):
        each = out.shape[0] // count_x
        for x in range(count_x):
            start = each * x
            for ref, f, row, count in items:
                out[pl.ds(start, count), :] = ref[f, x, pl.ds(row, count), :]
                start += count

    return put


def sides(i, j):
    return i == 0, i == lax.axis_size("gx") - 1, j == 0, j == lax.axis_size("gy") - 1


def lanes():
    return lax.broadcasted_iota(jnp.int32, (tile, 128), 1)


def z_shift(value, k, lane):
    size = value.shape[-1]
    moved = pltpu.roll(value, (-k) % size, 1)
    inside = lane < size - k if k > 0 else lane >= -k
    return jnp.where(inside, moved, 0.0)


def difference(at, base):
    return near * (at(base + 1) - at(base)) - far * (at(base + 2) - at(base - 1))


class Field:
    def __init__(self, ref, f, low_x=None, high_x=None, low_y=None, high_y=None, last=None, below=None):
        self.ref, self.f = ref, f
        self.low_x, self.high_x, self.low_y, self.high_y = low_x, high_x, low_y, high_y
        self.last, self.below = last, below

    def at(self, x, t):
        nx, ny = self.ref.shape[-3], self.ref.shape[-2]
        if x < 0:
            halo, index = self.low_x
            value = halo.load(ny * (index + x) + tile * t, tile)
            return value + self.below(t) if self.below is not None and x == -1 else value
        if x >= nx:
            halo, index = self.high_x
            return halo.load(ny * (index + x - nx) + tile * t, tile)
        if self.last is not None and x == nx - 1:
            return self.last[pl.ds(tile * t, tile), :]
        return self.ref[self.f, x, pl.ds(tile * t, tile), :]

    def y(self, x, t, k):
        nx, ny = self.ref.shape[-3], self.ref.shape[-2]
        start = tile * t + k
        if 0 <= start <= ny - tile:
            return self.ref[self.f, x, pl.ds(start, tile), :]
        halo, first = self.low_y if k < 0 else self.high_y
        moved = pltpu.roll(self.ref[self.f, x, pl.ds(tile * t, tile), :], (-k) % tile, 0)
        place = lax.broadcasted_iota(jnp.int32, moved.shape, 0)
        for n in range(abs(k)):
            row = halo.load(halo.rows // nx * x + first + (n + k + 1 if k < 0 else n), 1)
            moved = jnp.where(place == (n if k < 0 else tile - k + n), row, moved)
        return moved


class Differences:
    def __init__(self, x, t, lane):
        self.x, self.t, self.lane = x, t, lane

    def dx(self, field, base):
        return difference(lambda k: field.at(self.x + k, self.t), base)

    def dy(self, field, base):
        return difference(lambda k: field.y(self.x, self.t, k), base)

    def dz(self, field, base):
        value = field.at(self.x, self.t)
        return difference(lambda k: z_shift(value, k, self.lane) if k else value, base)


def inner_plane(x, base, nx):
    return x + base - 1 >= 0 and x + base + 2 < nx


def inner_velocity_plane(step, c, x, base, nx):
    return inner_plane(x, base, nx) and not (step == 1 and c == 2 and x == nx - 2)


def inner_tile(t, ny):
    return 0 < t < ny // tile - 1


def receive(ax, bx, by, ay):
    i, j, even_x, even_y = position()
    first_x, last_x, first_y, last_y = sides(i, j)
    odd_x, odd_y = jnp.logical_not(even_x), jnp.logical_not(even_y)
    low_x, high_x = Halo(ax, bx, odd_x, first_x), Halo(ax, bx, even_x, last_x)
    low_y, high_y = Halo(ay, by, odd_y, first_y), Halo(ay, by, even_y, last_y)
    return low_x, high_x, low_y, high_y


def inverse(value, outside):
    return jnp.where(outside, 0.0, 1.0 / jnp.where(outside, 1.0, value))


def first_pack(stress, density, shear, ax, bx, by, ay, ends, tiles, sems):
    i, j, even_x, even_y = position()
    nx, ny = density.shape[0], density.shape[1]
    def up(out):
        pairs = [
            (stress.at[3, pl.ds(nx - 2, 2)], 0, 2), (stress.at[4, pl.ds(nx - 2, 2)], 2, 2),
            (stress.at[0, pl.ds(nx - 1, 1)], 4, 1),
        ]
        return [pltpu.make_async_copy(source, out.at[pl.ds(n, count)], sems.at[1]) for source, n, count in pairs]

    def down(out):
        pairs = [
            (stress.at[pl.ds(3, 2), 0], 0, 2), (stress.at[0, pl.ds(0, 2)], 2, 2),
            (density.at[pl.ds(0, 1)], 4, 1),
        ]
        return [pltpu.make_async_copy(source, out.at[pl.ds(n, count)], sems.at[2]) for source, n, count in pairs]

    copies = [
        pltpu.make_async_copy(stress.at[pl.ds(1, 5), :, pl.ds(ny - tile, tile), :], tiles.at[pl.ds(0, 5)], sems.at[0]),
        pltpu.make_async_copy(stress.at[pl.ds(1, 5), :, pl.ds(0, tile), :], tiles.at[pl.ds(5, 5)], sems.at[0]),
        pltpu.make_async_copy(density.at[:, pl.ds(0, tile), :], tiles.at[10], sems.at[0]),
        pltpu.make_async_copy(shear.at[:, pl.ds(0, tile), :], tiles.at[11], sems.at[0]),
        pltpu.make_async_copy(shear.at[0], ends.at[0], sems.at[0]),
        pltpu.make_async_copy(shear.at[nx - 1], ends.at[1], sems.at[0]),
    ]
    for copy in copies:
        copy.start()

    @pl.when(even_x)
    def _():
        for copy in up(ax) + down(bx):
            copy.start()

    @pl.when(jnp.logical_not(even_x))
    def _():
        for copy in up(bx) + down(ax):
            copy.start()

    for copy in copies:
        copy.wait()
    Pack(ay, by, even_y).put(
        put_rows([(tiles, 2, tile - 2, 2), (tiles, 4, tile - 2, 2), (tiles, 0, tile - 1, 1)], nx),
        put_rows([(tiles, 7, 0, 1), (tiles, 9, 0, 1), (tiles, 5, 0, 2), (tiles, 10, 0, 1), (tiles, 11, 0, 1)], nx),
    )
    for copy in up(ax) + down(bx):
        copy.wait()


def velocity_terms(stress, halos=(None,) * 4, last_xz=None, below_xz=None):
    low_x, high_x, low_y, high_y = halos
    xx = Field(stress, 0, (low_x, 5), (high_x, 2))
    yy = Field(stress, 1, low_y=(low_y, 4), high_y=(high_y, 2))
    zz = Field(stress, 2)
    xy = Field(stress, 3, (low_x, 2), (high_x, 0), (low_y, 1), (high_y, 0))
    xz = Field(stress, 4, (low_x, 4), (high_x, 1), last=last_xz, below=below_xz)
    yz = Field(stress, 5, low_y=(low_y, 3), high_y=(high_y, 1))
    return ((xx, 0), (xy, -1), (xz, -1)), ((xy, -1), (yy, 0), (yz, -1)), ((xz, -1), (yz, -1), (zz, 0))


def velocity_inside(step, *refs):
    if step == 0:
        stress, density, out, buoy, buoys = refs
    else:
        velocity, stress, buoys, shear, ax, bx, out, factor_low = refs
    nx, ny = stress.shape[1], stress.shape[2]
    lane = lanes()
    terms = velocity_terms(stress)
    if step == 1:
        i, j, even_x, _ = position()
        for t in range(ny // tile):
            rows, source = pl.ds(tile * t, tile), pl.ds(4 * ny + tile * t, tile)
            below = 1.0 / jnp.where(i == 0, 1.0, jnp.where(even_x, bx[source, :], ax[source, :]))
            pair = below + 1.0 / shear[0, rows, :]
            factor = (-4.0 * time_step * far) / (pair + z_shift(pair, 1, lane))
            factor_low[rows, :] = jnp.where(i == 0, 0.0, factor)
    if step == 0:
        for x in range(nx):
            buoy[0, x] = 1.0 / density[x]
        buoy_field = Field(buoy, 0)
    for x in range(nx):
        for t in range(ny // tile):
            rows = pl.ds(tile * t, tile)
            d = Differences(x, t, lane)
            if step == 0:
                here = buoy_field.at(x, t)
                half = 0.5 * time_step
                if x < nx - 1:
                    buoys[0, x, rows, :] = half * (here + buoy_field.at(x + 1, t))
                if t < ny // tile - 1:
                    buoys[1, x, rows, :] = half * (here + buoy_field.y(x, t, 1))
                buoys[2, x, rows, :] = half * (here + z_shift(here, 1, lane))
            for c, ((fx, sx), (fy, sy), (fz, sz)) in enumerate(terms):
                late = step == 1 and c == 0 and x == nx - 1
                total = jnp.zeros((tile, 128), jnp.float32) if late else d.dz(fz, sz)
                whole_x, whole_y = inner_velocity_plane(step, c, x, sx, nx), inner_tile(t, ny)
                if whole_x:
                    total += d.dx(fx, sx)
                if whole_y:
                    total += d.dy(fy, sy)
                if whole_x and whole_y:
                    total = buoys[c, x, rows, :] * total
                    if step == 1:
                        total += velocity[c, x, rows, :]
                out[c, x, rows, :] = total


def velocity_edges(step, *refs):
    if step == 0:
        (velocity, stress, buoy, buoys, ends, part, ax, bx, by, ay, out, buoys_end, pax, pbx, pby, pay) = refs
        last_xz = below_xz = None
    else:
        (velocity, stress, buoys, buoys_end, shear_end, factor_low, part, ax, bx, by, ay,
         out, last_xz, pax, pbx, pby, pay) = refs

        def below_xz(t):
            rows = pl.ds(tile * t, tile)
            return factor_low[rows, :] * velocity[2, 1, rows, :]

    nx, ny = stress.shape[1], stress.shape[2]
    i, j, even_x, even_y = position()
    _, last_x, _, last_y = sides(i, j)
    halos = receive(ax, bx, by, ay)
    _, high_x, _, high_y = halos
    terms = velocity_terms(stress, halos, last_xz, below_xz)
    lane = lanes()
    if step == 1:
        for t in range(ny // tile):
            rows = pl.ds(tile * t, tile)
            further = high_x.load(4 * ny + tile * t, tile)
            last_xz[rows, :] = stress[4, nx - 1, rows, :] - far * shear_end[1, rows, :] * further
    if step == 0:
        half = 0.5 * time_step
        for t in range(ny // tile):
            rows = pl.ds(tile * t, tile)
            above = inverse(high_x.load(4 * ny + tile * t, tile), last_x)
            buoys_end[rows, :] = half * (buoy[0, nx - 1, rows, :] + above)
        rows = pl.ds(ny - tile, tile)
        place = lax.broadcasted_iota(jnp.int32, (tile, 128), 0)
        for x in range(nx):
            here = buoy[0, x, rows, :]
            row = inverse(high_y.load(high_y.rows // nx * x + 4, 1), last_y)
            next_y = jnp.where(place == tile - 1, row, pltpu.roll(here, tile - 1, 0))
            buoys_end[pl.ds(ny + tile * x, tile), :] = half * (here + next_y)
    for x in range(nx):
        for t in range(ny // tile):
            rows = pl.ds(tile * t, tile)
            d = Differences(x, t, lane)
            for c, ((fx, sx), (fy, sy), (fz, sz)) in enumerate(terms):
                whole_x, whole_y = inner_velocity_plane(step, c, x, sx, nx), inner_tile(t, ny)
                total = part[c, x, rows, :]
                if whole_x and whole_y:
                    out[c, x, rows, :] = velocity[c, x, rows, :] + total if step == 0 else total
                    continue
                if not whole_x:
                    total += d.dx(fx, sx)
                if not whole_y:
                    total += d.dy(fy, sy)
                if step == 1 and c == 0 and x == nx - 1:
                    total += d.dz(fz, sz)
                if c == 0 and x == nx - 1:
                    factor = buoys_end[rows, :]
                elif c == 1 and t == ny // tile - 1:
                    factor = buoys_end[pl.ds(ny + tile * x, tile), :]
                else:
                    factor = buoys[c, x, rows, :]
                out[c, x, rows, :] = velocity[c, x, rows, :] + factor * total

    planes_up = [(out, 0, nx - 2), (out, 0, nx - 1), (out, 1, nx - 1), (out, 2, nx - 1)]
    planes_down = [(out, 0, 0), (out, 1, 0), (out, 1, 1), (out, 2, 0)]
    if step == 0:
        planes_up.append((ends, None, 1))
        planes_down.append((ends, None, 0))
    else:
        planes_down.append((out, 2, 1))

    def down(package):
        put_planes(planes_down)(package)
        if step == 0:
            package[pl.ds(5 * ny, 1), :] = inverse(high_y.load(5, 1), last_y)

    Pack(pax, pbx, even_x).put(put_planes(planes_up), down)
    Pack(pay, pby, even_y).put(
        put_rows([(out, 1, ny - 2, 2), (out, 0, ny - 1, 1), (out, 2, ny - 1, 1)], nx),
        put_rows([(out, 1, 0, 1), (out, 0, 0, 2), (out, 2, 0, 2)], nx),
    )


def stress_fields(velocity, halos=(None,) * 4):
    low_x, high_x, low_y, high_y = halos
    vx = Field(velocity, 0, (low_x, 2), (high_x, 0), (low_y, 2), (high_y, 1))
    vy = Field(velocity, 1, (low_x, 3), (high_x, 1), (low_y, 1), (high_y, 0))
    vz = Field(velocity, 2, (low_x, 4), (high_x, 3), (low_y, 3), (high_y, 3))
    return vx, vy, vz


def new_normal(stress, lam, shear, x, rows, strains):
    la = time_step * lam[x, rows, :]
    two = (2.0 * time_step) * shear[x, rows, :]
    common = la * (strains[0] + strains[1] + strains[2])
    return [stress[c, x, rows, :] + (common + two * strains[c]) for c in range(3)]


def stress_inside(step, *refs):
    if step == 0:
        velocity, stress, lam, shear, by, ay, out, shears, comps, edge_c = refs
    else:
        velocity, stress, lam, shear, shears, out, final_velocity, sem = refs
    nx, ny = stress.shape[1], stress.shape[2]
    lane = lanes()
    vx, vy, vz = stress_fields(velocity)
    if step == 1:
        copy = pltpu.make_async_copy(velocity, final_velocity, sem)
        copy.start()
    if step == 0:
        i, j, _, even_y = position()
        _, _, _, last_y = sides(i, j)
        for x in range(nx):
            comps[x] = 1.0 / shear[x]
            edge_c[x, pl.ds(0, tile), :] = comps[x, pl.ds(ny - tile, tile), :]
            row = pl.ds(ay.shape[0] // nx * x + 5, 1)
            value = jnp.where(last_y, 1.0, jnp.where(even_y, ay[row, :], by[row, :]))
            edge_c[x, pl.ds(tile, 1), :] = jnp.where(last_y, 0.0, 1.0 / value)

        def comp(x, t, k):
            if k == 1 and t == ny // tile - 1:
                return edge_c[x, pl.ds(1, tile), :]
            return comps[x, pl.ds(tile * t + k, tile), :]

    for x in range(nx):
        for t in range(ny // tile):
            rows = pl.ds(tile * t, tile)
            d = Differences(x, t, lane)
            if step == 0:
                here, next_y = comp(x, t, 0), comp(x, t, 1)
                pair_y = here + next_y
                four = 4.0 * time_step
                if x == nx - 1:
                    shears[0, x, rows, :] = pair_y
                    shears[1, x, rows, :] = here + z_shift(here, 1, lane)
                else:
                    next_x = comp(x + 1, t, 0)
                    pair_x = here + next_x
                    shears[0, x, rows, :] = four / (pair_x + (next_y + comp(x + 1, t, 1)))
                    shears[1, x, rows, :] = four / (pair_x + z_shift(pair_x, 1, lane))
                shears[2, x, rows, :] = four / (pair_y + z_shift(pair_y, 1, lane))
            whole_y = inner_tile(t, ny)
            whole_x = inner_plane(x, -1, nx)
            zero = jnp.zeros((tile, 128), jnp.float32)
            strains = [d.dx(vx, -1) if whole_x else zero, d.dy(vy, -1) if whole_y else zero, d.dz(vz, -1)]
            if whole_x and whole_y:
                strains = new_normal(stress, lam, shear, x, rows, strains)
            for c in range(3):
                out[c, x, rows, :] = strains[c]
            whole_x = inner_plane(x, 0, nx)
            total = zero
            if whole_y:
                total += d.dy(vx, 0)
            if whole_x:
                total += d.dx(vy, 0)
            if whole_x and whole_y:
                total = stress[3, x, rows, :] + shears[0, x, rows, :] * total
            out[3, x, rows, :] = total
            total = d.dz(vx, 0)
            if whole_x:
                total = stress[4, x, rows, :] + shears[1, x, rows, :] * (total + d.dx(vz, 0))
            out[4, x, rows, :] = total
            total = d.dz(vy, 0)
            if whole_y:
                total = stress[5, x, rows, :] + shears[2, x, rows, :] * (total + d.dy(vz, 0))
            out[5, x, rows, :] = total
    if step == 1:
        copy.wait()


def stress_edges(step, *refs):
    if step == 0:
        (velocity, stress, lam, shear, shears, part, ax, bx, by, ay,
         out, shear_end, pax, pbx, pby, pay, above) = refs
    else:
        (velocity, stress, lam, shear, shears, shear_end, last_xz, part, ax, bx, by, ay,
         final_stress, out, sems) = refs
    nx, ny = stress.shape[1], stress.shape[2]
    i, j, even_x, even_y = position()
    _, last_x, _, _ = sides(i, j)
    halos = receive(ax, bx, by, ay)
    high_x = halos[1]
    vx, vy, vz = stress_fields(velocity, halos)
    lane = lanes()
    if step == 0:
        for t in range(ny // tile):
            above[pl.ds(tile * t, tile), :] = inverse(high_x.load(4 * ny + tile * t, tile), last_x)
        above[pl.ds(ny, 1), :] = high_x.load(5 * ny, 1)
        for t in range(ny // tile):
            rows = pl.ds(tile * t, tile)
            value = above[rows, :]
            pair = value + above[pl.ds(tile * t + 1, tile), :]
            shear_end[0, rows, :] = (4.0 * time_step) / (shears[0, nx - 1, rows, :] + pair)
            pair = value + z_shift(value, 1, lane)
            shear_end[1, rows, :] = (4.0 * time_step) / (shears[1, nx - 1, rows, :] + pair)
    copies = []
    for x in sorted(range(nx), key=lambda x: not inner_plane(x, 0, nx) or not inner_plane(x, -1, nx)):
        for t in range(ny // tile):
            rows = pl.ds(tile * t, tile)
            d = Differences(x, t, lane)
            whole_y = inner_tile(t, ny)
            whole_x = inner_plane(x, -1, nx)
            strains = [part[c, x, rows, :] for c in range(3)]
            if not (whole_x and whole_y):
                if not whole_x:
                    strains[0] = d.dx(vx, -1)
                if not whole_y:
                    strains[1] = d.dy(vy, -1)
                strains = new_normal(stress, lam, shear, x, rows, strains)
            for c in range(3):
                out[c, x, rows, :] = strains[c]
            whole_x = inner_plane(x, 0, nx)
            total = part[3, x, rows, :]
            if not (whole_x and whole_y):
                if not whole_y:
                    total += d.dy(vx, 0)
                if not whole_x:
                    total += d.dx(vy, 0)
                factor = shear_end[0, rows, :] if x == nx - 1 else shears[0, x, rows, :]
                total = stress[3, x, rows, :] + factor * total
            out[3, x, rows, :] = total
            total = part[4, x, rows, :]
            if not whole_x:
                before = stress[4, x, rows, :]
                factor = shears[1, x, rows, :]
                change = None
                if x == nx - 1:
                    factor = shear_end[1, rows, :]
                    if step == 0:
                        change = near * (vz.at(x + 1, t) - vz.at(x, t)) + far * vz.at(x - 1, t)
                    else:
                        before = last_xz[rows, :]
                if change is None:
                    change = d.dx(vz, 0)
                total = before + factor * (total + change)
            out[4, x, rows, :] = total
            total = part[5, x, rows, :]
            if not whole_y:
                total = stress[5, x, rows, :] + shears[2, x, rows, :] * (total + d.dy(vz, 0))
            out[5, x, rows, :] = total
        if step == 1:
            copy = pltpu.make_async_copy(out.at[:, x], final_stress.at[:, x], sems.at[x])
            copy.start()
            copies.append(copy)
    for copy in copies:
        copy.wait()
    if step == 0:
        Pack(pax, pbx, even_x).put(
            put_planes([(out, 3, nx - 2), (out, 3, nx - 1), (out, 4, nx - 2), (out, 4, nx - 1), (out, 0, nx - 1)]),
            put_planes([(out, 3, 0), (out, 4, 0), (out, 0, 0), (out, 0, 1), (velocity, 2, 1)]),
        )
        Pack(pay, pby, even_y).put(
            put_rows([(out, 3, ny - 2, 2), (out, 5, ny - 2, 2), (out, 1, ny - 1, 1)], nx),
            put_rows([(out, 3, 0, 1), (out, 5, 0, 1), (out, 1, 0, 2)], nx),
        )


def call(kernel, outs, scratch, args, flops, hbm_in=(), hbm_out=()):
    def spec(far_away):
        return pl.BlockSpec(memory_space=pltpu.HBM if far_away else pltpu.VMEM)

    scratch = [pltpu.VMEM(shape, jnp.float32) if isinstance(shape, tuple) else shape for shape in scratch]
    args = [pltpu.with_memory_space_constraint(a, pltpu.HBM) if n in hbm_in else a for n, a in enumerate(args)]
    return pl.pallas_call(
        kernel,
        out_shape=[(pltpu.HBM if n in hbm_out else pltpu.VMEM)(shape, jnp.float32) for n, shape in enumerate(outs)],
        in_specs=[spec(n in hbm_in) for n in range(len(args))],
        out_specs=[spec(n in hbm_out) for n in range(len(outs))],
        scratch_shapes=scratch,
        compiler_params=pltpu.CompilerParams(vmem_limit_bytes=16 * 1024 * 1024),
        cost_estimate=pl.CostEstimate(flops=flops, bytes_accessed=2 * 1024 * 1024, transcendentals=0),
    )(*args)


def per_device(velocity, stress, density, lame_lambda, lame_mu):
    _, nx, ny, nz = velocity.shape
    routes = pairings(lax.axis_size("gx"), lax.axis_size("gy"))
    cells = nx * ny * nz
    one, three = (1, nx, ny, nz), (3, nx, ny, nz)
    dma = pltpu.SemaphoreType.DMA

    def packages(x_rows, y_rows=5):
        return [(x_rows, nz)] * 2 + [(nx * y_rows, nz)] * 2

    def exchange(arrays):
        return [lax.ppermute(array, AXES, route) for array, route in zip(arrays, routes)]

    def kernel(function, step):
        return lambda *refs: function(step, *refs)

    first, second, later = (5 * ny, 6), (5 * ny + tile, 5), (5 * ny, 5)
    *packed, ends = call(
        first_pack, [(5, ny, nz)] * 2 + packages(*first)[2:] + [(2, ny, nz)], [(12, nx, tile, nz), dma((3,))],
        (stress, density, lame_mu), cells, hbm_in=(0, 1, 2))
    packed, velocity, stress, density, lame_lambda, lame_mu = lax.optimization_barrier(
        ([package.reshape(-1, nz) for package in packed], velocity, stress, density, lame_lambda, lame_mu))
    got = exchange(packed)
    part, buoy, buoys = call(
        kernel(velocity_inside, 0), [three, one, three], [], (stress, density), 60 * cells)
    new_velocity, buoys_end, *packed = call(
        kernel(velocity_edges, 0), [three, (ny + nx * tile, nz)] + packages(*second), [],
        (velocity, stress, buoy, buoys, ends, part, *got), 20 * cells)
    rows_y = got[2:]
    got = exchange(packed)
    part, shears = call(
        kernel(stress_inside, 0), [stress.shape, three], [(nx, ny, nz), (nx, 2 * tile, nz)],
        (new_velocity, stress, lame_lambda, lame_mu, *rows_y), 80 * cells)
    new_stress, shear_end, *packed = call(
        kernel(stress_edges, 0), [stress.shape, (2, ny, nz)] + packages(*later), [(ny + tile, nz)],
        (new_velocity, stress, lame_lambda, lame_mu, shears, part, *got), 20 * cells)
    velocity, stress = new_velocity, new_stress
    planes_x = got[:2]
    got = exchange(packed)
    part, factor_low = call(
        kernel(velocity_inside, 1), [three, (ny, nz)], [], (velocity, stress, buoys, lame_mu, *planes_x), 60 * cells)
    velocity, last_xz, *packed = call(
        kernel(velocity_edges, 1), [three, (ny, nz)] + packages(*later), [],
        (velocity, stress, buoys, buoys_end, shear_end, factor_low, part, *got), 20 * cells)
    got = exchange(packed)
    part, final_velocity = call(
        kernel(stress_inside, 1), [stress.shape, three], [dma],
        (velocity, stress, lame_lambda, lame_mu, shears), 80 * cells, hbm_out=(1,))
    (final_stress,) = call(
        kernel(stress_edges, 1), [stress.shape], [stress.shape, dma((nx,))],
        (velocity, stress, lame_lambda, lame_mu, shears, shear_end, last_xz, part, *got), 20 * cells, hbm_out=(0,))
    return (final_velocity, final_stress)


def solution(mesh):
    in_specs = (
        P(None, "gx", "gy", None),
        P(None, "gx", "gy", None),
        P("gx", "gy", None),
        P("gx", "gy", None),
        P("gx", "gy", None),
    )
    out_specs = (P(None, "gx", "gy", None), P(None, "gx", "gy", None))
    return jax.shard_map(
        per_device, mesh=mesh, in_specs=in_specs, out_specs=out_specs, check_vma=False
    )
```

```python
import jax
import jax.numpy as jnp
from jax import lax
from jax.experimental import pallas as pl
from jax.experimental.pallas import tpu as pltpu
from jax.sharding import PartitionSpec as P

near = 9.0 / 8.0
far = 1.0 / 24.0
time_step = 0.25
tile = 8
AXES = ("gx", "gy")


def pairings(count_x, count_y):
    other = 2 if count_x % 4 == 0 else 1

    def across(i, count):
        return ((i + 1) ^ 1) - 1

    def route(rule):
        pairs = []
        for i in range(count_x):
            for j in range(count_y):
                ti, tj = rule(i, j)
                pairs.append((i * count_y + j, ti * count_y + tj))
        return pairs

    def inner_x(i, j):
        return (i ^ 1, j)

    def outer_x(i, j):
        return (across(i, count_x), j) if 0 < i < count_x - 1 else (i, j ^ 1)

    def inner_y(i, j):
        return (i, j ^ 1)

    def outer_y(i, j):
        return (i, across(j, count_y)) if 0 < j < count_y - 1 else (i ^ other, j)

    return [route(rule) for rule in (inner_x, outer_x, outer_y, inner_y)]


def position():
    i, j = lax.axis_index("gx"), lax.axis_index("gy")
    return i, j, lax.rem(i, 2) == 0, lax.rem(j, 2) == 0


class Halo:
    def __init__(self, inner, outer, by_inner, outside):
        self.inner, self.outer, self.by_inner, self.outside = inner, outer, by_inner, outside
        self.rows = inner.shape[0]

    def load(self, start, count):
        rows = pl.ds(start, count)
        value = jnp.where(self.by_inner, self.inner[rows, :], self.outer[rows, :])
        return jnp.where(self.outside, 0.0, value)


class Pack:
    def __init__(self, inner, outer, even):
        self.inner, self.outer, self.even = inner, outer, even

    def put(self, up, down):
        even, inner, outer = self.even, self.inner, self.outer

        @pl.when(even)
        def _():
            up(inner)
            down(outer)

        @pl.when(jnp.logical_not(even))
        def _():
            up(outer)
            down(inner)


def put_planes(items):
    def put(out):
        start = 0
        for ref, f, x in items:
            value = ref[x] if f is None else ref[f, x]
            out[pl.ds(start, value.shape[0]), :] = value
            start += value.shape[0]

    return put


def put_rows(items, count_x):
    def put(out):
        each = out.shape[0] // count_x
        for x in range(count_x):
            start = each * x
            for ref, f, row, count in items:
                out[pl.ds(start, count), :] = ref[f, x, pl.ds(row, count), :]
                start += count

    return put


def sides(i, j):
    return i == 0, i == lax.axis_size("gx") - 1, j == 0, j == lax.axis_size("gy") - 1


def lanes():
    return lax.broadcasted_iota(jnp.int32, (tile, 128), 1)


def z_shift(value, k, lane):
    size = value.shape[-1]
    moved = pltpu.roll(value, (-k) % size, 1)
    inside = lane < size - k if k > 0 else lane >= -k
    return jnp.where(inside, moved, 0.0)


def difference(at, base):
    return near * (at(base + 1) - at(base)) - far * (at(base + 2) - at(base - 1))


class Field:
    def __init__(self, ref, f, low_x=None, high_x=None, low_y=None, high_y=None, last=None, below=None):
        self.ref, self.f = ref, f
        self.low_x, self.high_x, self.low_y, self.high_y = low_x, high_x, low_y, high_y
        self.last, self.below = last, below

    def at(self, x, t):
        nx, ny = self.ref.shape[-3], self.ref.shape[-2]
        if x < 0:
            halo, index = self.low_x
            value = halo.load(ny * (index + x) + tile * t, tile)
            return value + self.below(t) if self.below is not None and x == -1 else value
        if x >= nx:
            halo, index = self.high_x
            return halo.load(ny * (index + x - nx) + tile * t, tile)
        if self.last is not None and x == nx - 1:
            return self.last[pl.ds(tile * t, tile), :]
        return self.ref[self.f, x, pl.ds(tile * t, tile), :]

    def y(self, x, t, k):
        nx, ny = self.ref.shape[-3], self.ref.shape[-2]
        start = tile * t + k
        if 0 <= start <= ny - tile:
            return self.ref[self.f, x, pl.ds(start, tile), :]
        halo, first = self.low_y if k < 0 else self.high_y
        moved = pltpu.roll(self.ref[self.f, x, pl.ds(tile * t, tile), :], (-k) % tile, 0)
        place = lax.broadcasted_iota(jnp.int32, moved.shape, 0)
        for n in range(abs(k)):
            row = halo.load(halo.rows // nx * x + first + (n + k + 1 if k < 0 else n), 1)
            moved = jnp.where(place == (n if k < 0 else tile - k + n), row, moved)
        return moved


class Differences:
    def __init__(self, x, t, lane):
        self.x, self.t, self.lane = x, t, lane

    def dx(self, field, base):
        return difference(lambda k: field.at(self.x + k, self.t), base)

    def dy(self, field, base):
        return difference(lambda k: field.y(self.x, self.t, k), base)

    def dz(self, field, base):
        value = field.at(self.x, self.t)
        return difference(lambda k: z_shift(value, k, self.lane) if k else value, base)


def inner_plane(x, base, nx):
    return x + base - 1 >= 0 and x + base + 2 < nx


def inner_velocity_plane(step, c, x, base, nx):
    return inner_plane(x, base, nx) and not (step == 1 and c == 2 and x == nx - 2)


def inner_tile(t, ny):
    return 0 < t < ny // tile - 1


def receive(ax, bx, by, ay):
    i, j, even_x, even_y = position()
    first_x, last_x, first_y, last_y = sides(i, j)
    odd_x, odd_y = jnp.logical_not(even_x), jnp.logical_not(even_y)
    low_x, high_x = Halo(ax, bx, odd_x, first_x), Halo(ax, bx, even_x, last_x)
    low_y, high_y = Halo(ay, by, odd_y, first_y), Halo(ay, by, even_y, last_y)
    return low_x, high_x, low_y, high_y


def inverse(value, outside):
    return jnp.where(outside, 0.0, 1.0 / jnp.where(outside, 1.0, value))


def first_pack(stress, density, shear, ax, bx, by, ay, ends, tiles, sems):
    i, j, even_x, even_y = position()
    nx, ny = density.shape[0], density.shape[1]
    def up(out):
        pairs = [
            (stress.at[3, pl.ds(nx - 2, 2)], 0, 2), (stress.at[4, pl.ds(nx - 2, 2)], 2, 2),
            (stress.at[0, pl.ds(nx - 1, 1)], 4, 1),
        ]
        return [pltpu.make_async_copy(source, out.at[pl.ds(n, count)], sems.at[1]) for source, n, count in pairs]

    def down(out):
        pairs = [
            (stress.at[pl.ds(3, 2), 0], 0, 2), (stress.at[0, pl.ds(0, 2)], 2, 2),
            (density.at[pl.ds(0, 1)], 4, 1),
        ]
        return [pltpu.make_async_copy(source, out.at[pl.ds(n, count)], sems.at[2]) for source, n, count in pairs]

    copies = [
        pltpu.make_async_copy(stress.at[pl.ds(1, 5), :, pl.ds(ny - tile, tile), :], tiles.at[pl.ds(0, 5)], sems.at[0]),
        pltpu.make_async_copy(stress.at[pl.ds(1, 5), :, pl.ds(0, tile), :], tiles.at[pl.ds(5, 5)], sems.at[0]),
        pltpu.make_async_copy(density.at[:, pl.ds(0, tile), :], tiles.at[10], sems.at[0]),
        pltpu.make_async_copy(shear.at[:, pl.ds(0, tile), :], tiles.at[11], sems.at[0]),
        pltpu.make_async_copy(shear.at[0], ends.at[0], sems.at[0]),
        pltpu.make_async_copy(shear.at[nx - 1], ends.at[1], sems.at[0]),
    ]
    for copy in copies:
        copy.start()

    @pl.when(even_x)
    def _():
        for copy in up(ax) + down(bx):
            copy.start()

    @pl.when(jnp.logical_not(even_x))
    def _():
        for copy in up(bx) + down(ax):
            copy.start()

    for copy in copies:
        copy.wait()
    Pack(ay, by, even_y).put(
        put_rows([(tiles, 2, tile - 2, 2), (tiles, 4, tile - 2, 2), (tiles, 0, tile - 1, 1)], nx),
        put_rows([(tiles, 7, 0, 1), (tiles, 9, 0, 1), (tiles, 5, 0, 2), (tiles, 10, 0, 1), (tiles, 11, 0, 1)], nx),
    )
    for copy in up(ax) + down(bx):
        copy.wait()


def velocity_terms(stress, halos=(None,) * 4, last_xz=None, below_xz=None):
    low_x, high_x, low_y, high_y = halos
    xx = Field(stress, 0, (low_x, 5), (high_x, 2))
    yy = Field(stress, 1, low_y=(low_y, 4), high_y=(high_y, 2))
    zz = Field(stress, 2)
    xy = Field(stress, 3, (low_x, 2), (high_x, 0), (low_y, 1), (high_y, 0))
    xz = Field(stress, 4, (low_x, 4), (high_x, 1), last=last_xz, below=below_xz)
    yz = Field(stress, 5, low_y=(low_y, 3), high_y=(high_y, 1))
    return ((xx, 0), (xy, -1), (xz, -1)), ((xy, -1), (yy, 0), (yz, -1)), ((xz, -1), (yz, -1), (zz, 0))


def velocity_inside(step, *refs):
    if step == 0:
        stress, density, out, buoy, buoys = refs
    else:
        velocity, stress, buoys, shear, ax, bx, out, factor_low = refs
    nx, ny = stress.shape[1], stress.shape[2]
    lane = lanes()
    terms = velocity_terms(stress)
    if step == 1:
        i, j, even_x, _ = position()
        for t in range(ny // tile):
            rows, source = pl.ds(tile * t, tile), pl.ds(4 * ny + tile * t, tile)
            below = 1.0 / jnp.where(i == 0, 1.0, jnp.where(even_x, bx[source, :], ax[source, :]))
            pair = below + 1.0 / shear[0, rows, :]
            factor = (-4.0 * time_step * far) / (pair + z_shift(pair, 1, lane))
            factor_low[rows, :] = jnp.where(i == 0, 0.0, factor)
    if step == 0:
        for x in range(nx):
            buoy[0, x] = 1.0 / density[x]
        buoy_field = Field(buoy, 0)
    for x in range(nx):
        for t in range(ny // tile):
            rows = pl.ds(tile * t, tile)
            d = Differences(x, t, lane)
            if step == 0:
                here = buoy_field.at(x, t)
                half = 0.5 * time_step
                if x < nx - 1:
                    buoys[0, x, rows, :] = half * (here + buoy_field.at(x + 1, t))
                if t < ny // tile - 1:
                    buoys[1, x, rows, :] = half * (here + buoy_field.y(x, t, 1))
                buoys[2, x, rows, :] = half * (here + z_shift(here, 1, lane))
            for c, ((fx, sx), (fy, sy), (fz, sz)) in enumerate(terms):
                late = step == 1 and c == 0 and x == nx - 1
                total = jnp.zeros((tile, 128), jnp.float32) if late else d.dz(fz, sz)
                whole_x, whole_y = inner_velocity_plane(step, c, x, sx, nx), inner_tile(t, ny)
                if whole_x:
                    total += d.dx(fx, sx)
                if whole_y:
                    total += d.dy(fy, sy)
                if whole_x and whole_y:
                    total = buoys[c, x, rows, :] * total
                    if step == 1:
                        total += velocity[c, x, rows, :]
                out[c, x, rows, :] = total


def velocity_edges(step, *refs):
    if step == 0:
        (velocity, stress, buoy, buoys, ends, part, ax, bx, by, ay, out, buoys_end, pby, pay, pax, pbx) = refs
        last_xz = below_xz = None
    else:
        (velocity, stress, buoys, buoys_end, shear_end, factor_low, part, ax, bx, by, ay,
         out, last_xz, pax, pbx, pby, pay) = refs

        def below_xz(t):
            rows = pl.ds(tile * t, tile)
            return factor_low[rows, :] * velocity[2, 1, rows, :]

    nx, ny = stress.shape[1], stress.shape[2]
    i, j, even_x, even_y = position()
    _, last_x, _, last_y = sides(i, j)
    halos = receive(ax, bx, by, ay)
    _, high_x, _, high_y = halos
    terms = velocity_terms(stress, halos, last_xz, below_xz)
    lane = lanes()
    if step == 1:
        for t in range(ny // tile):
            rows = pl.ds(tile * t, tile)
            further = high_x.load(4 * ny + tile * t, tile)
            last_xz[rows, :] = stress[4, nx - 1, rows, :] - far * shear_end[1, rows, :] * further
    if step == 0:
        half = 0.5 * time_step
        for t in range(ny // tile):
            rows = pl.ds(tile * t, tile)
            above = inverse(high_x.load(4 * ny + tile * t, tile), last_x)
            buoys_end[rows, :] = half * (buoy[0, nx - 1, rows, :] + above)
        rows = pl.ds(ny - tile, tile)
        place = lax.broadcasted_iota(jnp.int32, (tile, 128), 0)
        for x in range(nx):
            here = buoy[0, x, rows, :]
            row = inverse(high_y.load(high_y.rows // nx * x + 4, 1), last_y)
            next_y = jnp.where(place == tile - 1, row, pltpu.roll(here, tile - 1, 0))
            buoys_end[pl.ds(ny + tile * x, tile), :] = half * (here + next_y)
    for x in range(nx):
        for t in range(ny // tile):
            rows = pl.ds(tile * t, tile)
            d = Differences(x, t, lane)
            for c, ((fx, sx), (fy, sy), (fz, sz)) in enumerate(terms):
                whole_x, whole_y = inner_velocity_plane(step, c, x, sx, nx), inner_tile(t, ny)
                total = part[c, x, rows, :]
                if whole_x and whole_y:
                    out[c, x, rows, :] = velocity[c, x, rows, :] + total if step == 0 else total
                    continue
                if not whole_x:
                    total += d.dx(fx, sx)
                if not whole_y:
                    total += d.dy(fy, sy)
                if step == 1 and c == 0 and x == nx - 1:
                    total += d.dz(fz, sz)
                if c == 0 and x == nx - 1:
                    factor = buoys_end[rows, :]
                elif c == 1 and t == ny // tile - 1:
                    factor = buoys_end[pl.ds(ny + tile * x, tile), :]
                else:
                    factor = buoys[c, x, rows, :]
                out[c, x, rows, :] = velocity[c, x, rows, :] + factor * total

    planes_up = [(out, 0, nx - 2), (out, 0, nx - 1), (out, 1, nx - 1), (out, 2, nx - 1)]
    planes_down = [(out, 0, 0), (out, 1, 0), (out, 1, 1), (out, 2, 0)]
    if step == 0:
        planes_up.append((ends, None, 1))
        planes_down.append((ends, None, 0))
    else:
        planes_down.append((out, 2, 1))

    def down(package):
        put_planes(planes_down)(package)
        if step == 0:
            package[pl.ds(5 * ny, 1), :] = inverse(high_y.load(5, 1), last_y)

    Pack(pax, pbx, even_x).put(put_planes(planes_up), down)
    Pack(pay, pby, even_y).put(
        put_rows([(out, 1, ny - 2, 2), (out, 0, ny - 1, 1), (out, 2, ny - 1, 1)], nx),
        put_rows([(out, 1, 0, 1), (out, 0, 0, 2), (out, 2, 0, 2)], nx),
    )


def stress_fields(velocity, halos=(None,) * 4):
    low_x, high_x, low_y, high_y = halos
    vx = Field(velocity, 0, (low_x, 2), (high_x, 0), (low_y, 2), (high_y, 1))
    vy = Field(velocity, 1, (low_x, 3), (high_x, 1), (low_y, 1), (high_y, 0))
    vz = Field(velocity, 2, (low_x, 4), (high_x, 3), (low_y, 3), (high_y, 3))
    return vx, vy, vz


def new_normal(stress, lam, shear, x, rows, strains):
    la = time_step * lam[x, rows, :]
    two = (2.0 * time_step) * shear[x, rows, :]
    common = la * (strains[0] + strains[1] + strains[2])
    return [stress[c, x, rows, :] + (common + two * strains[c]) for c in range(3)]


def stress_inside(step, *refs):
    if step == 0:
        velocity, stress, lam, shear, by, ay, out, shears, comps, edge_c = refs
    else:
        velocity, stress, lam, shear, shears, out, final_velocity, sem = refs
    nx, ny = stress.shape[1], stress.shape[2]
    lane = lanes()
    vx, vy, vz = stress_fields(velocity)
    if step == 1:
        copy = pltpu.make_async_copy(velocity, final_velocity, sem)
        copy.start()
    if step == 0:
        i, j, _, even_y = position()
        _, _, _, last_y = sides(i, j)
        for x in range(nx):
            comps[x] = 1.0 / shear[x]
            edge_c[x, pl.ds(0, tile), :] = comps[x, pl.ds(ny - tile, tile), :]
            row = pl.ds(ay.shape[0] // nx * x + 5, 1)
            value = jnp.where(last_y, 1.0, jnp.where(even_y, ay[row, :], by[row, :]))
            edge_c[x, pl.ds(tile, 1), :] = jnp.where(last_y, 0.0, 1.0 / value)

        def comp(x, t, k):
            if k == 1 and t == ny // tile - 1:
                return edge_c[x, pl.ds(1, tile), :]
            return comps[x, pl.ds(tile * t + k, tile), :]

    for x in range(nx):
        for t in range(ny // tile):
            rows = pl.ds(tile * t, tile)
            d = Differences(x, t, lane)
            if step == 0:
                here, next_y = comp(x, t, 0), comp(x, t, 1)
                pair_y = here + next_y
                four = 4.0 * time_step
                if x == nx - 1:
                    shears[0, x, rows, :] = pair_y
                    shears[1, x, rows, :] = here + z_shift(here, 1, lane)
                else:
                    next_x = comp(x + 1, t, 0)
                    pair_x = here + next_x
                    shears[0, x, rows, :] = four / (pair_x + (next_y + comp(x + 1, t, 1)))
                    shears[1, x, rows, :] = four / (pair_x + z_shift(pair_x, 1, lane))
                shears[2, x, rows, :] = four / (pair_y + z_shift(pair_y, 1, lane))
            whole_y = inner_tile(t, ny)
            whole_x = inner_plane(x, -1, nx)
            zero = jnp.zeros((tile, 128), jnp.float32)
            strains = [d.dx(vx, -1) if whole_x else zero, d.dy(vy, -1) if whole_y else zero, d.dz(vz, -1)]
            if whole_x and whole_y:
                strains = new_normal(stress, lam, shear, x, rows, strains)
            for c in range(3):
                out[c, x, rows, :] = strains[c]
            whole_x = inner_plane(x, 0, nx)
            total = zero
            if whole_y:
                total += d.dy(vx, 0)
            if whole_x:
                total += d.dx(vy, 0)
            if whole_x and whole_y:
                total = stress[3, x, rows, :] + shears[0, x, rows, :] * total
            out[3, x, rows, :] = total
            total = d.dz(vx, 0)
            if whole_x:
                total = stress[4, x, rows, :] + shears[1, x, rows, :] * (total + d.dx(vz, 0))
            out[4, x, rows, :] = total
            total = d.dz(vy, 0)
            if whole_y:
                total = stress[5, x, rows, :] + shears[2, x, rows, :] * (total + d.dy(vz, 0))
            out[5, x, rows, :] = total
    if step == 1:
        copy.wait()


def stress_edges(step, *refs):
    if step == 0:
        (velocity, stress, lam, shear, shears, part, ax, bx, by, ay,
         out, shear_end, pax, pbx, pby, pay, above) = refs
    else:
        (velocity, stress, lam, shear, shears, shear_end, last_xz, part, ax, bx, by, ay,
         final_stress, out, sems) = refs
    nx, ny = stress.shape[1], stress.shape[2]
    i, j, even_x, even_y = position()
    _, last_x, _, _ = sides(i, j)
    halos = receive(ax, bx, by, ay)
    high_x = halos[1]
    vx, vy, vz = stress_fields(velocity, halos)
    lane = lanes()
    if step == 0:
        for t in range(ny // tile):
            above[pl.ds(tile * t, tile), :] = inverse(high_x.load(4 * ny + tile * t, tile), last_x)
        above[pl.ds(ny, 1), :] = high_x.load(5 * ny, 1)
        for t in range(ny // tile):
            rows = pl.ds(tile * t, tile)
            value = above[rows, :]
            pair = value + above[pl.ds(tile * t + 1, tile), :]
            shear_end[0, rows, :] = (4.0 * time_step) / (shears[0, nx - 1, rows, :] + pair)
            pair = value + z_shift(value, 1, lane)
            shear_end[1, rows, :] = (4.0 * time_step) / (shears[1, nx - 1, rows, :] + pair)
    copies = []
    for x in sorted(range(nx), key=lambda x: not inner_plane(x, 0, nx) or not inner_plane(x, -1, nx)):
        for t in range(ny // tile):
            rows = pl.ds(tile * t, tile)
            d = Differences(x, t, lane)
            whole_y = inner_tile(t, ny)
            whole_x = inner_plane(x, -1, nx)
            strains = [part[c, x, rows, :] for c in range(3)]
            if not (whole_x and whole_y):
                if not whole_x:
                    strains[0] = d.dx(vx, -1)
                if not whole_y:
                    strains[1] = d.dy(vy, -1)
                strains = new_normal(stress, lam, shear, x, rows, strains)
            for c in range(3):
                out[c, x, rows, :] = strains[c]
            whole_x = inner_plane(x, 0, nx)
            total = part[3, x, rows, :]
            if not (whole_x and whole_y):
                if not whole_y:
                    total += d.dy(vx, 0)
                if not whole_x:
                    total += d.dx(vy, 0)
                factor = shear_end[0, rows, :] if x == nx - 1 else shears[0, x, rows, :]
                total = stress[3, x, rows, :] + factor * total
            out[3, x, rows, :] = total
            total = part[4, x, rows, :]
            if not whole_x:
                before = stress[4, x, rows, :]
                factor = shears[1, x, rows, :]
                change = None
                if x == nx - 1:
                    factor = shear_end[1, rows, :]
                    if step == 0:
                        change = near * (vz.at(x + 1, t) - vz.at(x, t)) + far * vz.at(x - 1, t)
                    else:
                        before = last_xz[rows, :]
                if change is None:
                    change = d.dx(vz, 0)
                total = before + factor * (total + change)
            out[4, x, rows, :] = total
            total = part[5, x, rows, :]
            if not whole_y:
                total = stress[5, x, rows, :] + shears[2, x, rows, :] * (total + d.dy(vz, 0))
            out[5, x, rows, :] = total
        if step == 1:
            copy = pltpu.make_async_copy(out.at[:, x], final_stress.at[:, x], sems.at[x])
            copy.start()
            copies.append(copy)
    for copy in copies:
        copy.wait()
    if step == 0:
        Pack(pax, pbx, even_x).put(
            put_planes([(out, 3, nx - 2), (out, 3, nx - 1), (out, 4, nx - 2), (out, 4, nx - 1), (out, 0, nx - 1)]),
            put_planes([(out, 3, 0), (out, 4, 0), (out, 0, 0), (out, 0, 1), (velocity, 2, 1)]),
        )
        Pack(pay, pby, even_y).put(
            put_rows([(out, 3, ny - 2, 2), (out, 5, ny - 2, 2), (out, 1, ny - 1, 1)], nx),
            put_rows([(out, 3, 0, 1), (out, 5, 0, 1), (out, 1, 0, 2)], nx),
        )


def call(kernel, outs, scratch, args, flops, hbm_in=(), hbm_out=()):
    def spec(far_away):
        return pl.BlockSpec(memory_space=pltpu.HBM if far_away else pltpu.VMEM)

    scratch = [pltpu.VMEM(shape, jnp.float32) if isinstance(shape, tuple) else shape for shape in scratch]
    args = [pltpu.with_memory_space_constraint(a, pltpu.HBM) if n in hbm_in else a for n, a in enumerate(args)]
    return pl.pallas_call(
        kernel,
        out_shape=[(pltpu.HBM if n in hbm_out else pltpu.VMEM)(shape, jnp.float32) for n, shape in enumerate(outs)],
        in_specs=[spec(n in hbm_in) for n in range(len(args))],
        out_specs=[spec(n in hbm_out) for n in range(len(outs))],
        scratch_shapes=scratch,
        compiler_params=pltpu.CompilerParams(vmem_limit_bytes=16 * 1024 * 1024),
        cost_estimate=pl.CostEstimate(flops=flops, bytes_accessed=2 * 1024 * 1024, transcendentals=0),
    )(*args)


def per_device(velocity, stress, density, lame_lambda, lame_mu):
    _, nx, ny, nz = velocity.shape
    routes = pairings(lax.axis_size("gx"), lax.axis_size("gy"))
    cells = nx * ny * nz
    one, three = (1, nx, ny, nz), (3, nx, ny, nz)
    dma = pltpu.SemaphoreType.DMA

    def packages(x_rows, y_rows=5):
        return [(x_rows, nz)] * 2 + [(nx * y_rows, nz)] * 2

    def exchange(arrays):
        return [lax.ppermute(array, AXES, route) for array, route in zip(arrays, routes)]

    def kernel(function, step):
        return lambda *refs: function(step, *refs)

    first, second, later = (5 * ny, 6), (5 * ny + tile, 5), (5 * ny, 5)
    *packed, ends = call(
        first_pack, [(5, ny, nz)] * 2 + packages(*first)[2:] + [(2, ny, nz)], [(12, nx, tile, nz), dma((3,))],
        (stress, density, lame_mu), cells, hbm_in=(0, 1, 2))
    packed, velocity, stress, density, lame_lambda, lame_mu = lax.optimization_barrier(
        ([package.reshape(-1, nz) for package in packed], velocity, stress, density, lame_lambda, lame_mu))
    got = exchange(packed)
    part, buoy, buoys = call(
        kernel(velocity_inside, 0), [three, one, three], [], (stress, density), 60 * cells)
    new_velocity, buoys_end, *packed = call(
        kernel(velocity_edges, 0),
        [three, (ny + nx * tile, nz)] + packages(*second)[2:] + packages(*second)[:2], [],
        (velocity, stress, buoy, buoys, ends, part, *got), 20 * cells)
    packed = packed[2:] + packed[:2]
    rows_y = got[2:]
    got = exchange(packed)
    part, shears = call(
        kernel(stress_inside, 0), [stress.shape, three], [(nx, ny, nz), (nx, 2 * tile, nz)],
        (new_velocity, stress, lame_lambda, lame_mu, *rows_y), 80 * cells)
    new_stress, shear_end, *packed = call(
        kernel(stress_edges, 0), [stress.shape, (2, ny, nz)] + packages(*later), [(ny + tile, nz)],
        (new_velocity, stress, lame_lambda, lame_mu, shears, part, *got), 20 * cells)
    velocity, stress = new_velocity, new_stress
    planes_x = got[:2]
    got = exchange(packed)
    part, factor_low = call(
        kernel(velocity_inside, 1), [three, (ny, nz)], [], (velocity, stress, buoys, lame_mu, *planes_x), 60 * cells)
    velocity, last_xz, *packed = call(
        kernel(velocity_edges, 1), [three, (ny, nz)] + packages(*later), [],
        (velocity, stress, buoys, buoys_end, shear_end, factor_low, part, *got), 20 * cells)
    got = exchange(packed)
    part, final_velocity = call(
        kernel(stress_inside, 1), [stress.shape, three], [dma],
        (velocity, stress, lame_lambda, lame_mu, shears), 80 * cells, hbm_out=(1,))
    (final_stress,) = call(
        kernel(stress_edges, 1), [stress.shape], [stress.shape, dma((nx,))],
        (velocity, stress, lame_lambda, lame_mu, shears, shear_end, last_xz, part, *got), 20 * cells, hbm_out=(0,))
    return (final_velocity, final_stress)


def solution(mesh):
    in_specs = (
        P(None, "gx", "gy", None),
        P(None, "gx", "gy", None),
        P("gx", "gy", None),
        P("gx", "gy", None),
        P("gx", "gy", None),
    )
    out_specs = (P(None, "gx", "gy", None), P(None, "gx", "gy", None))
    return jax.shard_map(
        per_device, mesh=mesh, in_specs=in_specs, out_specs=out_specs, check_vma=False
    )
```

```python
import jax
import jax.numpy as jnp
from jax import lax
from jax.experimental import pallas as pl
from jax.experimental.pallas import tpu as pltpu
from jax.sharding import PartitionSpec as P

near = 9.0 / 8.0
far = 1.0 / 24.0
time_step = 0.25
tile = 8
AXES = ("gx", "gy")


def pairings(count_x, count_y):
    other = 2 if count_x % 4 == 0 else 1

    def across(i, count):
        return ((i + 1) ^ 1) - 1

    def route(rule):
        pairs = []
        for i in range(count_x):
            for j in range(count_y):
                ti, tj = rule(i, j)
                pairs.append((i * count_y + j, ti * count_y + tj))
        return pairs

    def inner_x(i, j):
        return (i ^ 1, j)

    def outer_x(i, j):
        return (across(i, count_x), j) if 0 < i < count_x - 1 else (i, j ^ 1)

    def inner_y(i, j):
        return (i, j ^ 1)

    def outer_y(i, j):
        return (i, across(j, count_y)) if 0 < j < count_y - 1 else (i ^ other, j)

    return [route(rule) for rule in (inner_x, outer_x, outer_y, inner_y)]


def position():
    i, j = lax.axis_index("gx"), lax.axis_index("gy")
    return i, j, lax.rem(i, 2) == 0, lax.rem(j, 2) == 0


class Halo:
    def __init__(self, inner, outer, by_inner, outside):
        self.inner, self.outer, self.by_inner, self.outside = inner, outer, by_inner, outside
        self.rows = inner.shape[0]

    def load(self, start, count):
        rows = pl.ds(start, count)
        value = jnp.where(self.by_inner, self.inner[rows, :], self.outer[rows, :])
        return jnp.where(self.outside, 0.0, value)


class Pack:
    def __init__(self, inner, outer, even):
        self.inner, self.outer, self.even = inner, outer, even

    def put(self, up, down):
        even, inner, outer = self.even, self.inner, self.outer

        @pl.when(even)
        def _():
            up(inner)
            down(outer)

        @pl.when(jnp.logical_not(even))
        def _():
            up(outer)
            down(inner)


def put_planes(items):
    def put(out):
        start = 0
        for ref, f, x in items:
            value = ref[x] if f is None else ref[f, x]
            out[pl.ds(start, value.shape[0]), :] = value
            start += value.shape[0]

    return put


def put_rows(items, count_x):
    def put(out):
        each = out.shape[0] // count_x
        for x in range(count_x):
            start = each * x
            for ref, f, row, count in items:
                out[pl.ds(start, count), :] = ref[f, x, pl.ds(row, count), :]
                start += count

    return put


def sides(i, j):
    return i == 0, i == lax.axis_size("gx") - 1, j == 0, j == lax.axis_size("gy") - 1


def lanes():
    return lax.broadcasted_iota(jnp.int32, (tile, 128), 1)


def z_shift(value, k, lane):
    size = value.shape[-1]
    moved = pltpu.roll(value, (-k) % size, 1)
    inside = lane < size - k if k > 0 else lane >= -k
    return jnp.where(inside, moved, 0.0)


def difference(at, base):
    return near * (at(base + 1) - at(base)) - far * (at(base + 2) - at(base - 1))


class Field:
    def __init__(self, ref, f, low_x=None, high_x=None, low_y=None, high_y=None, last=None, below=None):
        self.ref, self.f = ref, f
        self.low_x, self.high_x, self.low_y, self.high_y = low_x, high_x, low_y, high_y
        self.last, self.below = last, below

    def at(self, x, t):
        nx, ny = self.ref.shape[-3], self.ref.shape[-2]
        if x < 0:
            halo, index = self.low_x
            value = halo.load(ny * (index + x) + tile * t, tile)
            return value + self.below(t) if self.below is not None and x == -1 else value
        if x >= nx:
            halo, index = self.high_x
            return halo.load(ny * (index + x - nx) + tile * t, tile)
        if self.last is not None and x == nx - 1:
            return self.last[pl.ds(tile * t, tile), :]
        return self.ref[self.f, x, pl.ds(tile * t, tile), :]

    def y(self, x, t, k):
        nx, ny = self.ref.shape[-3], self.ref.shape[-2]
        start = tile * t + k
        if 0 <= start <= ny - tile:
            return self.ref[self.f, x, pl.ds(start, tile), :]
        halo, first = self.low_y if k < 0 else self.high_y
        moved = pltpu.roll(self.ref[self.f, x, pl.ds(tile * t, tile), :], (-k) % tile, 0)
        place = lax.broadcasted_iota(jnp.int32, moved.shape, 0)
        for n in range(abs(k)):
            row = halo.load(halo.rows // nx * x + first + (n + k + 1 if k < 0 else n), 1)
            moved = jnp.where(place == (n if k < 0 else tile - k + n), row, moved)
        return moved


class Differences:
    def __init__(self, x, t, lane):
        self.x, self.t, self.lane = x, t, lane

    def dx(self, field, base):
        return difference(lambda k: field.at(self.x + k, self.t), base)

    def dy(self, field, base):
        return difference(lambda k: field.y(self.x, self.t, k), base)

    def dz(self, field, base):
        value = field.at(self.x, self.t)
        return difference(lambda k: z_shift(value, k, self.lane) if k else value, base)


def inner_plane(x, base, nx):
    return x + base - 1 >= 0 and x + base + 2 < nx


def inner_velocity_plane(step, c, x, base, nx):
    return inner_plane(x, base, nx) and not (step == 1 and c == 2 and x == nx - 2)


def inner_tile(t, ny):
    return 0 < t < ny // tile - 1


def receive(ax, bx, by, ay):
    i, j, even_x, even_y = position()
    first_x, last_x, first_y, last_y = sides(i, j)
    odd_x, odd_y = jnp.logical_not(even_x), jnp.logical_not(even_y)
    low_x, high_x = Halo(ax, bx, odd_x, first_x), Halo(ax, bx, even_x, last_x)
    low_y, high_y = Halo(ay, by, odd_y, first_y), Halo(ay, by, even_y, last_y)
    return low_x, high_x, low_y, high_y


def inverse(value, outside):
    return jnp.where(outside, 0.0, 1.0 / jnp.where(outside, 1.0, value))


def first_pack(stress, density, shear, ax, bx, by, ay, ends, tiles, sems):
    i, j, even_x, even_y = position()
    nx, ny = density.shape[0], density.shape[1]
    def up(out):
        pairs = [
            (stress.at[3, pl.ds(nx - 2, 2)], 0, 2), (stress.at[4, pl.ds(nx - 2, 2)], 2, 2),
            (stress.at[0, pl.ds(nx - 1, 1)], 4, 1),
        ]
        return [pltpu.make_async_copy(source, out.at[pl.ds(n, count)], sems.at[1]) for source, n, count in pairs]

    def down(out):
        pairs = [
            (stress.at[pl.ds(3, 2), 0], 0, 2), (stress.at[0, pl.ds(0, 2)], 2, 2),
            (density.at[pl.ds(0, 1)], 4, 1),
        ]
        return [pltpu.make_async_copy(source, out.at[pl.ds(n, count)], sems.at[2]) for source, n, count in pairs]

    copies = [
        pltpu.make_async_copy(stress.at[pl.ds(1, 5), :, pl.ds(ny - tile, tile), :], tiles.at[pl.ds(0, 5)], sems.at[0]),
        pltpu.make_async_copy(stress.at[pl.ds(1, 5), :, pl.ds(0, tile), :], tiles.at[pl.ds(5, 5)], sems.at[0]),
        pltpu.make_async_copy(density.at[:, pl.ds(0, tile), :], tiles.at[10], sems.at[0]),
        pltpu.make_async_copy(shear.at[:, pl.ds(0, tile), :], tiles.at[11], sems.at[0]),
        pltpu.make_async_copy(shear.at[0], ends.at[0], sems.at[0]),
        pltpu.make_async_copy(shear.at[nx - 1], ends.at[1], sems.at[0]),
    ]
    for copy in copies:
        copy.start()

    @pl.when(even_x)
    def _():
        for copy in up(ax) + down(bx):
            copy.start()

    @pl.when(jnp.logical_not(even_x))
    def _():
        for copy in up(bx) + down(ax):
            copy.start()

    for copy in copies:
        copy.wait()
    Pack(ay, by, even_y).put(
        put_rows([(tiles, 2, tile - 2, 2), (tiles, 4, tile - 2, 2), (tiles, 0, tile - 1, 1)], nx),
        put_rows([(tiles, 7, 0, 1), (tiles, 9, 0, 1), (tiles, 5, 0, 2), (tiles, 10, 0, 1), (tiles, 11, 0, 1)], nx),
    )
    for copy in up(ax) + down(bx):
        copy.wait()


def velocity_terms(stress, halos=(None,) * 4, last_xz=None, below_xz=None):
    low_x, high_x, low_y, high_y = halos
    xx = Field(stress, 0, (low_x, 5), (high_x, 2))
    yy = Field(stress, 1, low_y=(low_y, 4), high_y=(high_y, 2))
    zz = Field(stress, 2)
    xy = Field(stress, 3, (low_x, 2), (high_x, 0), (low_y, 1), (high_y, 0))
    xz = Field(stress, 4, (low_x, 4), (high_x, 1), last=last_xz, below=below_xz)
    yz = Field(stress, 5, low_y=(low_y, 3), high_y=(high_y, 1))
    return ((xx, 0), (xy, -1), (xz, -1)), ((xy, -1), (yy, 0), (yz, -1)), ((xz, -1), (yz, -1), (zz, 0))


def velocity_inside(step, *refs):
    if step == 0:
        stress, density, out, buoy, buoys = refs
    else:
        velocity, stress, buoys, shear, ax, bx, out, factor_low = refs
    nx, ny = stress.shape[1], stress.shape[2]
    lane = lanes()
    terms = velocity_terms(stress)
    if step == 1:
        i, j, even_x, _ = position()
        for t in range(ny // tile):
            rows, source = pl.ds(tile * t, tile), pl.ds(4 * ny + tile * t, tile)
            below = 1.0 / jnp.where(i == 0, 1.0, jnp.where(even_x, bx[source, :], ax[source, :]))
            pair = below + 1.0 / shear[0, rows, :]
            factor = (-4.0 * time_step * far) / (pair + z_shift(pair, 1, lane))
            factor_low[rows, :] = jnp.where(i == 0, 0.0, factor)
    if step == 0:
        for x in range(nx):
            buoy[0, x] = 1.0 / density[x]
        buoy_field = Field(buoy, 0)
    for x in range(nx):
        for t in range(ny // tile):
            rows = pl.ds(tile * t, tile)
            d = Differences(x, t, lane)
            if step == 0:
                here = buoy_field.at(x, t)
                half = 0.5 * time_step
                if x < nx - 1:
                    buoys[0, x, rows, :] = half * (here + buoy_field.at(x + 1, t))
                if t < ny // tile - 1:
                    buoys[1, x, rows, :] = half * (here + buoy_field.y(x, t, 1))
                buoys[2, x, rows, :] = half * (here + z_shift(here, 1, lane))
            for c, ((fx, sx), (fy, sy), (fz, sz)) in enumerate(terms):
                late = step == 1 and c == 0 and x == nx - 1
                total = jnp.zeros((tile, 128), jnp.float32) if late else d.dz(fz, sz)
                whole_x, whole_y = inner_velocity_plane(step, c, x, sx, nx), inner_tile(t, ny)
                if whole_x:
                    total += d.dx(fx, sx)
                if whole_y:
                    total += d.dy(fy, sy)
                if whole_x and whole_y:
                    total = buoys[c, x, rows, :] * total
                    if step == 1:
                        total += velocity[c, x, rows, :]
                out[c, x, rows, :] = total


def velocity_edges(step, *refs):
    if step == 0:
        (velocity, stress, buoy, buoys, ends, part, ax, bx, by, ay, out, buoys_end, pby, pay, pax, pbx) = refs
        last_xz = below_xz = None
    else:
        (velocity, stress, buoys, buoys_end, shear_end, factor_low, part, ax, bx, by, ay,
         out, last_xz, pby, pay, pax, pbx) = refs

        def below_xz(t):
            rows = pl.ds(tile * t, tile)
            return factor_low[rows, :] * velocity[2, 1, rows, :]

    nx, ny = stress.shape[1], stress.shape[2]
    i, j, even_x, even_y = position()
    _, last_x, _, last_y = sides(i, j)
    halos = receive(ax, bx, by, ay)
    _, high_x, _, high_y = halos
    terms = velocity_terms(stress, halos, last_xz, below_xz)
    lane = lanes()
    if step == 1:
        for t in range(ny // tile):
            rows = pl.ds(tile * t, tile)
            further = high_x.load(4 * ny + tile * t, tile)
            last_xz[rows, :] = stress[4, nx - 1, rows, :] - far * shear_end[1, rows, :] * further
    if step == 0:
        half = 0.5 * time_step
        for t in range(ny // tile):
            rows = pl.ds(tile * t, tile)
            above = inverse(high_x.load(4 * ny + tile * t, tile), last_x)
            buoys_end[rows, :] = half * (buoy[0, nx - 1, rows, :] + above)
        rows = pl.ds(ny - tile, tile)
        place = lax.broadcasted_iota(jnp.int32, (tile, 128), 0)
        for x in range(nx):
            here = buoy[0, x, rows, :]
            row = inverse(high_y.load(high_y.rows // nx * x + 4, 1), last_y)
            next_y = jnp.where(place == tile - 1, row, pltpu.roll(here, tile - 1, 0))
            buoys_end[pl.ds(ny + tile * x, tile), :] = half * (here + next_y)
    for x in range(nx):
        for t in range(ny // tile):
            rows = pl.ds(tile * t, tile)
            d = Differences(x, t, lane)
            for c, ((fx, sx), (fy, sy), (fz, sz)) in enumerate(terms):
                whole_x, whole_y = inner_velocity_plane(step, c, x, sx, nx), inner_tile(t, ny)
                total = part[c, x, rows, :]
                if whole_x and whole_y:
                    out[c, x, rows, :] = velocity[c, x, rows, :] + total if step == 0 else total
                    continue
                if not whole_x:
                    total += d.dx(fx, sx)
                if not whole_y:
                    total += d.dy(fy, sy)
                if step == 1 and c == 0 and x == nx - 1:
                    total += d.dz(fz, sz)
                if c == 0 and x == nx - 1:
                    factor = buoys_end[rows, :]
                elif c == 1 and t == ny // tile - 1:
                    factor = buoys_end[pl.ds(ny + tile * x, tile), :]
                else:
                    factor = buoys[c, x, rows, :]
                out[c, x, rows, :] = velocity[c, x, rows, :] + factor * total

    planes_up = [(out, 0, nx - 2), (out, 0, nx - 1), (out, 1, nx - 1), (out, 2, nx - 1)]
    planes_down = [(out, 0, 0), (out, 1, 0), (out, 1, 1), (out, 2, 0)]
    if step == 0:
        planes_up.append((ends, None, 1))
        planes_down.append((ends, None, 0))
    else:
        planes_down.append((out, 2, 1))

    def down(package):
        put_planes(planes_down)(package)
        if step == 0:
            package[pl.ds(5 * ny, 1), :] = inverse(high_y.load(5, 1), last_y)

    Pack(pax, pbx, even_x).put(put_planes(planes_up), down)
    Pack(pay, pby, even_y).put(
        put_rows([(out, 1, ny - 2, 2), (out, 0, ny - 1, 1), (out, 2, ny - 1, 1)], nx),
        put_rows([(out, 1, 0, 1), (out, 0, 0, 2), (out, 2, 0, 2)], nx),
    )


def stress_fields(velocity, halos=(None,) * 4):
    low_x, high_x, low_y, high_y = halos
    vx = Field(velocity, 0, (low_x, 2), (high_x, 0), (low_y, 2), (high_y, 1))
    vy = Field(velocity, 1, (low_x, 3), (high_x, 1), (low_y, 1), (high_y, 0))
    vz = Field(velocity, 2, (low_x, 4), (high_x, 3), (low_y, 3), (high_y, 3))
    return vx, vy, vz


def new_normal(stress, lam, shear, x, rows, strains):
    la = time_step * lam[x, rows, :]
    two = (2.0 * time_step) * shear[x, rows, :]
    common = la * (strains[0] + strains[1] + strains[2])
    return [stress[c, x, rows, :] + (common + two * strains[c]) for c in range(3)]


def stress_inside(step, *refs):
    if step == 0:
        velocity, stress, lam, shear, by, ay, out, shears, comps, edge_c = refs
    else:
        velocity, stress, lam, shear, shears, out, final_velocity, sem = refs
    nx, ny = stress.shape[1], stress.shape[2]
    lane = lanes()
    vx, vy, vz = stress_fields(velocity)
    if step == 1:
        copy = pltpu.make_async_copy(velocity, final_velocity, sem)
        copy.start()
    if step == 0:
        i, j, _, even_y = position()
        _, _, _, last_y = sides(i, j)
        for x in range(nx):
            comps[x] = 1.0 / shear[x]
            edge_c[x, pl.ds(0, tile), :] = comps[x, pl.ds(ny - tile, tile), :]
            row = pl.ds(ay.shape[0] // nx * x + 5, 1)
            value = jnp.where(last_y, 1.0, jnp.where(even_y, ay[row, :], by[row, :]))
            edge_c[x, pl.ds(tile, 1), :] = jnp.where(last_y, 0.0, 1.0 / value)

        def comp(x, t, k):
            if k == 1 and t == ny // tile - 1:
                return edge_c[x, pl.ds(1, tile), :]
            return comps[x, pl.ds(tile * t + k, tile), :]

    for x in range(nx):
        for t in range(ny // tile):
            rows = pl.ds(tile * t, tile)
            d = Differences(x, t, lane)
            if step == 0:
                here, next_y = comp(x, t, 0), comp(x, t, 1)
                pair_y = here + next_y
                four = 4.0 * time_step
                if x == nx - 1:
                    shears[0, x, rows, :] = pair_y
                    shears[1, x, rows, :] = here + z_shift(here, 1, lane)
                else:
                    next_x = comp(x + 1, t, 0)
                    pair_x = here + next_x
                    shears[0, x, rows, :] = four / (pair_x + (next_y + comp(x + 1, t, 1)))
                    shears[1, x, rows, :] = four / (pair_x + z_shift(pair_x, 1, lane))
                shears[2, x, rows, :] = four / (pair_y + z_shift(pair_y, 1, lane))
            whole_y = inner_tile(t, ny)
            whole_x = inner_plane(x, -1, nx)
            zero = jnp.zeros((tile, 128), jnp.float32)
            strains = [d.dx(vx, -1) if whole_x else zero, d.dy(vy, -1) if whole_y else zero, d.dz(vz, -1)]
            if whole_x and whole_y:
                strains = new_normal(stress, lam, shear, x, rows, strains)
            for c in range(3):
                out[c, x, rows, :] = strains[c]
            whole_x = inner_plane(x, 0, nx)
            total = zero
            if whole_y:
                total += d.dy(vx, 0)
            if whole_x:
                total += d.dx(vy, 0)
            if whole_x and whole_y:
                total = stress[3, x, rows, :] + shears[0, x, rows, :] * total
            out[3, x, rows, :] = total
            total = d.dz(vx, 0)
            if whole_x:
                total = stress[4, x, rows, :] + shears[1, x, rows, :] * (total + d.dx(vz, 0))
            out[4, x, rows, :] = total
            total = d.dz(vy, 0)
            if whole_y:
                total = stress[5, x, rows, :] + shears[2, x, rows, :] * (total + d.dy(vz, 0))
            out[5, x, rows, :] = total
    if step == 1:
        copy.wait()


def stress_edges(step, *refs):
    if step == 0:
        (velocity, stress, lam, shear, shears, part, ax, bx, by, ay,
         out, shear_end, pax, pbx, pby, pay, above) = refs
    else:
        (velocity, stress, lam, shear, shears, shear_end, last_xz, part, ax, bx, by, ay,
         final_stress, out, sems) = refs
    nx, ny = stress.shape[1], stress.shape[2]
    i, j, even_x, even_y = position()
    _, last_x, _, _ = sides(i, j)
    halos = receive(ax, bx, by, ay)
    high_x = halos[1]
    vx, vy, vz = stress_fields(velocity, halos)
    lane = lanes()
    if step == 0:
        for t in range(ny // tile):
            above[pl.ds(tile * t, tile), :] = inverse(high_x.load(4 * ny + tile * t, tile), last_x)
        above[pl.ds(ny, 1), :] = high_x.load(5 * ny, 1)
        for t in range(ny // tile):
            rows = pl.ds(tile * t, tile)
            value = above[rows, :]
            pair = value + above[pl.ds(tile * t + 1, tile), :]
            shear_end[0, rows, :] = (4.0 * time_step) / (shears[0, nx - 1, rows, :] + pair)
            pair = value + z_shift(value, 1, lane)
            shear_end[1, rows, :] = (4.0 * time_step) / (shears[1, nx - 1, rows, :] + pair)
    copies = []
    for x in sorted(range(nx), key=lambda x: not inner_plane(x, 0, nx) or not inner_plane(x, -1, nx)):
        for t in range(ny // tile):
            rows = pl.ds(tile * t, tile)
            d = Differences(x, t, lane)
            whole_y = inner_tile(t, ny)
            whole_x = inner_plane(x, -1, nx)
            strains = [part[c, x, rows, :] for c in range(3)]
            if not (whole_x and whole_y):
                if not whole_x:
                    strains[0] = d.dx(vx, -1)
                if not whole_y:
                    strains[1] = d.dy(vy, -1)
                strains = new_normal(stress, lam, shear, x, rows, strains)
            for c in range(3):
                out[c, x, rows, :] = strains[c]
            whole_x = inner_plane(x, 0, nx)
            total = part[3, x, rows, :]
            if not (whole_x and whole_y):
                if not whole_y:
                    total += d.dy(vx, 0)
                if not whole_x:
                    total += d.dx(vy, 0)
                factor = shear_end[0, rows, :] if x == nx - 1 else shears[0, x, rows, :]
                total = stress[3, x, rows, :] + factor * total
            out[3, x, rows, :] = total
            total = part[4, x, rows, :]
            if not whole_x:
                before = stress[4, x, rows, :]
                factor = shears[1, x, rows, :]
                change = None
                if x == nx - 1:
                    factor = shear_end[1, rows, :]
                    if step == 0:
                        change = near * (vz.at(x + 1, t) - vz.at(x, t)) + far * vz.at(x - 1, t)
                    else:
                        before = last_xz[rows, :]
                if change is None:
                    change = d.dx(vz, 0)
                total = before + factor * (total + change)
            out[4, x, rows, :] = total
            total = part[5, x, rows, :]
            if not whole_y:
                total = stress[5, x, rows, :] + shears[2, x, rows, :] * (total + d.dy(vz, 0))
            out[5, x, rows, :] = total
        if step == 1:
            copy = pltpu.make_async_copy(out.at[:, x], final_stress.at[:, x], sems.at[x])
            copy.start()
            copies.append(copy)
    for copy in copies:
        copy.wait()
    if step == 0:
        Pack(pax, pbx, even_x).put(
            put_planes([(out, 3, nx - 2), (out, 3, nx - 1), (out, 4, nx - 2), (out, 4, nx - 1), (out, 0, nx - 1)]),
            put_planes([(out, 3, 0), (out, 4, 0), (out, 0, 0), (out, 0, 1), (velocity, 2, 1)]),
        )
        Pack(pay, pby, even_y).put(
            put_rows([(out, 3, ny - 2, 2), (out, 5, ny - 2, 2), (out, 1, ny - 1, 1)], nx),
            put_rows([(out, 3, 0, 1), (out, 5, 0, 1), (out, 1, 0, 2)], nx),
        )


def call(kernel, outs, scratch, args, flops, hbm_in=(), hbm_out=()):
    def spec(far_away):
        return pl.BlockSpec(memory_space=pltpu.HBM if far_away else pltpu.VMEM)

    scratch = [pltpu.VMEM(shape, jnp.float32) if isinstance(shape, tuple) else shape for shape in scratch]
    args = [pltpu.with_memory_space_constraint(a, pltpu.HBM) if n in hbm_in else a for n, a in enumerate(args)]
    return pl.pallas_call(
        kernel,
        out_shape=[(pltpu.HBM if n in hbm_out else pltpu.VMEM)(shape, jnp.float32) for n, shape in enumerate(outs)],
        in_specs=[spec(n in hbm_in) for n in range(len(args))],
        out_specs=[spec(n in hbm_out) for n in range(len(outs))],
        scratch_shapes=scratch,
        compiler_params=pltpu.CompilerParams(vmem_limit_bytes=16 * 1024 * 1024),
        cost_estimate=pl.CostEstimate(flops=flops, bytes_accessed=2 * 1024 * 1024, transcendentals=0),
    )(*args)


def per_device(velocity, stress, density, lame_lambda, lame_mu):
    _, nx, ny, nz = velocity.shape
    routes = pairings(lax.axis_size("gx"), lax.axis_size("gy"))
    cells = nx * ny * nz
    one, three = (1, nx, ny, nz), (3, nx, ny, nz)
    dma = pltpu.SemaphoreType.DMA

    def packages(x_rows, y_rows=5):
        return [(x_rows, nz)] * 2 + [(nx * y_rows, nz)] * 2

    def exchange(arrays):
        return [lax.ppermute(array, AXES, route) for array, route in zip(arrays, routes)]

    def kernel(function, step):
        return lambda *refs: function(step, *refs)

    first, second, later = (5 * ny, 6), (5 * ny + tile, 5), (5 * ny, 5)
    *packed, ends = call(
        first_pack, [(5, ny, nz)] * 2 + packages(*first)[2:] + [(2, ny, nz)], [(12, nx, tile, nz), dma((3,))],
        (stress, density, lame_mu), cells, hbm_in=(0, 1, 2))
    packed, velocity, stress, density, lame_lambda, lame_mu = lax.optimization_barrier(
        ([package.reshape(-1, nz) for package in packed], velocity, stress, density, lame_lambda, lame_mu))
    got = exchange(packed)
    part, buoy, buoys = call(
        kernel(velocity_inside, 0), [three, one, three], [], (stress, density), 60 * cells)
    new_velocity, buoys_end, *packed = call(
        kernel(velocity_edges, 0),
        [three, (ny + nx * tile, nz)] + packages(*second)[2:] + packages(*second)[:2], [],
        (velocity, stress, buoy, buoys, ends, part, *got), 20 * cells)
    packed = packed[2:] + packed[:2]
    rows_y = got[2:]
    got = exchange(packed)
    part, shears = call(
        kernel(stress_inside, 0), [stress.shape, three], [(nx, ny, nz), (nx, 2 * tile, nz)],
        (new_velocity, stress, lame_lambda, lame_mu, *rows_y), 80 * cells)
    new_stress, shear_end, *packed = call(
        kernel(stress_edges, 0), [stress.shape, (2, ny, nz)] + packages(*later), [(ny + tile, nz)],
        (new_velocity, stress, lame_lambda, lame_mu, shears, part, *got), 20 * cells)
    velocity, stress = new_velocity, new_stress
    planes_x = got[:2]
    got = exchange(packed)
    part, factor_low = call(
        kernel(velocity_inside, 1), [three, (ny, nz)], [], (velocity, stress, buoys, lame_mu, *planes_x), 60 * cells)
    velocity, last_xz, *packed = call(
        kernel(velocity_edges, 1), [three, (ny, nz)] + packages(*later)[2:] + packages(*later)[:2], [],
        (velocity, stress, buoys, buoys_end, shear_end, factor_low, part, *got), 20 * cells)
    packed = packed[2:] + packed[:2]
    got = exchange(packed)
    part, final_velocity = call(
        kernel(stress_inside, 1), [stress.shape, three], [dma],
        (velocity, stress, lame_lambda, lame_mu, shears), 80 * cells, hbm_out=(1,))
    (final_stress,) = call(
        kernel(stress_edges, 1), [stress.shape], [stress.shape, dma((nx,))],
        (velocity, stress, lame_lambda, lame_mu, shears, shear_end, last_xz, part, *got), 20 * cells, hbm_out=(0,))
    return (final_velocity, final_stress)


def solution(mesh):
    in_specs = (
        P(None, "gx", "gy", None),
        P(None, "gx", "gy", None),
        P("gx", "gy", None),
        P("gx", "gy", None),
        P("gx", "gy", None),
    )
    out_specs = (P(None, "gx", "gy", None), P(None, "gx", "gy", None))
    return jax.shard_map(
        per_device, mesh=mesh, in_specs=in_specs, out_specs=out_specs, check_vma=False
    )
```
